128 devices in a mesh: wide: 32 (over x_lo, z, y), grp: 4 (over x_hi, core).
Axes of the slice: x: 4 (x_hi: 2, x_lo: 2; x = x_hi * 2 + x_lo), y: 4, z: 4, core: 2. Of those that a mesh axis runs over, the one named last changes fastest.
Arguments:
- tokens: bfloat16 [98304, 768], P(('wide', 'grp')), may hold values from -6 to 6
- exit_layer: int32 [768], P(('wide', 'grp')), may hold values from 1 to 12, as said below
- w_qkv: bfloat16 [768, 2304], P('wide'), may hold values from -0.21875 to 0.21875
- w_out: bfloat16 [768, 768], P('wide'), may hold values from -0.4375 to 0.4375
- gain_attn: bfloat16 [768], P('wide'), may hold values from 0.5 to 1.5
- w_up: bfloat16 [768, 3072], P('wide'), may hold values from -0.21875 to 0.21875
- w_down: bfloat16 [3072, 768], P('wide'), may hold values from -0.109375 to 0.109375
- gain_ffn: bfloat16 [768], P('wide'), may hold values from 0.5 to 1.5
- w_proj: bfloat16 [768, 128], P('wide'), may hold values from -0.21875 to 0.21875
- pool_query: bfloat16 [128], P('wide'), may hold values from -4 to 4
- w_hid: bfloat16 [128, 128], P('wide'), may hold values from -0.5 to 0.5
- w_cls: bfloat16 [128, 14], P('wide'), may hold values from -1 to 1
- cot_out: bfloat16 [98304, 768], P(('wide', 'grp')), may hold values from -6 to 6
- cot_logits: float32 [768, 14], P(('wide', 'grp')), may hold values from -6 to 6
Outputs:
- activations: bfloat16 [98304, 768], P(('wide', 'grp'))
- logits: float32 [768, 14], P(('wide', 'grp'))
- grad_tokens: float32 [98304, 768], P(('wide', 'grp'))
- grad_qkv: float32 [768, 2304], P('wide')
- grad_out: float32 [768, 768], P('wide')
- grad_gain_attn: float32 [768], P('wide')
- grad_up: float32 [768, 3072], P('wide')
- grad_down: float32 [3072, 768], P('wide')
- grad_gain_ffn: float32 [768], P('wide')
- grad_proj: float32 [768, 128], P('wide')
- grad_pool: float32 [128], P('wide')
- grad_hid: float32 [128, 128], P('wide')
- grad_cls: float32 [128, 14], P('wide')
The draws below stay inside these ranges and needn't reach their ends.
Inputs may be any that keep to these rules, and one draw needn't show every extreme that they name: `exit_layer`: sequences leave early more often than late; some sequence has each end value.
All inputs are finite; a program needn't handle non-finite values.
Results may differ from the reference program's by a relative error of at most 0.033.
Values may be sent and summed in bfloat16 or wider, within the bound.
A program may use at most 192 MiB of HBM per device.

```python
import jax
import jax.numpy as jnp
from jax import lax

D = 768
HEADS = 12
HEAD_DIM = 64
FF = 3072
SW = 128
POOL_HEADS = 2
CLASSES = 14
SEQ = 128
MAX_LAYER = 12
LAYER = 3
SEQ_DEV = 6
SEQS = 768
TOKENS = 98304
N_GRP = 4


def draw_exit_layer(key, part):
    key = jax.random.fold_in(key, 11)
    picks = jax.random.randint(key, (2, SEQS), 0, MAX_LAYER)
    layers = 1 + jnp.minimum(picks[0], picks[1])
    layers = layers.at[0].set(MAX_LAYER)
    layers = layers.at[1].set(1)
    return layers.astype(jnp.int32)


def levels(key, dims, shards, low, top_value):
    level = 1.0
    for dim, blocks in shards:
        heights = jax.random.uniform(jax.random.fold_in(jax.random.fold_in(key, 6), dim), (blocks,), jnp.float32, low / len(shards), top_value / len(shards))
        level = level * jnp.repeat(jnp.exp(heights), dims[dim] // blocks).reshape((-1,) + (1,) * (len(dims) - 1 - dim))
    return level


def noise(rng, shape, scale, limit, split=(), held_as=jnp.bfloat16):
    values = scale * jax.random.normal(rng, shape, jnp.float32)
    if split:
        values = values * levels(rng, shape, split, -0.22, 0.18)
    return jnp.clip(values, -limit, limit).astype(held_as)


def setup_inputs(seed: int = 0) -> dict:
    key_of = jax.random.split(jax.random.key(seed), 15)
    return {
        "tokens": noise(key_of[0], (TOKENS, D), 1.0, 6.0, ((0, 128),)),
        "exit_layer": draw_exit_layer(jax.random.fold_in(key_of[14], 71), 0),
        "w_qkv": noise(key_of[2], (D, 3 * D), D ** -0.5, 0.21875, ((0, 32),)),
        "w_out": noise(key_of[3], (D, D), (D // 4) ** -0.5, 0.4375, ((0, 32),)),
        "gain_attn": jnp.clip(1.0 + 0.1 * jax.random.normal(key_of[4], (D,), jnp.float32), 0.5, 1.5).astype(jnp.bfloat16),
        "w_up": noise(key_of[5], (D, FF), D ** -0.5, 0.21875, ((0, 32),)),
        "w_down": noise(key_of[6], (FF, D), FF ** -0.5, 0.109375, ((0, 32),)),
        "gain_ffn": jnp.clip(1.0 + 0.1 * jax.random.normal(key_of[7], (D,), jnp.float32), 0.5, 1.5).astype(jnp.bfloat16),
        "w_proj": noise(key_of[8], (D, SW), D ** -0.5, 0.21875, ((0, 32),)),
        "pool_query": noise(key_of[9], (SW,), 1.0, 4.0, ((0, 32),)),
        "w_hid": noise(key_of[10], (SW, SW), SW ** -0.5, 0.5, ((0, 32),)),
        "w_cls": noise(key_of[11], (SW, CLASSES), (SW // 4) ** -0.5, 1.0, ((0, 32),)),
        "cot_out": noise(key_of[12], (TOKENS, D), 1.0, 6.0, ((0, 128),)),
        "cot_logits": noise(key_of[13], (SEQS, CLASSES), 1.0, 6.0, ((0, 128),), jnp.float32),
    }


@jax.custom_vjp
def low(v):
    return lax.optimization_barrier(v.astype(jnp.bfloat16)).astype(jnp.float32)

@jax.custom_vjp
def low_back(v):
    return v

def low_keep(v):
    return (low(v), None)

def low_pass(kept, grad):
    return (grad,)

def back_keep(v):
    return (v, None)

def back_low(kept, grad):
    return (low(grad),)
low.defvjp(low_keep, low_pass)
low_back.defvjp(back_keep, back_low)

def matmul(left, right):
    return jnp.dot(left, right, precision=lax.Precision.HIGHEST)

def layer_norm(hidden, gain):
    centre = hidden - lax.optimization_barrier(jnp.mean(hidden, axis=-1, keepdims=True))
    spread = lax.optimization_barrier(jnp.mean(centre * centre, axis=-1, keepdims=True))
    return centre * lax.rsqrt(spread + 1e-06) * gain

def student(projected, pool_query, w_hid, w_cls):
    seq_count = projected.shape[0] // SEQ
    head_size = SW // POOL_HEADS
    pieces = projected.reshape(seq_count, SEQ, POOL_HEADS, head_size)
    queries = pool_query.reshape(POOL_HEADS, head_size)
    pool_scores = jnp.einsum('bshd,hd->bsh', pieces, queries, precision=lax.Precision.HIGHEST) * head_size ** (-0.5)
    pool_weights = jax.nn.softmax(pool_scores, axis=1)
    pooled = jnp.einsum('bsh,bshd->bhd', pool_weights, pieces, precision=lax.Precision.HIGHEST).reshape(seq_count, SW)
    hidden = jnp.tanh(matmul(pooled, w_hid))
    return matmul(hidden, w_cls)

def forward(tokens, w_qkv, w_out, gain_attn, w_up, w_down, gain_ffn, w_proj, pool_query, w_hid, w_cls, alive_tok, alive_seq):
    tok_rows = tokens.shape[0]
    seq_count = tok_rows // SEQ
    merged = low(low_back(matmul(tokens, w_qkv)))
    stacked = merged.reshape(seq_count, SEQ, 3, HEADS, HEAD_DIM)
    queries = stacked[:, :, 0]
    key_part = stacked[:, :, 1]
    value_part = stacked[:, :, 2]
    scores = low_back(jnp.einsum('bqhd,bkhd->bhqk', queries, key_part, precision=lax.Precision.HIGHEST) * HEAD_DIM ** (-0.5))
    probs = low(jax.nn.softmax(scores, axis=-1))
    context = low(low_back(jnp.einsum('bhqk,bkhd->bqhd', probs, value_part, precision=lax.Precision.HIGHEST).reshape(tok_rows, D)))
    mixed = tokens + low_back(matmul(context, w_out))
    normed = low(layer_norm(mixed, gain_attn))
    upward = low_back(matmul(normed, w_up))
    active = low(jax.nn.gelu(upward))
    second = normed + low_back(matmul(active, w_down))
    output = low(layer_norm(second, gain_ffn))
    projected = low_back(matmul(output, w_proj))
    logits = student(projected, pool_query, w_hid, w_cls) * alive_seq[:, None]
    return (output * alive_tok[:, None], logits)

def reference(tokens, exit_layer, w_qkv, w_out, gain_attn, w_up, w_down, gain_ffn, w_proj, pool_query, w_hid, w_cls, cot_out, cot_logits):
    params = tuple((item.astype(jnp.float32) for item in (w_qkv, w_out, gain_attn, w_up, w_down, gain_ffn, w_proj, pool_query, w_hid, w_cls)))
    block_seqs = SEQ_DEV * N_GRP
    blocks = SEQS // block_seqs
    tok_blocks = tokens.reshape(blocks, block_seqs * SEQ, D)
    exit_blocks = exit_layer.reshape(blocks, block_seqs)
    cot_blocks = cot_out.reshape(blocks, block_seqs * SEQ, D)
    logit_blocks = cot_logits.reshape(blocks, block_seqs, CLASSES)

    def step(totals, inputs):
        tok_block, exit_block, cot_block, logit_cot = inputs
        alive_seq = (exit_block >= LAYER).astype(jnp.float32)
        alive_tok = jnp.repeat(alive_seq, SEQ)

        def block_forward(block_in, *weights):
            return forward(block_in, *weights, alive_tok, alive_seq)
        outputs, pull = jax.vjp(block_forward, tok_block.astype(jnp.float32), *params)
        grads = pull((cot_block.astype(jnp.float32), logit_cot))
        totals = tuple((left + right for left, right in zip(totals, grads[1:])))
        return (totals, (outputs[0].astype(jnp.bfloat16), outputs[1], grads[0]))
    zeros = tuple((jnp.zeros(item.shape, jnp.float32) for item in params))
    totals, (acts, logits, grad_in) = lax.scan(step, zeros, (tok_blocks, exit_blocks, cot_blocks, logit_blocks))
    return (acts.reshape(TOKENS, D), logits.reshape(SEQS, CLASSES), grad_in.reshape(TOKENS, D), totals[0], totals[1], totals[2], totals[3], totals[4], totals[5], totals[6], totals[7], totals[8], totals[9])
```

```python
import functools
import jax
import jax.numpy as jnp
from jax import lax
from jax.sharding import PartitionSpec as P
from jax.experimental import pallas as pl
from jax.experimental.pallas import tpu as pltpu


HEADS = 12
HEAD_DIM = 64
SW = 128
POOL_HEADS = 2
SEQ = 128
LAYER = 3
MESH = pl.DeviceIdType.MESH
BF = jnp.bfloat16
F32 = jnp.float32
KINDS = ("cols", "cols", "cols", "rows", "small")
ORDERS = ((("y", "z", "x"), ("z", "x", "y"), ("y", "x", "z")),
          (("z", "y", "x"), ("z", "x", "y"), ("y", "x", "z")))


class Place:
    def __init__(self):
        wide, grp = lax.axis_index("wide"), lax.axis_index("grp")
        self.xl, self.z, self.y = wide // 16, (wide // 4) % 4, wide % 4
        self.x = (grp // 2) * 2 + self.xl
        self.core = grp % 2

    def near(self, axis, step):
        x, y, z = self.x, self.y, self.z
        if axis == "x":
            x = (x + step + 4) % 4
        if axis == "y":
            y = (y + step + 4) % 4
        if axis == "z":
            z = (z + step + 4) % 4
        return ((x % 2) * 16 + z * 4 + y, (x // 2) * 2 + self.core)

    def sibling(self):
        return (self.xl * 16 + self.z * 4 + self.y, (self.x // 2) * 2 + 1 - self.core)

    def at(self, axis, step=0):
        if axis == "x":
            return (self.xl + step) % 2
        return ((self.y if axis == "y" else self.z) + step + 4) % 4

    def box(self, have, **fixed):
        out = []
        for axis in ("x", "z", "y"):
            if axis in fixed:
                out.append(fixed[axis])
            elif axis in have:
                out.append(slice(None))
            else:
                out.append(self.at(axis))
        return tuple(out)


def greet(place):
    barrier = pltpu.get_barrier_semaphore()
    ids = [place.near(a, s) for a in ("x", "y", "z") for s in (1, -1)] + [place.sibling()]
    for i in ids:
        pl.semaphore_signal(barrier, inc=1, device_id=i, device_id_type=MESH)
    pl.semaphore_wait(barrier, len(ids))


class Wire:
    def __init__(self, send, recv, first=0):
        self.send, self.recv, self.next = send, recv, first
        self.started = []

    def number(self):
        self.next += 1
        return self.next - 1

    def copy(self, n, src, dst, to):
        return pltpu.make_async_remote_copy(src_ref=src, dst_ref=dst, send_sem=self.send.at[n],
                                            recv_sem=self.recv.at[n], device_id=to, device_id_type=MESH)

    def go(self, n, src, dst, to):
        c = self.copy(n, src, dst, to)
        c.start()
        self.started.append(c)
        return c


def gather_unit(place, wire, sib, core, order, own, full):
    way = 1 if core == 0 else -1
    have = []
    for axis in order:
        mine = place.box(have)
        src = full(mine) if have else own
        if axis == "x":
            n = wire.number()
            c = wire.go(n, src, full(mine), place.near("x", way))
            yield
            got = place.box(have, x=place.at("x", 1))
            wire.copy(n, full(got), full(got), place.near("x", way)).wait_recv()
            sib(got)
        else:
            n1, n2, n3 = wire.number(), wire.number(), wire.number()
            wire.go(n1, src, full(mine), place.near(axis, way))
            wire.go(n2, src, full(mine), place.near(axis, -way))
            yield
            got = place.box(have, **{axis: place.at(axis, -way)})
            wire.copy(n1, full(got), full(got), place.near(axis, way)).wait_recv()
            wire.go(n3, full(got), full(got), place.near(axis, way))
            sib(got)
            yield
            got = place.box(have, **{axis: place.at(axis, way)})
            wire.copy(n2, full(got), full(got), place.near(axis, way)).wait_recv()
            sib(got)
            got = place.box(have, **{axis: place.at(axis, 2)})
            wire.copy(n3, full(got), full(got), place.near(axis, way)).wait_recv()
            sib(got)
        have.append(axis)


EVENTS = 7


def boxes_of(place, core, order):
    way = 1 if core == 0 else -1
    have, out = [], []
    for axis in order:
        if axis == "x":
            out.append(place.box(have, x=place.at("x", 1)))
        else:
            out.extend(place.box(have, **{axis: place.at(axis, s)}) for s in (-way, way, 2))
        have.append(axis)
    return out


def piece(kind, core, k, width):
    unit = core * 3 + k
    if kind == "cols":
        return (slice(None), pl.ds(unit * (width // 6), width // 6))
    if kind == "rows":
        return (unit,)
    return (pl.ds(core * 16, 16),) if k == 1 else None


def gather_kernel(kinds, *refs):
    n = len(kinds)
    shards, fulls = refs[:n], refs[n:2 * n]
    send, recv, ssend, srecv, local = refs[2 * n:]
    place = Place()
    own_box = place.box(())
    greet(place)
    kept = [pltpu.make_async_remote_copy(src_ref=s, dst_ref=f.at[own_box], send_sem=local.at[i], recv_sem=local.at[n + i],
                                         device_id=place.sibling(), device_id_type=MESH)
            for i, (s, f) in enumerate(zip(shards, fulls))]
    for c in kept:
        c.start()

    def run(core):
        keep = list(kept)
        wire = Wire(send, recv)
        side = Wire(ssend, srecv, first=core * n * 3 * EVENTS)
        units = []
        for i, kind in enumerate(kinds):
            for k in range(3):
                tail = piece(kind, core, k, shards[i].shape[-1])
                if tail is None:
                    continue
                full = functools.partial(lambda f, t, b: f.at[b + t], fulls[i], tail)

                def sib(b, full=full):
                    side.go(side.number(), full(b), full(b), place.sibling())

                units.append(gather_unit(place, wire, sib, core, ORDERS[core][k], shards[i].at[tail], full))
        live, begun = units, False
        while live:
            still = []
            if begun and keep:
                for c in keep:
                    c.wait()
                keep.clear()
            begun = True
            for u in live:
                try:
                    next(u)
                    still.append(u)
                except StopIteration:
                    pass
            live = still
        other = Wire(ssend, srecv, first=(1 - core) * n * 3 * EVENTS)
        todo = []
        for i, kind in enumerate(kinds):
            for k in range(3):
                tail = piece(kind, 1 - core, k, shards[i].shape[-1])
                if tail is not None:
                    todo.append((fulls[i], tail, boxes_of(place, 1 - core, ORDERS[1 - core][k]), ORDERS[1 - core][k]))
        for f, tail, b in in_turn(todo):
            r = f.at[b + tail]
            other.copy(other.number(), r, r, place.sibling()).wait_recv()
        for c in wire.started + side.started:
            c.wait_send()

    pl.when(place.core == 0)(lambda: run(0))
    pl.when(place.core == 1)(lambda: run(1))


def in_turn(todo):
    stages = []
    for f, tail, boxes, order in todo:
        per, at = [], 0
        for axis in order:
            if axis == "x":
                per.append(1)
            else:
                per.extend((1, 2))
        groups = []
        for p in per:
            groups.append(boxes[at:at + p])
            at += p
        stages.append((f, tail, groups))
    for s in range(5):
        for f, tail, groups in stages:
            for b in groups[s]:
                yield f, tail, b


def gather_all(shards, kinds, cid):
    n = len(shards)
    count = n * 3 * EVENTS
    return pl.pallas_call(
        functools.partial(gather_kernel, kinds),
        out_shape=[jax.ShapeDtypeStruct((2, 4, 4) + s.shape, s.dtype) for s in shards],
        in_specs=[pl.BlockSpec(memory_space=pl.ANY)] * n,
        out_specs=[pl.BlockSpec(memory_space=pl.ANY)] * n,
        scratch_shapes=[pltpu.SemaphoreType.DMA((count,)), pltpu.SemaphoreType.DMA((count,)),
                        pltpu.SemaphoreType.DMA((2 * count,)), pltpu.SemaphoreType.DMA((2 * count,)),
                        pltpu.SemaphoreType.DMA((2 * n,))],
        compiler_params=pltpu.CompilerParams(collective_id=cid, has_side_effects=True),
        name="gather_weights",
    )(*shards)


def whole(dims, step):
    count = 1
    for d in dims:
        count *= d

    def one(i, carry):
        index, rest = [], i
        for d in reversed(dims):
            index.append(rest % d)
            rest = rest // d
        step(tuple(reversed(index)))
        return carry

    if count == 1:
        step((0,) * len(dims))
    else:
        lax.fori_loop(0, count, one, 0)


SIZE = {"x": 2, "z": 4, "y": 4}


def landing(order):
    out = []
    left = [a for a in ("x", "z", "y")]
    for axis in reversed(order):
        left = [a for a in left if a != axis]
        dims = tuple(SIZE[a] for a in left)
        out.append((1 if axis == "x" else 3, dims))
    return out


def add_box(place, held, left, fixed, terms):
    dims = tuple(SIZE[a] for a in left)

    def step(index):
        at = dict(zip(left, index))
        b = tuple(fixed[a] if a in fixed else at[a] if a in at else place.at(a) for a in ("x", "z", "y"))
        total = held[b]
        for t in terms:
            total = total + t[index]
        held[b] = total

    whole(dims, step)


def reduce_unit(place, wire, side, core, order, mine, theirs, first, held, lands, last, result, put):
    way = 1 if core == 0 else -1
    n = side.number()
    side.go(n, theirs, first, place.sibling())
    yield
    side.other(n, first).wait_recv()

    def start(index):
        held[index] = mine[index] + first[index]

    whole((2, 4, 4), start)
    left = ["x", "z", "y"]
    for axis, bufs in zip(reversed(order), lands):
        left = [a for a in left if a != axis]
        mine_at = place.at(axis)
        if axis == "x":
            n = wire.number()
            wire.go(n, held.at[place.box(left, x=place.at("x", 1))], bufs[0], place.near("x", way))
            yield
            wire.copy(n, bufs[0], bufs[0], place.near("x", way)).wait_recv()
            add_box(place, held, left, {axis: mine_at}, [bufs[0]])
        else:
            n1, n2, n3 = wire.number(), wire.number(), wire.number()
            ahead, back = place.near(axis, way), place.near(axis, -way)
            wire.go(n1, held.at[place.box(left, **{axis: place.at(axis, 2)})], bufs[0], ahead)
            wire.go(n2, held.at[place.box(left, **{axis: place.at(axis, -way)})], bufs[1], back)
            yield
            wire.copy(n1, bufs[0], bufs[0], ahead).wait_recv()
            add_box(place, held, left, {axis: place.at(axis, way)}, [bufs[0]])
            wire.go(n3, held.at[place.box(left, **{axis: place.at(axis, way)})], bufs[2], ahead)
            yield
            wire.copy(n2, bufs[1], bufs[1], ahead).wait_recv()
            wire.copy(n3, bufs[2], bufs[2], ahead).wait_recv()
            add_box(place, held, left, {axis: mine_at}, [bufs[1], bufs[2]])
    n = wire.number()
    own = place.box(())
    wire.go(n, held.at[own], last, place.near("x", 2))
    yield
    wire.copy(n, last, last, place.near("x", 2)).wait_recv()
    total = held[own] + last[...]
    result[...] = total
    n = side.number()
    side.go(n, result, put[2], place.sibling())
    put[0][...] = total.astype(F32)
    yield
    side.other(n, put[2]).wait_recv()
    put[1][...] = put[2][...].astype(F32)


class Side(Wire):
    def other(self, n, dst):
        return self.copy(n, dst, dst, self.place.sibling())


def pieces_of(kinds, shapes):
    out = []
    for i, (kind, shape) in enumerate(zip(kinds, shapes)):
        for k in range(3):
            if kind == "cols":
                out.append((i, k, (shape[0], shape[1] // 6)))
            elif kind == "rows":
                out.append((i, k, shape[1:]))
            elif k == 1:
                out.append((i, k, (16, shape[1])))
    return out


def reduce_scratch(kinds, shapes):
    out = []
    for i, k, shape in pieces_of(kinds, shapes):
        for _ in range(2):
            out.append(pltpu.VMEM((2, 4, 4) + shape, BF))
        for copies, dims in landing(ORDERS[0][k]):
            for _ in range(copies):
                out.append(pltpu.VMEM(dims + shape, BF))
        for _ in range(3):
            out.append(pltpu.VMEM(shape, BF))
    return out


def reduce_kernel(kinds, shapes, *refs):
    n = len(kinds)
    grads, outs = refs[:n], refs[n:2 * n]
    scratch = list(refs[2 * n:-4])
    send, recv, ssend, srecv = refs[-4:]
    place = Place()
    greet(place)
    plan = []
    for i, k, shape in pieces_of(kinds, shapes):
        first, held = scratch.pop(0), scratch.pop(0)
        lands = []
        for copies, dims in landing(ORDERS[0][k]):
            lands.append([scratch.pop(0) for _ in range(copies)])
        last, result, twin = scratch.pop(0), scratch.pop(0), scratch.pop(0)
        plan.append((i, k, first, held, lands, last, result, twin))

    def run(core):
        wire, side = Wire(send, recv), Side(ssend, srecv)
        side.place = place
        units = []
        for i, k, first, held, lands, last, result, twin in plan:
            width = shapes[i][-1]
            mine, theirs = piece(kinds[i], core, k, width), piece(kinds[i], 1 - core, k, width)
            lead = (slice(None),) * 3
            units.append(reduce_unit(
                place, wire, side, core, ORDERS[core][k], grads[i].at[lead + mine], grads[i].at[lead + theirs],
                first, held, lands, last, result, (outs[i].at[mine], outs[i].at[theirs], twin)))
        live = units
        while live:
            still = []
            for u in live:
                try:
                    next(u)
                    still.append(u)
                except StopIteration:
                    pass
            live = still
        for c in wire.started + side.started:
            c.wait_send()

    pl.when(place.core == 0)(lambda: run(0))
    pl.when(place.core == 1)(lambda: run(1))


def reduce_all(grads, kinds, cid):
    shapes = tuple(g.shape[3:] for g in grads)
    n = len(grads)
    count = len(pieces_of(kinds, shapes))
    return pl.pallas_call(
        functools.partial(reduce_kernel, kinds, shapes),
        out_shape=[jax.ShapeDtypeStruct(s, F32) for s in shapes],
        in_specs=[pl.BlockSpec(memory_space=pltpu.VMEM)] * n,
        out_specs=[pl.BlockSpec(memory_space=pltpu.VMEM)] * n,
        scratch_shapes=reduce_scratch(kinds, shapes) + [
            pltpu.SemaphoreType.DMA((count * 8,)), pltpu.SemaphoreType.DMA((count * 8,)),
            pltpu.SemaphoreType.DMA((count * 2,)), pltpu.SemaphoreType.DMA((count * 2,))],
        compiler_params=pltpu.CompilerParams(collective_id=cid, has_side_effects=True, vmem_limit_bytes=60 * 2 ** 20),
        name="reduce_grads",
    )(*grads)


def layer_norm(hidden, gain):
    centre = hidden - jnp.mean(hidden, axis=-1, keepdims=True)
    spread = jnp.mean(centre * centre, axis=-1, keepdims=True)
    return centre * lax.rsqrt(spread + 1e-06) * gain


def pool_head(projected, pool_query, w_hid, w_cls):
    seq_count = projected.shape[0] // SEQ
    head_size = SW // POOL_HEADS
    pieces = projected.reshape(seq_count, SEQ, POOL_HEADS, head_size)
    queries = pool_query.reshape(POOL_HEADS, head_size)
    pool_scores = jnp.einsum(
        "bshd,hd->bsh", pieces, queries, precision=lax.Precision.HIGHEST
    ) * head_size ** (-0.5)
    pool_weights = jax.nn.softmax(pool_scores, axis=1)
    pooled = jnp.einsum(
        "bsh,bshd->bhd", pool_weights, pieces, precision=lax.Precision.HIGHEST
    ).reshape(seq_count, SW)
    hidden = jnp.tanh(jnp.dot(pooled, w_hid, precision=lax.Precision.HIGHEST))
    return jnp.dot(hidden, w_cls, precision=lax.Precision.HIGHEST)


def local(
    tokens,
    exit_layer,
    w_qkv,
    w_out,
    gain_attn,
    w_up,
    w_down,
    gain_ffn,
    w_proj,
    pool_query,
    w_hid,
    w_cls,
    cot_out,
    cot_logits,
):
    misc = jnp.concatenate([gain_attn, gain_ffn, pool_query, w_cls.reshape(-1)])
    misc = jnp.pad(misc, (0, 4 * 128 - misc.shape[0])).reshape(4, 128)
    small = jnp.concatenate([w_proj, w_hid, misc], axis=0)
    full = gather_all((w_qkv, w_out, w_up, w_down.reshape(6, 16, -1), small), KINDS, 0)
    full_qkv, full_out, full_up = (f.reshape(-1, f.shape[-1]) for f in full[:3])
    full_down = full[3].reshape(-1, full[3].shape[-1])
    small = full[4].reshape(32, 32, 128)
    full_proj = small[:, :24].reshape(768, 128)
    full_hid = small[:, 24:28].reshape(128, 128)
    misc = small[:, 28]
    full_g1, full_g2 = misc[:, :24].reshape(768), misc[:, 24:48].reshape(768)
    full_pool, full_cls = misc[:, 48:52].reshape(128), misc[:, 52:108].reshape(128, 14)
    tok_rows, model_width = tokens.shape
    seq_count = exit_layer.shape[0]
    scale = HEAD_DIM ** (-0.5)
    alive_seq = (exit_layer >= LAYER).astype(jnp.float32)
    alive_tok = jnp.repeat(alive_seq, SEQ)[:, None]
    merged = jnp.dot(tokens, full_qkv, preferred_element_type=jnp.float32).astype(jnp.bfloat16)
    stacked = merged.reshape(seq_count, SEQ, 3, HEADS, HEAD_DIM)
    queries = stacked[:, :, 0]
    key_part = stacked[:, :, 1]
    value_part = stacked[:, :, 2]
    scores = (
        jnp.einsum("bqhd,bkhd->bhqk", queries, key_part, preferred_element_type=jnp.float32) * scale
    )
    top = jnp.max(scores, axis=-1, keepdims=True)
    log_total = top + jnp.log(jnp.sum(jnp.exp(scores - top), axis=-1, keepdims=True))
    probs = jnp.exp(scores - log_total).astype(jnp.bfloat16)
    context = (
        jnp.einsum("bhqk,bkhd->bqhd", probs, value_part, preferred_element_type=jnp.float32)
        .reshape(tok_rows, model_width)
        .astype(jnp.bfloat16)
    )
    mixed = tokens.astype(jnp.float32) + jnp.dot(
        context, full_out, preferred_element_type=jnp.float32
    )
    normed_f, norm1_pull = jax.vjp(layer_norm, mixed, full_g1.astype(jnp.float32))
    normed = normed_f.astype(jnp.bfloat16)
    upward = jnp.dot(normed, full_up, preferred_element_type=jnp.float32)
    active_f, gelu_pull = jax.vjp(jax.nn.gelu, upward)
    active = active_f.astype(jnp.bfloat16)
    second = normed.astype(jnp.float32) + jnp.dot(
        active, full_down, preferred_element_type=jnp.float32
    )
    output_f, norm2_pull = jax.vjp(layer_norm, second, full_g2.astype(jnp.float32))
    output = output_f.astype(jnp.bfloat16)
    projected = jnp.dot(output, full_proj, preferred_element_type=jnp.float32)
    student_out, head_pull = jax.vjp(
        pool_head,
        projected,
        full_pool.astype(jnp.float32),
        full_hid.astype(jnp.float32),
        full_cls.astype(jnp.float32),
    )
    activations = (output.astype(jnp.float32) * alive_tok).astype(jnp.bfloat16)
    logits = student_out * alive_seq[:, None]
    grad_projected, grad_pool, grad_hid, grad_cls = head_pull(cot_logits * alive_seq[:, None])
    proj_low = grad_projected.astype(jnp.bfloat16)
    grad_proj = jnp.einsum("nd,ns->ds", output, proj_low, preferred_element_type=jnp.float32)
    grad_output = cot_out.astype(jnp.float32) * alive_tok + jnp.einsum(
        "ns,ds->nd", proj_low, full_proj, preferred_element_type=jnp.float32
    )
    grad_second, grad_g2 = norm2_pull(grad_output)
    down_low = grad_second.astype(jnp.bfloat16)
    grad_down = jnp.einsum("nf,nd->fd", active, down_low, preferred_element_type=jnp.float32)
    grad_active = jnp.einsum("nd,fd->nf", down_low, full_down, preferred_element_type=jnp.float32)
    (grad_upward,) = gelu_pull(grad_active)
    up_low = grad_upward.astype(jnp.bfloat16)
    grad_up = jnp.einsum("nd,nf->df", normed, up_low, preferred_element_type=jnp.float32)
    grad_normed = grad_second + jnp.einsum(
        "nf,df->nd", up_low, full_up, preferred_element_type=jnp.float32
    )
    grad_mixed, grad_g1 = norm1_pull(grad_normed)
    attn_low = grad_mixed.astype(jnp.bfloat16)
    grad_out = jnp.einsum("ni,nd->id", context, attn_low, preferred_element_type=jnp.float32)
    context_low = jnp.einsum(
        "nd,id->ni", attn_low, full_out, preferred_element_type=jnp.float32
    ).astype(jnp.bfloat16)
    context_low = context_low.reshape(seq_count, SEQ, HEADS, HEAD_DIM)
    probs_f = jnp.exp(
        jnp.einsum("bqhd,bkhd->bhqk", queries, key_part, preferred_element_type=jnp.float32) * scale
        - log_total
    )
    probs_low = probs_f.astype(jnp.bfloat16)
    grad_probs = jnp.einsum(
        "bqhd,bkhd->bhqk", context_low, value_part, preferred_element_type=jnp.float32
    )
    grad_values = jnp.einsum(
        "bhqk,bqhd->bkhd", probs_low, context_low, preferred_element_type=jnp.float32
    )
    grad_scores = probs_f * (grad_probs - jnp.sum(probs_f * grad_probs, axis=-1, keepdims=True))
    scores_low = grad_scores.astype(jnp.bfloat16)
    grad_queries = (
        jnp.einsum("bhqk,bkhd->bqhd", scores_low, key_part, preferred_element_type=jnp.float32)
        * scale
    )
    grad_keys = (
        jnp.einsum("bhqk,bqhd->bkhd", scores_low, queries, preferred_element_type=jnp.float32)
        * scale
    )
    merged_low = (
        jnp.stack([grad_queries, grad_keys, grad_values], axis=2)
        .reshape(tok_rows, 3 * model_width)
        .astype(jnp.bfloat16)
    )
    grad_qkv = jnp.einsum("nd,nc->dc", tokens, merged_low, preferred_element_type=jnp.float32)
    grad_tokens = grad_mixed + jnp.einsum(
        "nc,dc->nd", merged_low, full_qkv, preferred_element_type=jnp.float32
    )
    misc = jnp.concatenate(
        [grad_g1.reshape(32, 24), grad_g2.reshape(32, 24), grad_pool.reshape(32, 4), grad_cls.reshape(32, 56)], axis=1
    )
    misc = jnp.pad(misc, ((0, 0), (0, 4 * 128 - misc.shape[1]))).reshape(32, 4, 128)
    small = jnp.concatenate([grad_proj.reshape(32, 24, 128), grad_hid.reshape(32, 4, 128), misc], axis=1)
    sums = reduce_all(
        (
            grad_qkv.astype(BF).reshape(2, 4, 4, 24, -1),
            grad_out.astype(BF).reshape(2, 4, 4, 24, -1),
            grad_up.astype(BF).reshape(2, 4, 4, 24, -1),
            grad_down.astype(BF).reshape(2, 4, 4, 6, 16, -1),
            small.astype(BF).reshape(2, 4, 4, 32, 128),
        ),
        KINDS,
        1,
    )
    small = sums[4]
    misc = small[28]
    summed = (
        sums[0], sums[1], misc[:24], sums[2], sums[3].reshape(96, -1), misc[24:48],
        small[:24], misc[48:52], small[24:28], misc[52:108].reshape(4, 14),
    )
    return (
        activations,
        logits,
        grad_tokens,
        summed[0],
        summed[1],
        summed[2],
        summed[3],
        summed[4],
        summed[5],
        summed[6],
        summed[7],
        summed[8],
        summed[9],
    )


def solution(mesh):
    in_specs = (
        P(("wide", "grp"), None),
        P(("wide", "grp")),
        P("wide", None),
        P("wide", None),
        P("wide"),
        P("wide", None),
        P("wide", None),
        P("wide"),
        P("wide", None),
        P("wide"),
        P("wide", None),
        P("wide", None),
        P(("wide", "grp"), None),
        P(("wide", "grp"), None),
    )
    out_specs = (
        P(("wide", "grp"), None),
        P(("wide", "grp"), None),
        P(("wide", "grp"), None),
        P("wide", None),
        P("wide", None),
        P("wide"),
        P("wide", None),
        P("wide", None),
        P("wide"),
        P("wide", None),
        P("wide"),
        P("wide", None),
        P("wide", None),
    )
    return jax.shard_map(local, mesh=mesh, in_specs=in_specs, out_specs=out_specs, check_vma=False)
```

```python
import functools
import jax
import jax.numpy as jnp
from jax import lax
from jax.sharding import PartitionSpec as P
from jax.experimental import pallas as pl
from jax.experimental.pallas import tpu as pltpu

D = 768
FF = 3072
TOK = 768
SEQ_DEV = 6
PAIRS = 6
SEQ = 128
LAYER = 3
MESH = pl.DeviceIdType.MESH
BF = jnp.bfloat16
F32 = jnp.float32
SIZE = {"x": 2, "z": 4, "y": 4}
ORDERS = (
    (("y", "z", "x"), ("z", "x", "y"), ("y", "x", "z")),
    (("z", "y", "x"), ("z", "x", "y"), ("y", "x", "z")),
)
EVENTS = 7
SUMS = 8
VMEM = 62 * 2**20


class Place:
    def __init__(self):
        wide, grp = lax.axis_index("wide"), lax.axis_index("grp")
        xl, z, y = wide // 16, (wide // 4) % 4, wide % 4
        x = (grp // 2) * 2 + xl
        self.core = grp % 2
        self.places = {("x", 0): xl, ("x", 1): 1 - xl}
        for axis, here in (("z", z), ("y", y)):
            for step in range(4):
                self.places[axis, step] = (here + step) % 4
        self.ids = {}
        for step in (1, 2, 3):
            far = (x + step) % 4
            self.ids["x", step] = ((far % 2) * 16 + z * 4 + y, (far // 2) * 2 + self.core)
            self.ids["y", step] = (xl * 16 + z * 4 + self.places["y", step], grp)
            self.ids["z", step] = (xl * 16 + self.places["z", step] * 4 + y, grp)
        self.sibling = (wide, grp + 1 - 2 * self.core)

    def near(self, axis, step):
        return self.ids[axis, step % 4]

    def at(self, axis, step=0):
        return self.places[axis, step % SIZE[axis]]

    def box(self, have, **fixed):
        out = []
        for axis in ("x", "z", "y"):
            if axis in fixed:
                out.append(fixed[axis])
            elif axis in have:
                out.append(slice(None))
            else:
                out.append(self.at(axis))
        return tuple(out)

    def on_core(self, step):
        for core in (0, 1):
            pl.when(self.core == core)(functools.partial(step, core))


def greet(place):
    barrier = pltpu.get_barrier_semaphore()
    ids = [place.near(a, s) for a in ("x", "y", "z") for s in (1, -1)] + [place.near("x", 2), place.sibling]
    for i in ids:
        pl.semaphore_signal(barrier, inc=1, device_id=i, device_id_type=MESH)
    pl.semaphore_wait(barrier, len(ids))


class Wire:
    def __init__(self, send, recv):
        self.send, self.recv = send, recv
        self.started = []

    def copy(self, n, src, dst, to):
        return pltpu.make_async_remote_copy(
            src_ref=src, dst_ref=dst, send_sem=self.send.at[n], recv_sem=self.recv.at[n],
            device_id=to, device_id_type=MESH,
        )

    def go(self, n, src, dst, to):
        self.copy(n, src, dst, to).start()
        self.started.append((n, src, dst, to))

    def landed(self, n, dst, to):
        self.copy(n, dst, dst, to).wait_recv()

    def sent(self):
        for c in self.started:
            self.copy(*c).wait_send()


def piece(kind, core, k, width):
    if kind == "cols":
        return (slice(None), pl.ds((core * 3 + k) * (width // 6), width // 6))
    return (pl.ds(core * 16, 16), slice(None)) if k == 1 else None


def gather_unit(place, wire, base, sib, core, order, own, full):
    way = 1 if core == 0 else -1
    have, e = [], 0
    for axis in order:
        mine = place.box(have)
        src = full(mine) if have else own
        ahead, back = place.near(axis, way), place.near(axis, -way)
        if axis == "x":
            wire.go(base + e, src, full(mine), ahead)
            yield
            got = place.box(have, x=place.at("x", 1))
            wire.landed(base + e, full(got), ahead)
            sib(e, got)
            e += 1
        else:
            wire.go(base + e, src, full(mine), ahead)
            wire.go(base + e + 1, src, full(mine), back)
            yield
            got = place.box(have, **{axis: place.at(axis, -way)})
            wire.landed(base + e, full(got), ahead)
            wire.go(base + e + 2, full(got), full(got), ahead)
            sib(e, got)
            yield
            for late, step in ((1, way), (2, 2)):
                got = place.box(have, **{axis: place.at(axis, step)})
                wire.landed(base + e + late, full(got), ahead)
                sib(e + late, got)
            e += 3
        have.append(axis)


def passed_on(place, core, order):
    way = 1 if core == 0 else -1
    have, out = [], []
    for axis in order:
        if axis == "x":
            out.append(place.box(have, x=place.at("x", 1)))
        else:
            out.extend(place.box(have, **{axis: place.at(axis, s)}) for s in (-way, way, 2))
        have.append(axis)
    return out


class Gather:
    def __init__(self, place, kinds, shards, fulls, send, recv, ssend, srecv, lsem):
        self.place, self.kinds, self.shards, self.fulls = place, kinds, shards, fulls
        self.wires = [Wire(send, recv) for _ in range(2)]
        self.sides = [Wire(ssend, srecv) for _ in range(2)]
        self.keep = Wire(lsem, lsem)
        n = len(kinds)
        self.units = [[[] for _ in range(n)] for _ in range(2)]
        for core in range(2):
            for i in range(n):
                for k in range(3):
                    tail = self.tail(core, i, k)
                    if tail is None:
                        continue
                    full = functools.partial(self.part, i, tail)
                    sib = functools.partial(self.pass_on, core, i, k, full)
                    self.units[core][i].append(gather_unit(
                        place, self.wires[core], (i * 3 + k) * EVENTS, sib, core, ORDERS[core][k],
                        shards[i].at[tail], full))

    def tail(self, core, i, k):
        return piece(self.kinds[i], core, k, self.shards[i].shape[-1])

    def part(self, i, tail, box):
        return self.fulls[i].at[box + tail]

    def number(self, core, i, k, e):
        return ((core * len(self.kinds) + i) * 3 + k) * EVENTS + e

    def pass_on(self, core, i, k, full, e, box):
        self.sides[core].go(self.number(core, i, k, e), full(box), full(box), self.place.sibling)

    def own(self):
        n = len(self.kinds)
        for i in range(n):
            src, dst = self.shards[i], self.fulls[i].at[self.place.box(())]
            pltpu.make_async_remote_copy(src_ref=src, dst_ref=dst, send_sem=self.keep.send.at[i],
                                         recv_sem=self.keep.send.at[n + i], device_id=self.place.sibling,
                                         device_id_type=MESH).start()

    def own_landed(self):
        n = len(self.kinds)
        for i in range(n):
            src, dst = self.shards[i], self.fulls[i].at[self.place.box(())]
            pltpu.make_async_remote_copy(src_ref=src, dst_ref=dst, send_sem=self.keep.send.at[i],
                                         recv_sem=self.keep.send.at[n + i], device_id=self.place.sibling,
                                         device_id_type=MESH).wait()

    def step(self, *arrays):
        def one(core):
            for i in arrays:
                for u in self.units[core][i]:
                    next(u, None)

        self.place.on_core(one)

    def whole(self, *arrays):
        def one(core):
            other = 1 - core
            for i in arrays:
                for k in range(3):
                    tail = self.tail(other, i, k)
                    if tail is None:
                        continue
                    for e, box in enumerate(passed_on(self.place, other, ORDERS[other][k])):
                        self.sides[other].landed(self.number(other, i, k, e), self.part(i, tail, box),
                                                 self.place.sibling)

        self.place.on_core(one)

    def end(self):
        def one(core):
            self.wires[core].sent()
            self.sides[core].sent()

        self.place.on_core(one)


def dot(a, b, dims=((1,), (0,))):
    return lax.dot_general(a, b, (dims, ((), ())), preferred_element_type=F32)


def exact(a, b, dims=((1,), (0,))):
    return lax.dot_general(a, b, (dims, ((), ())), precision=lax.Precision.HIGHEST, preferred_element_type=F32)


def iota(shape, dim):
    return lax.broadcasted_iota(jnp.int32, shape, dim)


def over24(i):
    return (i * 2731) >> 16


def ones_where(hit):
    return jnp.where(hit, 1.0, 0.0).astype(BF)


def picks():
    i, j = iota((768, 1024), 0), iota((768, 1024), 1)
    proj = ones_where(j == i + 8 * over24(i))
    i, j = iota((128, 1024), 0), iota((128, 1024), 1)
    at = 32 * (i >> 2) + (i & 3)
    hid, cls = ones_where(j == at + 24), ones_where(j == at + 28)
    i, j = iota((32, 1024), 0), iota((32, 1024), 1)
    misc = ones_where(j == 32 * i + 28)
    return proj, hid, cls, misc


def spread(first, size, per):
    i, l = iota((128, size), 0), iota((128, size), 1)
    block = over24(l) if per == 24 else l >> 2
    w, m = iota((32, size), 0), iota((32, size), 1)
    held = over24(m) if per == 24 else m >> 2
    return ones_where(i - first == l - per * block), held == w


ROWS = (("gain_attn", 16, 768, 24), ("gain_ffn", 40, 768, 24), ("pool", 64, 128, 4))


def normalise(h):
    centre = h - jnp.mean(h, axis=-1, keepdims=True)
    r = lax.rsqrt(jnp.mean(centre * centre, axis=-1, keepdims=True) + 1e-06)
    return centre * r, r


def norm_back(g, gain, n, r):
    gn = g * gain
    return r * (gn - jnp.mean(gn, axis=-1, keepdims=True) - n * jnp.mean(gn * n, axis=-1, keepdims=True))


TANH_A = 0.7978845608028654
TANH_B = 0.7978845608028654 * 0.044715


def gelu(u):
    u2 = u * u
    h = 0.5 + 0.5 * jnp.tanh(u * (TANH_A + TANH_B * u2))
    y = u * h
    return y, h + y * (1.0 - h) * (2.0 * TANH_A + 6.0 * TANH_B * u2)


def at_block(i):
    return i // 8, (i // 2) % 4, i % 2


def join(blocks, whole):
    def one(i, carry):
        x, z, y = at_block(i)
        pair = jnp.concatenate([blocks[x, z, 2 * y], blocks[x, z, 2 * y + 1]], axis=0)
        whole[pl.ds(pl.multiple_of(i * 48, 48), 48), :] = pair
        return carry

    lax.fori_loop(0, 16, one, 0)


def loop(n, step):
    def one(i, carry):
        step(i)
        return carry

    lax.fori_loop(0, n, one, 0)


def span(i, size):
    return pl.ds(pl.multiple_of(i * size, size), size)


def halves():
    lane = iota((1, 128), 1)
    return jnp.where(lane < 64, 1.0, 0.0), jnp.where(lane < 64, 0.0, 1.0)


KINDS = ("small", "cols", "cols", "cols", "cols")
SMALL, QKV, OUT, UP, DOWN = range(5)


def forward_kernel(tokens, cot, alive, alive_seq, cotl, s_small, s_qkv, s_out, s_up, s_down,
                   o_act, o_logits, o_wqkv, o_wout, o_wup, o_wdown, o_merged, o_probs, o_ctx, o_normed, o_n1, o_r1,
                   o_active, o_dact, o_gsec, o_dlow, o_tokens2, o_small, rows,
                   b_small, b_qkv, b_out, b_up, b_down, w_qkv, w_out, w_up, tok, cotv, merged, probs, ctx, normed, n1, r1,
                   active, dact, gsec, r2, dlow, out, projected, gproj, wproj, hid, cls,
                   send, recv, ssend, srecv, lsem, insem, outsem, xsend, xrecv):
    place = Place()
    loads = [pltpu.make_async_copy(tokens, tok, insem.at[0]), pltpu.make_async_copy(cot, cotv, insem.at[1])]
    for c in loads:
        c.start()
    greet(place)
    g = Gather(place, KINDS, (s_small, s_qkv, s_out, s_up, s_down), (b_small, b_qkv, b_out, b_up, b_down),
               send, recv, ssend, srecv, lsem)
    stores = []
    cross = Wire(xsend, xrecv)

    def keep(src, dst):
        c = pltpu.make_async_copy(src, dst, outsem.at[len(stores)])
        c.start()
        stores.append(c)

    def share(n, src, dst):
        keep(src, dst.at[0])
        cross.go(n, src, dst.at[1], place.sibling)

    g.step(QKV, OUT, SMALL, UP, DOWN)
    g.own()
    loads[0].wait()
    share(0, tok, o_tokens2)
    g.own_landed()
    g.step(QKV, OUT, SMALL, UP, DOWN)
    g.step(QKV, OUT, SMALL, UP, DOWN)
    g.step(QKV, OUT, SMALL)
    g.step(QKV, OUT, SMALL)
    g.step(UP, DOWN)
    g.step(QKV, SMALL)
    g.step(UP, DOWN)
    g.whole(QKV, SMALL)
    join(b_qkv, w_qkv)

    def qkv(j):
        c = span(j, 384)
        merged[:, c] = dot(tok[...], w_qkv[:, c]).astype(BF)

    loop(6, qkv)
    keep(w_qkv, o_wqkv)
    keep(merged, o_merged)

    p_proj, p_hid, p_cls, p_misc = picks()
    pack = b_small[...].reshape(1024, 128)
    wproj[...] = dot(p_proj, pack).astype(BF)
    hid[...] = dot(p_hid, pack)
    cls[...] = jnp.where(iota((128, 128), 1) < 14, dot(p_cls, pack), 0.0)
    misc = dot(p_misc, pack).astype(BF)
    for n, (name, first, size, per) in enumerate(ROWS):
        tile, held = spread(first, size, per)
        row = jnp.sum(jnp.where(held, dot(misc, tile), 0.0), axis=0, keepdims=True)
        rows[n, :, pl.ds(0, size)] = jnp.broadcast_to(row, (8, size))
    low_half, high_half = halves()
    g.step(OUT)

    qa, qb = (low_half * 0.125).astype(BF), (high_half * 0.125).astype(BF)

    def attend(s):
        r = span(s, SEQ)
        for p in range(PAIRS):
            q, k, v = (merged[r, pl.ds(768 * a + 128 * p, 128)] for a in range(3))
            scores = dot(jnp.concatenate([q * qa, q * qb], axis=0), k, ((1,), (1,)))
            e = jnp.exp(scores - jnp.max(scores, axis=-1, keepdims=True))
            pr = (e * (1.0 / jnp.sum(e, axis=-1, keepdims=True))).astype(BF)
            probs[s * PAIRS + p] = pr
            both = dot(pr, v)
            ctx[r, pl.ds(128 * p, 128)] = (both[:SEQ] * low_half + both[SEQ:] * high_half).astype(BF)

    loop(SEQ_DEV, attend)
    keep(probs, o_probs)
    share(1, ctx, o_ctx)
    g.whole(OUT)
    join(b_out, w_out)
    gain1 = rows[0, pl.ds(0, 1), :]

    def mix(j):
        r = span(j, 384)
        n, inv = normalise(tok[r, :].astype(F32) + dot(ctx[r, :], w_out[...]))
        n1[r, :] = n.astype(BF)
        normed[r, :] = (n * gain1).astype(BF)
        r1[r, :] = jnp.broadcast_to(inv, (384, 128))

    loop(2, mix)
    keep(w_out, o_wout)
    keep(n1, o_n1)
    keep(r1, o_r1)
    share(2, normed, o_normed)
    g.step(UP)
    g.whole(UP)
    join(b_up, w_up)

    def upward(j):
        c = span(j, 512)
        y, dy = gelu(dot(normed[...], w_up[:, c]))
        active[:, c] = y.astype(BF)
        dact[:, c] = dy.astype(BF)

    loop(6, upward)
    share(3, active, o_active)
    keep(dact, o_dact)
    keep(w_up, o_wup)
    g.step(DOWN)
    g.whole(DOWN)
    keep(b_down, o_wdown)
    loads[1].wait()
    gain2 = rows[1, pl.ds(0, 1), :]

    def downward(j):
        r = span(j, 384)
        second = normed[r, :].astype(F32) + dot(active[r, :], b_down[...].reshape(FF, D))
        n, inv = normalise(second)
        gsec[r, :] = n
        r2[r, :] = jnp.broadcast_to(inv, (384, 128))
        low = (n * gain2).astype(BF)
        out[r, :] = low
        projected[r, :] = dot(low, wproj[...])

    loop(2, downward)

    query = rows[2, pl.ds(0, 1), pl.ds(0, 128)]
    whole = low_half + high_half
    weights, pooled = [], []
    for s in range(SEQ_DEV):
        pr = projected[pl.ds(s * SEQ, SEQ), :]
        t = pr * query
        per_head = []
        for half in (low_half, high_half):
            score = jnp.sum(t * half, axis=-1, keepdims=True) * 0.125
            e = jnp.exp(score - jnp.max(score, axis=0, keepdims=True))
            per_head.append(e / jnp.sum(e, axis=0, keepdims=True))
        weights.append(per_head)
        pooled.append(jnp.sum(pr * (per_head[0] * low_half + per_head[1] * high_half), axis=0, keepdims=True))
    none = jnp.zeros((1, 128), F32)
    pooled = jnp.concatenate(pooled + [none, none], axis=0)
    hidden = jnp.tanh(exact(pooled, hid[...]))
    o_logits[...] = exact(hidden, cls[...]) * alive_seq[...]
    g_log = cotl[...] * alive_seq[...]
    o_small[1] = exact(hidden, g_log, ((0,), (0,))).astype(BF)
    g_pre = exact(g_log, cls[...], ((1,), (1,))) * (1.0 - hidden * hidden)
    o_small[0] = exact(pooled, g_pre, ((0,), (0,))).astype(BF)
    g_pooled = exact(g_pre, hid[...], ((1,), (1,)))
    g_query = none
    for s in range(SEQ_DEV):
        r = pl.ds(s * SEQ, SEQ)
        pr = projected[r, :]
        gp = g_pooled[s:s + 1]
        t = pr * gp
        total = (weights[s][0] * low_half + weights[s][1] * high_half) * gp
        for half, w in zip((low_half, high_half), weights[s]):
            dw = jnp.sum(t * half, axis=-1, keepdims=True)
            ds = w * (dw - jnp.sum(w * dw, axis=0, keepdims=True)) * 0.125
            total = total + ds * (query * half)
            g_query = g_query + jnp.sum(ds * pr, axis=0, keepdims=True) * half
        gproj[r, :] = total.astype(BF)
    o_small[2] = jnp.broadcast_to(g_query, (128, 128)).astype(BF)

    def back(j):
        r = span(j, 384)
        keep_tok = alive[r, pl.ds(0, 1)]
        low = out[r, :]
        g_out = keep_tok * cotv[r, :].astype(F32) + dot(gproj[r, :], wproj[...], ((1,), (1,)))
        n = gsec[r, :]
        part = jnp.sum(g_out * n, axis=0, keepdims=True)
        rows[3, pl.ds(0, 1), :] = jnp.where(j == 0, part, part + rows[3, pl.ds(0, 1), :])
        g2 = norm_back(g_out, gain2, n, r2[r, pl.ds(0, 1)])
        gsec[r, :] = g2
        dlow[r, :] = g2.astype(BF)
        cotv[r, :] = (keep_tok * low.astype(F32)).astype(BF)

    loop(2, back)
    share(4, dlow, o_dlow)
    keep(gsec, o_gsec)
    keep(cotv, o_act)
    o_small[3:9] = dot(out[...], gproj[...], ((0,), (0,))).astype(BF).reshape(6, 128, 128)
    g.end()
    for c in stores:
        c.wait()
    for n, src, dst in ((0, tok, o_tokens2), (1, ctx, o_ctx), (2, normed, o_normed), (3, active, o_active), (4, dlow, o_dlow)):
        cross.landed(n, dst.at[1], place.sibling)
    cross.sent()


def forward(tokens, cot, alive, alive_seq, cotl, shards):
    hbm, vmem = pl.BlockSpec(memory_space=pl.ANY), pl.BlockSpec(memory_space=pltpu.VMEM)
    n = len(KINDS)
    count = n * 3 * EVENTS

    def arr(*shape, dtype=BF):
        return jax.ShapeDtypeStruct(shape, dtype)

    outs = [
        (arr(TOK, D), hbm), (arr(8, 128, dtype=F32), vmem),
        (arr(D, 3 * D), hbm), (arr(D, D), hbm), (arr(D, FF), hbm), (arr(2, 4, 4, 96, D), hbm),
        (arr(TOK, 3 * D), hbm), (arr(SEQ_DEV * PAIRS, 256, 128), hbm), (arr(2, TOK, D), hbm), (arr(2, TOK, D), hbm),
        (arr(TOK, D), hbm), (arr(TOK, 128, dtype=F32), hbm), (arr(2, TOK, FF), hbm), (arr(TOK, FF), hbm),
        (arr(TOK, D, dtype=F32), hbm), (arr(2, TOK, D), hbm), (arr(2, TOK, D), hbm),
        (arr(9, 128, 128), vmem), (arr(4, 8, D, dtype=F32), vmem),
    ]
    dma = pltpu.SemaphoreType.DMA
    scratch = [
        pltpu.VMEM((2, 4, 4, 32, 128), BF), pltpu.VMEM((2, 4, 4, 24, 3 * D), BF), pltpu.VMEM((2, 4, 4, 24, D), BF),
        pltpu.VMEM((2, 4, 4, 24, FF), BF), pltpu.VMEM((2, 4, 4, 96, D), BF),
        pltpu.VMEM((D, 3 * D), BF), pltpu.VMEM((D, D), BF), pltpu.VMEM((D, FF), BF),
        pltpu.VMEM((TOK, D), BF), pltpu.VMEM((TOK, D), BF), pltpu.VMEM((TOK, 3 * D), BF),
        pltpu.VMEM((SEQ_DEV * PAIRS, 256, 128), BF), pltpu.VMEM((TOK, D), BF), pltpu.VMEM((TOK, D), BF),
        pltpu.VMEM((TOK, D), BF), pltpu.VMEM((TOK, 128), F32), pltpu.VMEM((TOK, FF), BF), pltpu.VMEM((TOK, FF), BF),
        pltpu.VMEM((TOK, D), F32), pltpu.VMEM((TOK, 128), F32), pltpu.VMEM((TOK, D), BF), pltpu.VMEM((TOK, D), BF),
        pltpu.VMEM((TOK, 128), F32), pltpu.VMEM((TOK, 128), BF), pltpu.VMEM((D, 128), BF),
        pltpu.VMEM((128, 128), F32), pltpu.VMEM((128, 128), F32),
        dma((count,)), dma((count,)), dma((2 * count,)), dma((2 * count,)), dma((2 * n,)),
        dma((2,)), dma((20,)), dma((5,)), dma((5,)),
    ]
    return pl.pallas_call(
        forward_kernel,
        out_shape=[o for o, _ in outs],
        in_specs=[hbm, hbm, vmem, vmem, vmem] + [hbm] * n,
        out_specs=[s for _, s in outs],
        scratch_shapes=scratch,
        compiler_params=pltpu.CompilerParams(collective_id=0, has_side_effects=True, vmem_limit_bytes=VMEM),
        cost_estimate=pl.CostEstimate(flops=12 * 10**9, bytes_accessed=60 * 10**6, transcendentals=4 * 10**6),
        name="forward",
    )(tokens, cot, alive, alive_seq, cotl, *shards)


def landing(order):
    out, left = [], ["x", "z", "y"]
    for axis in reversed(order):
        left = [a for a in left if a != axis]
        out.append((1 if axis == "x" else 3, tuple(SIZE[a] for a in left)))
    return out


def add_box(place, held, left, fixed, terms):
    dims = tuple(SIZE[a] for a in left)

    def step(i):
        index = []
        for d in reversed(dims):
            index.append(i % d)
            i = i // d
        index = tuple(reversed(index))
        at = dict(zip(left, index))
        b = tuple(fixed[a] if a in fixed else at[a] if a in at else place.at(a) for a in ("x", "z", "y"))
        total = held[b]
        for t in terms:
            total = total + t[index]
        held[b] = total

    if dims:
        count = 1
        for d in dims:
            count *= d
        loop(count, step)
    else:
        step(0)


def reduce_unit(place, wire, side, base, base2, core, order, held, lands, last, result, twin, put):
    way = 1 if core == 0 else -1
    left, e = ["x", "z", "y"], base
    for axis, bufs in zip(reversed(order), lands):
        left = [a for a in left if a != axis]
        ahead, back = place.near(axis, way), place.near(axis, -way)
        mine = {axis: place.at(axis)}
        if axis == "x":
            wire.go(e, held.at[place.box(left, x=place.at("x", 1))], bufs[0], ahead)
            yield
            wire.landed(e, bufs[0], ahead)
            add_box(place, held, left, mine, [bufs[0]])
            e += 1
        else:
            wire.go(e, held.at[place.box(left, **{axis: place.at(axis, 2)})], bufs[0], ahead)
            wire.go(e + 1, held.at[place.box(left, **{axis: place.at(axis, -way)})], bufs[1], back)
            yield
            wire.landed(e, bufs[0], ahead)
            onward = {axis: place.at(axis, way)}
            add_box(place, held, left, onward, [bufs[0]])
            wire.go(e + 2, held.at[place.box(left, **onward)], bufs[2], ahead)
            yield
            wire.landed(e + 1, bufs[1], ahead)
            wire.landed(e + 2, bufs[2], ahead)
            add_box(place, held, left, mine, [bufs[1], bufs[2]])
            e += 3
    own = place.box(())
    wire.go(e, held.at[own], last, place.near("x", 2))
    yield
    wire.landed(e, last, place.near("x", 2))
    total = held[own] + last[...]
    result[...] = total
    side.go(base2, result, twin, place.sibling)
    put[0][...] = total.astype(F32)
    yield
    side.landed(base2, twin, place.sibling)
    put[1][...] = twin[...].astype(F32)


STEPS = 8
PIECES = [(i, k) for i in (DOWN, UP, OUT, QKV, SMALL) for k in range(3) if i != SMALL or k == 1]


def piece_shape(i):
    return {SMALL: (16, 128), QKV: (24, 384), OUT: (24, 128), UP: (24, 512), DOWN: (96, 128)}[i]


def reduce_scratch():
    out = []
    for i, k in PIECES:
        shape = piece_shape(i)
        out.append(pltpu.VMEM((2, 4, 4) + shape, BF))
        for copies, dims in landing(ORDERS[0][k]):
            out.extend([pltpu.VMEM(dims + shape, BF)] * copies)
        out.extend([pltpu.VMEM(shape, BF)] * 3)
    return out


class Reduce:
    def __init__(self, place, scratch, outs, send, recv, ssend, srecv):
        self.place = place
        self.wires = [Wire(send, recv) for _ in range(2)]
        self.sides = [Wire(ssend, srecv) for _ in range(2)]
        self.held, self.units, self.live, self.done = {}, [{}, {}], [], {}
        for n, (i, k) in enumerate(PIECES):
            held = scratch.pop(0)
            lands = [[scratch.pop(0) for _ in range(copies)] for copies, _ in landing(ORDERS[0][k])]
            last, result, twin = (scratch.pop(0) for _ in range(3))
            self.held[i, k] = held
            for core in range(2):
                kind = "small" if i == SMALL else "cols"
                width = outs[i].shape[-1]
                put = (outs[i].at[piece(kind, core, k, width)], outs[i].at[piece(kind, 1 - core, k, width)])
                self.units[core][i, k] = reduce_unit(
                    place, self.wires[core], self.sides[core], n * SUMS, n, core, ORDERS[core][k],
                    held, lands, last, result, twin, put)

    def advance(self, pieces):
        def one(core):
            for p in pieces:
                next(self.units[core][p], None)

        self.place.on_core(one)

    def start(self, *pieces):
        self.advance(pieces)
        for p in pieces:
            self.live.append(p)
            self.done[p] = 1

    def pump(self, *arrays):
        todo = [p for p in self.live if not arrays or p[0] in arrays]
        self.advance(todo)
        for p in todo:
            self.done[p] += 1
            if self.done[p] == STEPS:
                self.live.remove(p)

    def end(self):
        while self.live:
            self.pump()

        def one(core):
            self.wires[core].sent()
            self.sides[core].sent()

        self.place.on_core(one)


def lay(held, value):
    for i in range(16):
        x, z, y = at_block(i)
        for j in range(2):
            held[x, z, 2 * y + j] = value[48 * i + 24 * j:48 * i + 24 * j + 24].astype(BF)


def backward_kernel(tokens2, merged_h, probs_h, ctx2_h, normed2_h, n1_h, r1_h, active2_h, dact_h, gsec_h, dlow2_h,
                    wqkv_h, wout_h, wup_h, wdown_h, small, rows,
                    o_gtok, o_qkv, o_out, o_up, o_down, o_small,
                    tok2, act2, dact, normed2, ctx2, dlow2, n1, r1, gsec, attn, attn_s, gctx, gup_s, gm_s, probs,
                    w_big, w_small, w_out, packed, packed_s, *rest):
    scratch = list(rest[:-8])
    send, recv, ssend, srecv, insem, wsem, xsend, xrecv = rest[-8:]
    place = Place()
    core = place.core
    loads = {}

    def load(name, src, dst):
        c = pltpu.make_async_copy(src, dst, insem.at[len(loads)])
        c.start()
        loads[name] = c

    def ready(*names):
        for name in names:
            loads[name].wait()

    def w_load(i, src, dst):
        c = pltpu.make_async_copy(src, dst, wsem.at[i])
        return c

    load("dlow", dlow2_h, dlow2)
    for j in range(2):
        w_load(j, wdown_h.at[0, j], w_small.at[j]).start()
    load("dact", dact_h, dact)
    load("active", active2_h, act2)
    load("normed", normed2_h, normed2)
    load("gsec", gsec_h, gsec)
    load("n1", n1_h, n1)
    load("r1", r1_h, r1)
    load("wout", wout_h, w_out)
    load("ctx", ctx2_h, ctx2)
    load("probs", probs_h, probs)
    load("tokens", tokens2, tok2)
    greet(place)
    red = Reduce(place, scratch, {QKV: o_qkv, OUT: o_out, UP: o_up, DOWN: o_down, SMALL: o_small},
                 send, recv, ssend, srecv)
    cross = Wire(xsend, xrecv)

    def mine(size):
        return pl.ds(pl.multiple_of(core * size, 128), size)

    def other(size):
        return pl.ds(pl.multiple_of((1 - core) * size, 128), size)

    ready("dlow", "dact")
    for j in range(8):
        slot = j % 2
        w_load(slot, wdown_h.at[j // 4, j % 4], w_small.at[slot]).wait()
        c = pl.ds(384 * j, 384)
        g = dot(dlow2[0], w_small[slot].reshape(384, D), ((1,), (1,)))
        dact[:, c] = (g * dact[:, c].astype(F32)).astype(BF)
        if j + 2 < 8:
            w_load(slot, wdown_h.at[(j + 2) // 4, (j + 2) % 4], w_small.at[slot]).start()
    gup = dact
    cross.go(0, gup.at[:, other(FF // 2)], gup_s, place.sibling)
    for j in range(2):
        w_load(2 + j, wup_h.at[pl.ds(256 * j, 256)], w_big.at[j]).start()
    ready("active")

    def down(j):
        r = span(j, 384)
        right = dlow2[:, :, mine(384)].reshape(2 * TOK, 384)
        g = dot(act2[:, :, r].reshape(2 * TOK, 384), right, ((0,), (0,))).astype(BF)
        for k in range(3):
            red.held[DOWN, k][j // 4, j % 4] = g[:, 128 * k:128 * k + 128].reshape(4, 96, 128)

    loop(8, down)
    red.start((DOWN, 0), (DOWN, 1), (DOWN, 2))
    ready("normed")
    load("merged", merged_h, act2.at[0, :, pl.ds(0, 3 * D)])
    merged = act2.at[0, :, pl.ds(0, 3 * D)]
    cross.landed(0, gup_s, place.sibling)
    for k in range(3):
        own = gup[:, pl.ds(pl.multiple_of(core * (FF // 2) + 512 * k, 128), 512)]
        lay(red.held[UP, k], dot(normed2[0], own, ((0,), (0,))) + dot(normed2[1], gup_s[:, 512 * k:512 * k + 512], ((0,), (0,))))
        red.start((UP, k))
        if k == 1:
            red.pump(DOWN)
    ready("gsec", "n1", "r1")
    for j in range(3):
        slot = j % 2
        w_load(2 + slot, wup_h.at[pl.ds(256 * j, 256)], w_big.at[slot]).wait()
        c = pl.ds(256 * j, 256)
        gsec[:, c] = gsec[:, c] + dot(gup[...], w_big[slot], ((1,), (1,)))
        if j == 0:
            w_load(2, wup_h.at[pl.ds(512, 256)], w_big.at[0]).start()
        red.pump(*((DOWN,) if j == 0 else ()))
    for j in range(2):
        w_load(2 + (j + 1) % 2, wqkv_h.at[pl.ds(256 * j, 256)], w_big.at[(j + 1) % 2, :, pl.ds(0, 3 * D)]).start()
    gain1 = rows[0, pl.ds(0, 1), :]

    def norm1(j, total):
        r = span(j, 384)
        g, n = gsec[r, :], n1[r, :].astype(F32)
        total = total + jnp.sum(g * n, axis=0, keepdims=True)
        g = norm_back(g, gain1, n, r1[r, pl.ds(0, 1)])
        gsec[r, :] = g
        attn[r, :] = g.astype(BF)
        return total

    g_gain1 = lax.fori_loop(0, 2, norm1, jnp.zeros((1, D), F32))
    cross.go(1, attn.at[:, other(384)], attn_s, place.sibling)
    ready("wout", "ctx")

    def context(j):
        r = span(j, 384)
        gctx[r, :] = dot(attn[r, :], w_out[...], ((1,), (1,))).astype(BF)

    loop(2, context)
    red.pump()

    p_proj, p_hid, p_cls, p_misc = picks()
    pack = dot(p_proj, small[3:9].reshape(D, 128), ((0,), (0,)))
    pack = pack + dot(p_hid, small[0], ((0,), (0,)))
    lane = iota((128, 128), 1)
    pack = pack + dot(p_cls, jnp.where(lane < 14, small[1].astype(F32), 0.0).astype(BF), ((0,), (0,)))
    values = (g_gain1, rows[3, pl.ds(0, 1), :], small[2, pl.ds(0, 1), :].astype(F32))
    misc = jnp.zeros((32, 128), F32)
    for (name, first, size, per), value in zip(ROWS, values):
        tile, held = spread(first, size, per)
        misc = misc + dot(jnp.where(held, value, 0.0).astype(BF), tile, ((1,), (1,)))
    packed[...] = (pack + dot(p_misc, misc.astype(BF), ((0,), (0,)))).astype(BF).reshape(2, 4, 4, 32, 128)
    place.on_core(lambda c: cross.copy(3, packed.at[:, :, :, pl.ds(16 - 16 * c, 16)], packed_s, place.sibling).start())

    cross.landed(1, attn_s, place.sibling)
    g = dot(ctx2[0], attn[:, mine(384)], ((0,), (0,))) + dot(ctx2[1], attn_s[...], ((0,), (0,)))
    for k in range(3):
        lay(red.held[OUT, k], g[:, 128 * k:128 * k + 128])
    cross.landed(3, packed_s, place.sibling)

    def small_half(c):
        red.held[SMALL, 1][...] = packed[:, :, :, 16 * c:16 * c + 16, :] + packed_s[...]

    place.on_core(small_half)
    red.start((OUT, 0), (OUT, 1), (OUT, 2), (SMALL, 1))
    ready("merged", "probs")

    low_half, high_half = halves()
    la, lb = low_half.astype(BF), high_half.astype(BF)
    qa, qb = (low_half * 0.125).astype(BF), (high_half * 0.125).astype(BF)

    def attend_back(s):
        r = span(s, SEQ)
        for p in range(PAIRS):
            at = [pl.ds(768 * a + 128 * p, 128) for a in range(3)]
            q, k, v = (merged[r, c] for c in at)
            d = gctx[r, pl.ds(128 * p, 128)]
            d2 = jnp.concatenate([d * la, d * lb], axis=0)
            q2 = jnp.concatenate([q * qa, q * qb], axis=0)
            pr = probs[s * PAIRS + p]
            gp = dot(d2, v, ((1,), (1,)))
            merged[r, at[2]] = dot(pr, d2, ((0,), (0,))).astype(BF)
            pf = pr.astype(F32)
            t = pf * gp
            gs = (t - pf * jnp.sum(t, axis=-1, keepdims=True)).astype(BF)
            both = dot(gs, k)
            merged[r, at[0]] = ((both[:SEQ] * low_half + both[SEQ:] * high_half) * 0.125).astype(BF)
            merged[r, at[1]] = dot(gs, q2, ((0,), (0,))).astype(BF)

    for part in range(3):
        lax.fori_loop(2 * part, 2 * part + 2, lambda s, c: (attend_back(s), c)[1], 0)
        red.pump()
    cross.go(2, act2.at[0, :, other(3 * D // 2)], gm_s, place.sibling)
    ready("tokens")

    def tokens_part(j):
        slot = (j + 1) % 2
        w_load(2 + slot, wqkv_h.at[pl.ds(256 * j, 256)], w_big.at[slot, :, pl.ds(0, 3 * D)]).wait()
        c = pl.ds(256 * j, 256)
        gsec[:, c] = gsec[:, c] + dot(merged[...], w_big[slot, :, :3 * D], ((1,), (1,)))

    tokens_part(0)
    w_load(3, wqkv_h.at[pl.ds(512, 256)], w_big.at[1, :, pl.ds(0, 3 * D)]).start()
    red.pump()
    cross.landed(2, gm_s, place.sibling)
    for k in range(3):
        own = merged[:, pl.ds(pl.multiple_of(core * (3 * D // 2) + 384 * k, 128), 384)]
        lay(red.held[QKV, k], dot(tok2[0], own, ((0,), (0,))) + dot(tok2[1], gm_s[:, 384 * k:384 * k + 384], ((0,), (0,))))
        red.start((QKV, k))
    red.pump()
    tokens_part(1)
    red.pump()
    tokens_part(2)
    store = pltpu.make_async_copy(gsec, o_gtok, insem.at[len(loads)])
    store.start()
    red.end()
    cross.sent()
    place.on_core(lambda c: cross.copy(3, packed.at[:, :, :, pl.ds(16 - 16 * c, 16)], packed_s, place.sibling).wait_send())
    store.wait()


def backward(*args):
    hbm, vmem = pl.BlockSpec(memory_space=pl.ANY), pl.BlockSpec(memory_space=pltpu.VMEM)

    def arr(*shape, dtype=F32):
        return jax.ShapeDtypeStruct(shape, dtype)

    dma = pltpu.SemaphoreType.DMA
    count = len(PIECES)
    scratch = [
        pltpu.VMEM((2, TOK, D), BF), pltpu.VMEM((2, TOK, FF), BF), pltpu.VMEM((TOK, FF), BF),
        pltpu.VMEM((2, TOK, D), BF), pltpu.VMEM((2, TOK, D), BF), pltpu.VMEM((2, TOK, D), BF),
        pltpu.VMEM((TOK, D), BF), pltpu.VMEM((TOK, 128), F32), pltpu.VMEM((TOK, D), F32),
        pltpu.VMEM((TOK, D), BF), pltpu.VMEM((TOK, D // 2), BF), pltpu.VMEM((TOK, D), BF),
        pltpu.VMEM((TOK, FF // 2), BF), pltpu.VMEM((TOK, 3 * D // 2), BF),
        pltpu.VMEM((SEQ_DEV * PAIRS, 256, 128), BF),
        pltpu.VMEM((2, 256, FF), BF), pltpu.VMEM((2, 4, 96, D), BF), pltpu.VMEM((D, D), BF),
        pltpu.VMEM((2, 4, 4, 32, 128), BF), pltpu.VMEM((2, 4, 4, 16, 128), BF),
    ] + reduce_scratch() + [
        dma((count * SUMS,)), dma((count * SUMS,)), dma((count,)), dma((count,)), dma((16,)), dma((4,)), dma((4,)), dma((4,)),
    ]
    return pl.pallas_call(
        backward_kernel,
        out_shape=[arr(TOK, D), arr(24, 3 * D), arr(24, D), arr(24, FF), arr(96, D), arr(32, 128)],
        in_specs=[hbm] * 15 + [vmem] * 2,
        out_specs=[hbm] + [vmem] * 5,
        scratch_shapes=scratch,
        compiler_params=pltpu.CompilerParams(collective_id=1, has_side_effects=True, vmem_limit_bytes=VMEM),
        cost_estimate=pl.CostEstimate(flops=24 * 10**9, bytes_accessed=60 * 10**6, transcendentals=0),
        name="backward",
    )(*args)


def local(tokens, exit_layer, w_qkv, w_out, gain_attn, w_up, w_down, gain_ffn, w_proj, pool_query, w_hid, w_cls,
          cot_out, cot_logits):
    line = jnp.concatenate([gain_attn, gain_ffn, pool_query])
    last = jnp.pad(w_cls, ((0, 0), (0, 128 - 14)))
    last = last + jnp.pad(line[None], ((0, 3), (16, 128 - 16 - line.shape[0])))
    small = jnp.concatenate([w_proj, w_hid, last], axis=0)
    alive = (exit_layer >= LAYER).astype(F32)
    alive_tok = jnp.broadcast_to(jnp.repeat(alive, SEQ)[:, None], (TOK, 128))
    alive_seq = jnp.broadcast_to(jnp.pad(alive, (0, 2))[:, None], (8, 128))
    cotl = jnp.pad(cot_logits, ((0, 2), (0, 128 - 14)))
    (act, logits, f_qkv, f_out, f_up, f_down, merged, probs, ctx, normed, n1, r1, active, dact, gsec, dlow, tokens2,
     small_g, rows) = forward(tokens, cot_out, alive_tok, alive_seq, cotl, (small, w_qkv, w_out, w_up, w_down))
    g_tok, g_qkv, g_out, g_up, g_down, g_small = backward(
        tokens2, merged, probs, ctx, normed, n1, r1, active, dact, gsec, dlow, f_qkv, f_out, f_up, f_down, small_g, rows)
    line = g_small[28]
    return (act, logits[:SEQ_DEV, :14], g_tok, g_qkv, g_out, line[16:40], g_up, g_down, line[40:64],
            g_small[:24], line[64:68], g_small[24:28], g_small[28:32, :14])


def solution(mesh):
    both, wide = P(("wide", "grp"), None), P("wide", None)
    in_specs = (both, P(("wide", "grp")), wide, wide, P("wide"), wide, wide, P("wide"), wide, P("wide"), wide, wide,
                both, both)
    out_specs = (both, both, both, wide, wide, P("wide"), wide, wide, P("wide"), wide, P("wide"), wide, wide)
    return jax.shard_map(local, mesh=mesh, in_specs=in_specs, out_specs=out_specs, check_vma=False)
```

```python
import functools
import jax
import jax.numpy as jnp
from jax import lax
from jax.sharding import PartitionSpec as P
from jax.experimental import pallas as pl
from jax.experimental.pallas import tpu as pltpu

D = 768
FF = 3072
TOK = 768
SEQ_DEV = 6
PAIRS = 6
SEQ = 128
LAYER = 3
MESH = pl.DeviceIdType.MESH
BF = jnp.bfloat16
F32 = jnp.float32
SIZE = {"x": 2, "z": 4, "y": 4}
ORDERS = (
    (("y", "z", "x"), ("z", "x", "y"), ("y", "x", "z")),
    (("z", "y", "x"), ("z", "x", "y"), ("y", "x", "z")),
)
EVENTS = 7
SUMS = 8
VMEM = 62 * 2**20


class Place:
    def __init__(self):
        wide, grp = lax.axis_index("wide"), lax.axis_index("grp")
        xl, z, y = wide // 16, (wide // 4) % 4, wide % 4
        x = (grp // 2) * 2 + xl
        self.core = grp % 2
        self.places = {("x", 0): xl, ("x", 1): 1 - xl}
        for axis, here in (("z", z), ("y", y)):
            for step in range(4):
                self.places[axis, step] = (here + step) % 4
        self.ids = {}
        for step in (1, 2, 3):
            far = (x + step) % 4
            self.ids["x", step] = ((far % 2) * 16 + z * 4 + y, (far // 2) * 2 + self.core)
            self.ids["y", step] = (xl * 16 + z * 4 + self.places["y", step], grp)
            self.ids["z", step] = (xl * 16 + self.places["z", step] * 4 + y, grp)
        self.sibling = (wide, grp + 1 - 2 * self.core)

    def near(self, axis, step):
        return self.ids[axis, step % 4]

    def at(self, axis, step=0):
        return self.places[axis, step % SIZE[axis]]

    def box(self, have, **fixed):
        out = []
        for axis in ("x", "z", "y"):
            if axis in fixed:
                out.append(fixed[axis])
            elif axis in have:
                out.append(slice(None))
            else:
                out.append(self.at(axis))
        return tuple(out)

    def on_core(self, step):
        for core in (0, 1):
            pl.when(self.core == core)(functools.partial(step, core))


def greet(place):
    barrier = pltpu.get_barrier_semaphore()
    ids = [place.near(a, s) for a in ("x", "y", "z") for s in (1, -1, 2)] + [place.sibling]
    for i in ids:
        pl.semaphore_signal(barrier, inc=1, device_id=i, device_id_type=MESH)
    pl.semaphore_wait(barrier, len(ids))


class Wire:
    def __init__(self, send, recv):
        self.send, self.recv = send, recv
        self.started = []

    def copy(self, n, src, dst, to):
        return pltpu.make_async_remote_copy(
            src_ref=src, dst_ref=dst, send_sem=self.send.at[n], recv_sem=self.recv.at[n],
            device_id=to, device_id_type=MESH,
        )

    def go(self, n, src, dst, to):
        self.copy(n, src, dst, to).start()
        self.started.append((n, src, dst, to))

    def landed(self, n, dst, to):
        self.copy(n, dst, dst, to).wait_recv()

    def sent(self):
        for c in self.started:
            self.copy(*c).wait_send()


def piece(kind, core, k, width):
    if kind == "cols":
        return (slice(None), pl.ds((core * 3 + k) * (width // 6), width // 6))
    return (pl.ds(core * 16, 16), slice(None)) if k == 1 else None


class Lane:
    def __init__(self, send, recv, first_send, first_recv):
        self.send, self.recv, self.first_send, self.first_recv = send, recv, first_send, first_recv
        self.out, self.count = {}, 0

    def copy(self, slot, e, src, dst, to):
        return pltpu.make_async_remote_copy(
            src_ref=src, dst_ref=dst, send_sem=self.send.at[self.first_send + slot],
            recv_sem=self.recv.at[self.first_recv + e], device_id=to, device_id_type=MESH,
        )

    def go(self, e, src, dst, to):
        slot = self.count % 3
        self.count += 1
        if slot in self.out:
            self.copy(slot, *self.out[slot]).wait_send()
        self.copy(slot, e, src, dst, to).start()
        self.out[slot] = (e, src, dst, to)

    def landed(self, e, dst, to):
        self.copy(0, e, dst, dst, to).wait_recv()

    def sent(self):
        for slot, c in self.out.items():
            self.copy(slot, *c).wait_send()


def gather_unit(place, lane, sib, core, order, own, full):
    way = 1 if core == 0 else -1
    have, e = [], 0
    for axis in order:
        mine = place.box(have)
        src = full(mine) if have else own
        ahead, back, far = place.near(axis, way), place.near(axis, -way), place.near(axis, 2)
        last = axis == order[2]
        if axis == "x":
            lane.go(e, src, full(mine), ahead)
            yield
            got = place.box(have, x=place.at("x", 1))
            lane.landed(e, full(got), ahead)
            if last:
                sib(got)
            e += 1
        elif not have:
            for n, to in enumerate((ahead, back, far)):
                lane.go(e + n, src, full(mine), to)
            yield
            for n, step in enumerate((-way, way, 2)):
                lane.landed(e + n, full(place.box(have, **{axis: place.at(axis, step)})), ahead)
            e += 3
        else:
            lane.go(e, src, full(mine), ahead)
            lane.go(e + 1, src, full(mine), back)
            yield
            got = place.box(have, **{axis: place.at(axis, -way)})
            lane.landed(e, full(got), ahead)
            lane.go(e + 2, full(got), full(got), ahead)
            if last:
                sib(got)
            yield
            for late, step in ((1, way), (2, 2)):
                got = place.box(have, **{axis: place.at(axis, step)})
                lane.landed(e + late, full(got), ahead)
                if last:
                    sib(got)
            e += 3
        have.append(axis)
        if axis == order[1]:
            sib(place.box(have))


class Gather:
    def __init__(self, place, kinds, shards, fulls, send, recv, side, keep):
        self.place, self.kinds, self.shards, self.fulls = place, kinds, shards, fulls
        self.side, self.keep = side, keep
        n = len(kinds)
        self.lanes = [[], []]
        self.units = [[[] for _ in range(n)] for _ in range(2)]
        for core in range(2):
            for i in range(n):
                for k in range(3):
                    tail = piece(kinds[i], core, k, shards[i].shape[-1])
                    if tail is None:
                        continue
                    at = len(self.lanes[core])
                    lane = Lane(send, recv, at * 3, at * EVENTS)
                    self.lanes[core].append(lane)
                    full = functools.partial(self.part, i, tail)
                    sib = functools.partial(self.pass_on, i, full)
                    self.units[core][i].append(gather_unit(
                        place, lane, sib, core, ORDERS[core][k], shards[i].at[tail], full))

    def part(self, i, tail, box):
        return self.fulls[i].at[box + tail]

    def half(self, i, core):
        size = self.shards[i].shape[-1] // 2
        if self.kinds[i] == "cols":
            return (slice(None), pl.ds(core * size, size))
        return (pl.ds(core * 16, 16), slice(None))

    def to_side(self, sems, n, src, dst):
        return pltpu.make_async_remote_copy(
            src_ref=src, dst_ref=dst, send_sem=sems.at[n], recv_sem=sems.at[len(self.kinds) + n],
            device_id=self.place.sibling, device_id_type=MESH)

    def pass_on(self, i, full, box):
        self.to_side(self.side, i, full(box), full(box)).start()

    def own(self, i, core):
        half = self.half(i, 1 - core)
        return self.to_side(self.keep, i, self.shards[i].at[half], self.fulls[i].at[self.place.box(()) + half])

    def own_start(self):
        self.place.on_core(lambda core: [self.own(i, core).start() for i in range(len(self.kinds))] and None)

    def own_landed(self):
        def one(core):
            for i in range(len(self.kinds)):
                self.own(i, core).wait_send()
                self.own(i, 1 - core).wait_recv()

        self.place.on_core(one)

    def step(self, *arrays):
        def one(core):
            for i in arrays:
                for u in self.units[core][i]:
                    next(u, None)

        self.place.on_core(one)

    def everything(self, i, core):
        part = self.fulls[i].at[(slice(None),) * 3 + self.half(i, core)]
        return self.to_side(self.side, i, part, part)

    def whole(self, *arrays):
        def one(core):
            for i in arrays:
                self.everything(i, 1 - core).wait_recv()

        self.place.on_core(one)

    def end(self):
        def one(core):
            for lane in self.lanes[core]:
                lane.sent()
            for i in range(len(self.kinds)):
                self.everything(i, core).wait_send()

        self.place.on_core(one)


def dot(a, b, dims=((1,), (0,))):
    return lax.dot_general(a, b, (dims, ((), ())), preferred_element_type=F32)


def exact(a, b, dims=((1,), (0,))):
    return lax.dot_general(a, b, (dims, ((), ())), precision=lax.Precision.HIGHEST, preferred_element_type=F32)


def iota(shape, dim):
    return lax.broadcasted_iota(jnp.int32, shape, dim)


def over24(i):
    return (i * 2731) >> 16


def ones_where(hit):
    return jnp.where(hit, 1.0, 0.0).astype(BF)


def picks():
    i, j = iota((768, 1024), 0), iota((768, 1024), 1)
    proj = ones_where(j == i + 8 * over24(i))
    i, j = iota((128, 1024), 0), iota((128, 1024), 1)
    at = 32 * (i >> 2) + (i & 3)
    hid, cls = ones_where(j == at + 24), ones_where(j == at + 28)
    i, j = iota((32, 1024), 0), iota((32, 1024), 1)
    misc = ones_where(j == 32 * i + 28)
    return proj, hid, cls, misc


def spread(first, size, per):
    i, l = iota((128, size), 0), iota((128, size), 1)
    block = over24(l) if per == 24 else l >> 2
    w, m = iota((32, size), 0), iota((32, size), 1)
    held = over24(m) if per == 24 else m >> 2
    return ones_where(i - first == l - per * block), held == w


ROWS = (("gain_attn", 16, 768, 24), ("gain_ffn", 40, 768, 24), ("pool", 64, 128, 4))


def normalise(h):
    centre = h - jnp.mean(h, axis=-1, keepdims=True)
    r = lax.rsqrt(jnp.mean(centre * centre, axis=-1, keepdims=True) + 1e-06)
    return centre * r, r


def norm_back(g, gain, n, r):
    gn = g * gain
    return r * (gn - jnp.mean(gn, axis=-1, keepdims=True) - n * jnp.mean(gn * n, axis=-1, keepdims=True))


TANH_A = 0.7978845608028654
TANH_B = 0.7978845608028654 * 0.044715


def gelu(u):
    u2 = u * u
    h = 0.5 + 0.5 * jnp.tanh(u * (TANH_A + TANH_B * u2))
    y = u * h
    return y, h + y * (1.0 - h) * (2.0 * TANH_A + 6.0 * TANH_B * u2)


def at_block(i):
    return i // 8, (i // 2) % 4, i % 2


def join(blocks, whole):
    def one(i, carry):
        x, z, y = at_block(i)
        pair = jnp.concatenate([blocks[x, z, 2 * y], blocks[x, z, 2 * y + 1]], axis=0)
        whole[pl.ds(pl.multiple_of(i * 48, 48), 48), :] = pair
        return carry

    lax.fori_loop(0, 16, one, 0)


def loop(n, step):
    def one(i, carry):
        step(i)
        return carry

    lax.fori_loop(0, n, one, 0)


def once(step):
    step()


def span(i, size):
    return pl.ds(pl.multiple_of(i * size, size), size)


def halves():
    lane = iota((1, 128), 1)
    return jnp.where(lane < 64, 1.0, 0.0), jnp.where(lane < 64, 0.0, 1.0)


KINDS = ("small", "cols", "cols", "cols", "cols")
SMALL, QKV, OUT, UP, DOWN = range(5)


def forward_kernel(tokens, cot, exit_layer, cot_logits, s_small, s_qkv, s_out, s_up, s_down,
                   o_act, o_logits, o_wqkv, o_wout, o_wup, o_wdown, o_merged, o_probs, o_ctx, o_normed, o_n1, o_r1,
                   o_active, o_dact, o_gsec, o_dlow, o_tokens2, o_small, rows,
                   b_small, b_qkv, b_out, b_up, b_down, w_qkv, w_out, w_up, tok, cotv, merged, probs, ctx, normed, n1, r1,
                   active, dact, gsec, r2, dlow, out, projected, gproj, wproj, hid, cls,
                   alive, alive_seq, cotl, send, recv, ssem, lsem, insem, outsem, xsend, xrecv):
    place = Place()
    loads = [pltpu.make_async_copy(tokens, tok, insem.at[0]), pltpu.make_async_copy(cot, cotv, insem.at[1])]
    for c in loads:
        c.start()
    greet(place)
    g = Gather(place, KINDS, (s_small, s_qkv, s_out, s_up, s_down), (b_small, b_qkv, b_out, b_up, b_down),
               send, recv, ssem, lsem)
    stores = []
    cross = Wire(xsend, xrecv)

    def keep(src, dst):
        c = pltpu.make_async_copy(src, dst, outsem.at[len(stores)])
        c.start()
        stores.append(c)

    def share(n, src, dst):
        keep(src, dst.at[0])
        cross.go(n, src, dst.at[1], place.sibling)

    g.step(QKV, SMALL, OUT)
    g.own_start()
    g.step(UP, DOWN)
    loads[0].wait()
    share(0, tok, o_tokens2)
    cotl[...] = jnp.zeros((8, 128), F32)
    cotl[0:SEQ_DEV, 0:14] = cot_logits[...]
    alive_seq[...] = jnp.zeros((8, 128), F32)
    for s in range(SEQ_DEV):
        stays = jnp.clip(exit_layer[s] - (LAYER - 1), 0, 1).astype(F32)
        alive[pl.ds(s * SEQ, SEQ), :] = jnp.full((SEQ, 128), stays)
        alive_seq[pl.ds(s, 1), :] = jnp.full((1, 128), stays)
    g.own_landed()
    g.step(QKV, SMALL, OUT)
    g.step(UP, DOWN)
    g.step(QKV, SMALL, OUT)
    g.step(QKV, SMALL, OUT)
    g.step(UP, DOWN)
    g.step(QKV, SMALL)
    g.whole(QKV, SMALL)
    join(b_qkv, w_qkv)

    def qkv(j):
        c = span(j, D)
        merged[:, c] = dot(tok[...], w_qkv[:, c]).astype(BF)

    loop(3, qkv)
    keep(w_qkv, o_wqkv)
    keep(merged, o_merged)

    def small_weights():
        p_proj, p_hid, p_cls, p_misc = picks()
        pack = b_small[...].reshape(1024, 128)
        wproj[...] = dot(p_proj, pack).astype(BF)
        hid[...] = dot(p_hid, pack)
        cls[...] = jnp.where(iota((128, 128), 1) < 14, dot(p_cls, pack), 0.0)
        misc = dot(p_misc, pack).astype(BF)
        for n, (name, first, size, per) in enumerate(ROWS):
            tile, held = spread(first, size, per)
            row = jnp.sum(jnp.where(held, dot(misc, tile), 0.0), axis=0, keepdims=True)
            rows[n, :, pl.ds(0, size)] = jnp.broadcast_to(row, (8, size))

    once(small_weights)
    low_half, high_half = halves()
    g.step(OUT)

    qa, qb = (low_half * 0.125).astype(BF), (high_half * 0.125).astype(BF)

    def attend(s):
        r = span(s, SEQ)
        scores, prs = [], []
        for p in range(PAIRS):
            q, k = (merged[r, pl.ds(768 * a + 128 * p, 128)] for a in range(2))
            scores.append(dot(jnp.concatenate([q * qa, q * qb], axis=0), k, ((1,), (1,))))
        for p in range(PAIRS):
            e = jnp.exp(scores[p] - jnp.max(scores[p], axis=-1, keepdims=True))
            prs.append((e * (1.0 / jnp.sum(e, axis=-1, keepdims=True))).astype(BF))
            probs[s * PAIRS + p] = prs[p]
        for p in range(PAIRS):
            both = dot(prs[p], merged[r, pl.ds(1536 + 128 * p, 128)])
            ctx[r, pl.ds(128 * p, 128)] = (both[:SEQ] * low_half + both[SEQ:] * high_half).astype(BF)

    for part, late in enumerate((UP, DOWN, None)):

        def attend_two(s):
            attend(s + 2 * part)

        loop(2, attend_two)
        if late:
            g.step(late)
    keep(probs, o_probs)
    g.whole(OUT)
    join(b_out, w_out)
    gain1 = rows[0, pl.ds(0, 1), :]

    def mix(j):
        r = span(j, 384)
        n, inv = normalise(tok[r, :].astype(F32) + dot(ctx[r, :], w_out[...]))
        n1[r, :] = n.astype(BF)
        normed[r, :] = (n * gain1).astype(BF)
        r1[r, :] = jnp.broadcast_to(inv, (384, 128))

    loop(2, mix)
    g.step(UP)
    g.whole(UP)
    share(2, normed, o_normed)
    share(1, ctx, o_ctx)
    keep(w_out, o_wout)
    keep(n1, o_n1)
    keep(r1, o_r1)
    join(b_up, w_up)

    def active_part(j):
        c = span(j, D)
        return pltpu.make_async_remote_copy(
            src_ref=active.at[:, c], dst_ref=o_active.at[1, :, c], send_sem=xsend.at[5 + j], recv_sem=xrecv.at[5 + j],
            device_id=place.sibling, device_id_type=MESH)

    def upward(j):
        c = span(j, D)
        y, dy = gelu(dot(normed[...], w_up[:, c]))
        active[:, c] = y.astype(BF)
        dact[:, c] = dy.astype(BF)
        active_part(j).start()

    def upward_late(j):
        upward(j + 2)

    loop(2, upward)
    g.step(DOWN)
    loop(2, upward_late)
    g.whole(DOWN)
    keep(active, o_active.at[0])
    keep(dact, o_dact)
    keep(w_up, o_wup)
    keep(b_down, o_wdown)
    loads[1].wait()
    gain2 = rows[1, pl.ds(0, 1), :]

    def downward(j):
        r = span(j, 384)
        second = normed[r, :].astype(F32) + dot(active[r, :], b_down[...].reshape(FF, D))
        n, inv = normalise(second)
        gsec[r, :] = n
        r2[r, :] = jnp.broadcast_to(inv, (384, 128))
        low = (n * gain2).astype(BF)
        out[r, :] = low
        projected[r, :] = dot(low, wproj[...])

    loop(2, downward)

    query = rows[2, pl.ds(0, 1), pl.ds(0, 128)]

    def student():
        weights, pooled = [], []
        for s in range(SEQ_DEV):
            pr = projected[pl.ds(s * SEQ, SEQ), :]
            t = pr * query
            per_head = []
            for half in (low_half, high_half):
                score = jnp.sum(t * half, axis=-1, keepdims=True) * 0.125
                e = jnp.exp(score - jnp.max(score, axis=0, keepdims=True))
                per_head.append(e / jnp.sum(e, axis=0, keepdims=True))
            weights.append(per_head)
            pooled.append(jnp.sum(pr * (per_head[0] * low_half + per_head[1] * high_half), axis=0, keepdims=True))
        none = jnp.zeros((1, 128), F32)
        pooled = jnp.concatenate(pooled + [none, none], axis=0)
        hidden = jnp.tanh(exact(pooled, hid[...]))
        o_logits[...] = exact(hidden, cls[...]) * alive_seq[...]
        g_log = cotl[...] * alive_seq[...]
        o_small[1] = exact(hidden, g_log, ((0,), (0,))).astype(BF)
        g_pre = exact(g_log, cls[...], ((1,), (1,))) * (1.0 - hidden * hidden)
        o_small[0] = exact(pooled, g_pre, ((0,), (0,))).astype(BF)
        g_pooled = exact(g_pre, hid[...], ((1,), (1,)))
        g_query = none
        for s in range(SEQ_DEV):
            r = pl.ds(s * SEQ, SEQ)
            pr = projected[r, :]
            gp = g_pooled[s:s + 1]
            t = pr * gp
            total = (weights[s][0] * low_half + weights[s][1] * high_half) * gp
            for half, w in zip((low_half, high_half), weights[s]):
                dw = jnp.sum(t * half, axis=-1, keepdims=True)
                ds = w * (dw - jnp.sum(w * dw, axis=0, keepdims=True)) * 0.125
                total = total + ds * (query * half)
                g_query = g_query + jnp.sum(ds * pr, axis=0, keepdims=True) * half
            gproj[r, :] = total.astype(BF)
        o_small[2] = jnp.broadcast_to(g_query, (128, 128)).astype(BF)

    once(student)

    def back(j):
        r = span(j, 384)
        keep_tok = alive[r, pl.ds(0, 1)]
        low = out[r, :]
        g_out = keep_tok * cotv[r, :].astype(F32) + dot(gproj[r, :], wproj[...], ((1,), (1,)))
        n = gsec[r, :]
        part = jnp.sum(g_out * n, axis=0, keepdims=True)
        rows[3, pl.ds(0, 1), :] = jnp.where(j == 0, part, part + rows[3, pl.ds(0, 1), :])
        g2 = norm_back(g_out, gain2, n, r2[r, pl.ds(0, 1)])
        gsec[r, :] = g2
        dlow[r, :] = g2.astype(BF)
        cotv[r, :] = (keep_tok * low.astype(F32)).astype(BF)
        low_part(j).start()
        for c in late(j):
            c.start()

    def low_part(j):
        r = span(j, 384)
        return pltpu.make_async_remote_copy(
            src_ref=dlow.at[r], dst_ref=o_dlow.at[1, r], send_sem=xsend.at[9 + j], recv_sem=xrecv.at[9 + j],
            device_id=place.sibling, device_id_type=MESH)

    def late(j):
        r = span(j, 384)
        return [pltpu.make_async_copy(src.at[r], dst.at[r], outsem.at[16 + 3 * j + n])
                for n, (src, dst) in enumerate(((dlow, o_dlow.at[0]), (gsec, o_gsec), (cotv, o_act)))]

    loop(2, back)

    def proj_grad():
        o_small[3:9] = dot(out[...], gproj[...], ((0,), (0,))).astype(BF).reshape(6, 128, 128)

    once(proj_grad)
    g.end()
    for c in stores + late(0) + late(1):
        c.wait()
    for n, dst in ((0, o_tokens2), (1, o_ctx), (2, o_normed)):
        cross.landed(n, dst.at[1], place.sibling)
    cross.sent()
    for c in [active_part(j) for j in range(4)] + [low_part(j) for j in range(2)]:
        c.wait()


def forward(tokens, cot, exit_layer, cot_logits, shards):
    hbm, vmem = pl.BlockSpec(memory_space=pl.ANY), pl.BlockSpec(memory_space=pltpu.VMEM)
    n = len(KINDS)
    count = n * 3 - 2

    def arr(*shape, dtype=BF):
        return jax.ShapeDtypeStruct(shape, dtype)

    outs = [
        (arr(TOK, D), hbm), (arr(8, 128, dtype=F32), vmem),
        (arr(D, 3 * D), hbm), (arr(D, D), hbm), (arr(D, FF), hbm), (arr(2, 4, 4, 96, D), hbm),
        (arr(TOK, 3 * D), hbm), (arr(SEQ_DEV * PAIRS, 256, 128), hbm), (arr(2, TOK, D), hbm), (arr(2, TOK, D), hbm),
        (arr(TOK, D), hbm), (arr(TOK, 128, dtype=F32), hbm), (arr(2, TOK, FF), hbm), (arr(TOK, FF), hbm),
        (arr(TOK, D, dtype=F32), hbm), (arr(2, TOK, D), hbm), (arr(2, TOK, D), hbm),
        (arr(9, 128, 128), vmem), (arr(4, 8, D, dtype=F32), vmem),
    ]
    dma = pltpu.SemaphoreType.DMA
    scratch = [
        pltpu.VMEM((2, 4, 4, 32, 128), BF), pltpu.VMEM((2, 4, 4, 24, 3 * D), BF), pltpu.VMEM((2, 4, 4, 24, D), BF),
        pltpu.VMEM((2, 4, 4, 24, FF), BF), pltpu.VMEM((2, 4, 4, 96, D), BF),
        pltpu.VMEM((D, 3 * D), BF), pltpu.VMEM((D, D), BF), pltpu.VMEM((D, FF), BF),
        pltpu.VMEM((TOK, D), BF), pltpu.VMEM((TOK, D), BF), pltpu.VMEM((TOK, 3 * D), BF),
        pltpu.VMEM((SEQ_DEV * PAIRS, 256, 128), BF), pltpu.VMEM((TOK, D), BF), pltpu.VMEM((TOK, D), BF),
        pltpu.VMEM((TOK, D), BF), pltpu.VMEM((TOK, 128), F32), pltpu.VMEM((TOK, FF), BF), pltpu.VMEM((TOK, FF), BF),
        pltpu.VMEM((TOK, D), F32), pltpu.VMEM((TOK, 128), F32), pltpu.VMEM((TOK, D), BF), pltpu.VMEM((TOK, D), BF),
        pltpu.VMEM((TOK, 128), F32), pltpu.VMEM((TOK, 128), BF), pltpu.VMEM((D, 128), BF),
        pltpu.VMEM((128, 128), F32), pltpu.VMEM((128, 128), F32),
        pltpu.VMEM((TOK, 128), F32), pltpu.VMEM((8, 128), F32), pltpu.VMEM((8, 128), F32),
        dma((count * 3,)), dma((count * EVENTS,)), dma((2 * n,)), dma((2 * n,)),
        dma((2,)), dma((22,)), dma((11,)), dma((11,)),
    ]
    return pl.pallas_call(
        forward_kernel,
        out_shape=[o for o, _ in outs],
        in_specs=[hbm, hbm, pl.BlockSpec(memory_space=pltpu.SMEM), vmem] + [hbm] * n,
        out_specs=[s for _, s in outs],
        scratch_shapes=scratch,
        compiler_params=pltpu.CompilerParams(collective_id=0, has_side_effects=True, vmem_limit_bytes=VMEM),
        cost_estimate=pl.CostEstimate(flops=12 * 10**9, bytes_accessed=60 * 10**6, transcendentals=4 * 10**6),
        name="forward",
    )(tokens, cot, exit_layer, cot_logits, *shards)


def landing(order):
    out, left = [], ["x", "z", "y"]
    for axis in reversed(order):
        left = [a for a in left if a != axis]
        out.append((1 if axis == "x" else 3, tuple(SIZE[a] for a in left)))
    return out


def add_box(place, held, left, fixed, terms):
    dims = tuple(SIZE[a] for a in left)

    def step(i):
        index = []
        for d in reversed(dims):
            index.append(i % d)
            i = i // d
        index = tuple(reversed(index))
        at = dict(zip(left, index))
        b = tuple(fixed[a] if a in fixed else at[a] if a in at else place.at(a) for a in ("x", "z", "y"))
        total = held[b]
        for t in terms:
            total = total + t[index]
        held[b] = total

    if dims:
        count = 1
        for d in dims:
            count *= d
        loop(count, step)
    else:
        step(0)


def reduce_unit(place, wire, side, base, base2, core, order, held, lands, last, result, twin, put):
    way = 1 if core == 0 else -1
    left, e = ["x", "z", "y"], base
    for axis, bufs in zip(reversed(order), lands):
        left = [a for a in left if a != axis]
        ahead, back = place.near(axis, way), place.near(axis, -way)
        mine = {axis: place.at(axis)}
        if not left:
            for n, (step, to) in enumerate(((way, ahead), (-way, back), (2, place.near(axis, 2)))):
                wire.go(e + n, held.at[place.box(left, **{axis: place.at(axis, step)})], bufs[n], to)
            yield
            for n in range(3):
                wire.landed(e + n, bufs[n], ahead)
            add_box(place, held, left, mine, bufs)
            e += 3
        elif axis == "x":
            wire.go(e, held.at[place.box(left, x=place.at("x", 1))], bufs[0], ahead)
            yield
            wire.landed(e, bufs[0], ahead)
            add_box(place, held, left, mine, [bufs[0]])
            e += 1
        else:
            wire.go(e, held.at[place.box(left, **{axis: place.at(axis, 2)})], bufs[0], ahead)
            wire.go(e + 1, held.at[place.box(left, **{axis: place.at(axis, -way)})], bufs[1], back)
            yield
            wire.landed(e, bufs[0], ahead)
            onward = {axis: place.at(axis, way)}
            add_box(place, held, left, onward, [bufs[0]])
            wire.go(e + 2, held.at[place.box(left, **onward)], bufs[2], ahead)
            yield
            wire.landed(e + 1, bufs[1], ahead)
            wire.landed(e + 2, bufs[2], ahead)
            add_box(place, held, left, mine, [bufs[1], bufs[2]])
            e += 3
    own = place.box(())
    wire.go(e, held.at[own], last, place.near("x", 2))
    yield
    wire.landed(e, last, place.near("x", 2))
    total = held[own] + last[...]
    result[...] = total
    side.go(base2, result, twin, place.sibling)
    put[0][...] = total.astype(F32)
    yield
    side.landed(base2, twin, place.sibling)
    put[1][...] = twin[...].astype(F32)


STEPS = 7
PIECES = [(i, k) for i in (DOWN, UP, OUT, QKV, SMALL) for k in range(3) if i != SMALL or k == 1]


def piece_shape(i):
    return {SMALL: (16, 128), QKV: (24, 384), OUT: (24, 128), UP: (24, 512), DOWN: (96, 128)}[i]


def reduce_scratch():
    out = []
    for i, k in PIECES:
        shape = piece_shape(i)
        out.append(pltpu.VMEM((2, 4, 4) + shape, BF))
        for copies, dims in landing(ORDERS[0][k]):
            out.extend([pltpu.VMEM(dims + shape, BF)] * copies)
        out.extend([pltpu.VMEM(shape, BF)] * 3)
    return out


class Reduce:
    def __init__(self, place, scratch, outs, send, recv, ssend, srecv):
        self.place = place
        self.wires = [Wire(send, recv) for _ in range(2)]
        self.sides = [Wire(ssend, srecv) for _ in range(2)]
        self.held, self.units, self.live, self.done = {}, [{}, {}], [], {}
        for n, (i, k) in enumerate(PIECES):
            held = scratch.pop(0)
            lands = [[scratch.pop(0) for _ in range(copies)] for copies, _ in landing(ORDERS[0][k])]
            last, result, twin = (scratch.pop(0) for _ in range(3))
            self.held[i, k] = held
            for core in range(2):
                kind = "small" if i == SMALL else "cols"
                width = outs[i].shape[-1]
                put = (outs[i].at[piece(kind, core, k, width)], outs[i].at[piece(kind, 1 - core, k, width)])
                self.units[core][i, k] = reduce_unit(
                    place, self.wires[core], self.sides[core], n * SUMS, n, core, ORDERS[core][k],
                    held, lands, last, result, twin, put)

    def advance(self, pieces):
        def one(core):
            for p in pieces:
                next(self.units[core][p], None)

        self.place.on_core(one)

    def start(self, *pieces):
        self.advance(pieces)
        for p in pieces:
            self.live.append(p)
            self.done[p] = 1

    def pump(self, *arrays):
        todo = [p for p in self.live if not arrays or p[0] in arrays]
        self.advance(todo)
        for p in todo:
            self.done[p] += 1
            if self.done[p] == STEPS:
                self.live.remove(p)

    def end(self):
        while self.live:
            self.pump()

        def one(core):
            self.wires[core].sent()
            self.sides[core].sent()

        self.place.on_core(one)


def lay(held, value):
    for i in range(16):
        x, z, y = at_block(i)
        for j in range(2):
            held[x, z, 2 * y + j] = value[48 * i + 24 * j:48 * i + 24 * j + 24].astype(BF)


def backward_kernel(tokens2, merged_h, probs_h, ctx2_h, normed2_h, n1_h, r1_h, active2_h, dact_h, gsec_h, dlow2_h,
                    wqkv_h, wout_h, wup_h, wdown_h, small, rows,
                    o_gtok, o_qkv, o_out, o_up, o_down, o_small,
                    tok2, act2, dact, normed2, ctx2, dlow2, n1, r1, gsec, attn, attn_s, gctx, gup_s, gm_s, probs,
                    w_big, w_small, w_out, packed, packed_s, g_row, *rest):
    scratch = list(rest[:-8])
    send, recv, ssend, srecv, insem, wsem, xsend, xrecv = rest[-8:]
    place = Place()
    core = place.core
    loads = {}

    def load(name, src, dst):
        c = pltpu.make_async_copy(src, dst, insem.at[len(loads)])
        c.start()
        loads[name] = c

    def ready(*names):
        for name in names:
            loads[name].wait()

    def w_load(i, src, dst):
        c = pltpu.make_async_copy(src, dst, wsem.at[i])
        return c

    load("dlow", dlow2_h, dlow2)
    def down_load(j, slot):
        return w_load(slot, wdown_h.at[j // 2, pl.ds(lax.rem(j, 2) * 2, 2)], w_small.at[slot])

    for j in range(2):
        down_load(j, j).start()
    load("dact", dact_h, dact)
    load("active", active2_h, act2)
    greet(place)
    red = Reduce(place, scratch, {QKV: o_qkv, OUT: o_out, UP: o_up, DOWN: o_down, SMALL: o_small},
                 send, recv, ssend, srecv)
    cross = Wire(xsend, xrecv)

    def mine(size):
        return pl.ds(pl.multiple_of(core * size, 128), size)

    def other(size):
        return pl.ds(pl.multiple_of((1 - core) * size, 128), size)

    ready("dlow", "dact")
    def hidden(j):
        slot = lax.rem(j, 2)
        down_load(j, slot).wait()
        c = span(j, D)
        g = dot(dlow2[0], w_small[slot].reshape(D, D), ((1,), (1,)))
        dact[:, c] = (g * dact[:, c].astype(F32)).astype(BF)
        pl.when(j < 2)(lambda: down_load(j + 2, slot).start())

    loop(4, hidden)
    load("normed", normed2_h, normed2)
    load("gsec", gsec_h, gsec)
    load("n1", n1_h, n1)
    load("r1", r1_h, r1)
    load("wout", wout_h, w_out)
    load("ctx", ctx2_h, ctx2)
    load("probs", probs_h, probs)
    load("tokens", tokens2, tok2)
    gup = dact
    cross.go(0, gup.at[:, other(FF // 2)], gup_s, place.sibling)

    def up_load(j, slot):
        return w_load(2 + slot, wup_h.at[span(j, 256)], w_big.at[slot])

    def qkv_load(j, slot):
        return w_load(2 + slot, wqkv_h.at[span(j, 256)], w_big.at[slot, :, pl.ds(0, 3 * D)])

    for j in range(2):
        up_load(j, j).start()
    ready("active")

    def down(j):
        left = dlow2[:, :, mine(384)].reshape(2 * TOK, 384)
        g = dot(left, act2[:, :, span(j, D)].reshape(2 * TOK, D), ((0,), (0,))).T.astype(BF)
        for k in range(3):
            red.held[DOWN, k][j // 2, pl.ds(lax.rem(j, 2) * 2, 2)] = g[:, 128 * k:128 * k + 128].reshape(2, 4, 96, 128)

    loop(4, down)
    red.start((DOWN, 0), (DOWN, 1), (DOWN, 2))
    ready("normed")
    load("merged", merged_h, act2.at[0, :, pl.ds(0, 3 * D)])
    merged = act2.at[0, :, pl.ds(0, 3 * D)]
    cross.landed(0, gup_s, place.sibling)
    for k in range(3):
        own = gup[:, pl.ds(pl.multiple_of(core * (FF // 2) + 512 * k, 128), 512)]

        def grad_up():
            lay(red.held[UP, k], dot(normed2[0], own, ((0,), (0,))) + dot(normed2[1], gup_s[:, 512 * k:512 * k + 512], ((0,), (0,))))

        once(grad_up)
        red.start((UP, k))
    ready("gsec", "n1", "r1")

    def g_normed(j):
        slot = lax.rem(j, 2)
        up_load(j, slot).wait()
        c = span(j, 256)
        gsec[:, c] = gsec[:, c] + dot(gup[...], w_big[slot], ((1,), (1,)))
        pl.when(j < 1)(lambda: up_load(j + 2, slot).start())

    loop(3, g_normed)
    red.pump(DOWN)
    for j in range(2):
        qkv_load(j, 1 - j).start()
    gain1 = rows[0, pl.ds(0, 1), :]

    def norm1(j):
        r = span(j, 384)
        g, n = gsec[r, :], n1[r, :].astype(F32)
        part = jnp.sum(g * n, axis=0, keepdims=True)
        g_row[0:1] = jnp.where(j == 0, part, part + g_row[0:1])
        g = norm_back(g, gain1, n, r1[r, pl.ds(0, 1)])
        gsec[r, :] = g
        attn[r, :] = g.astype(BF)

    loop(2, norm1)
    cross.go(1, attn.at[:, other(384)], attn_s, place.sibling)
    ready("wout", "ctx")

    def context(j):
        r = span(j, 384)
        gctx[r, :] = dot(attn[r, :], w_out[...], ((1,), (1,))).astype(BF)

    loop(2, context)

    def pack_small():
        p_proj, p_hid, p_cls, p_misc = picks()
        pack = dot(p_proj, small[3:9].reshape(D, 128), ((0,), (0,)))
        pack = pack + dot(p_hid, small[0], ((0,), (0,)))
        lane = iota((128, 128), 1)
        pack = pack + dot(p_cls, jnp.where(lane < 14, small[1].astype(F32), 0.0).astype(BF), ((0,), (0,)))
        values = (g_row[0:1], rows[3, pl.ds(0, 1), :], small[2, pl.ds(0, 1), :].astype(F32))
        misc = jnp.zeros((32, 128), F32)
        for (name, first, size, per), value in zip(ROWS, values):
            tile, held = spread(first, size, per)
            misc = misc + dot(jnp.where(held, value, 0.0).astype(BF), tile, ((1,), (1,)))
        packed[...] = (pack + dot(p_misc, misc.astype(BF), ((0,), (0,)))).astype(BF).reshape(2, 4, 4, 32, 128)

    once(pack_small)
    place.on_core(lambda c: cross.copy(3, packed.at[:, :, :, pl.ds(16 - 16 * c, 16)], packed_s, place.sibling).start())

    ready("merged", "probs")

    low_half, high_half = halves()
    la, lb = low_half.astype(BF), high_half.astype(BF)
    qa, qb = (low_half * 0.125).astype(BF), (high_half * 0.125).astype(BF)

    def attend_back(s):
        r = span(s, SEQ)
        at = [[pl.ds(768 * a + 128 * p, 128) for a in range(3)] for p in range(PAIRS)]
        d2, q2, gp, gs = [], [], [], []
        for p in range(PAIRS):
            q, d = merged[r, at[p][0]], gctx[r, pl.ds(128 * p, 128)]
            d2.append(jnp.concatenate([d * la, d * lb], axis=0))
            q2.append(jnp.concatenate([q * qa, q * qb], axis=0))
            gp.append(dot(d2[p], merged[r, at[p][2]], ((1,), (1,))))
        for p in range(PAIRS):
            pr = probs[s * PAIRS + p]
            merged[r, at[p][2]] = dot(pr, d2[p], ((0,), (0,))).astype(BF)
            pf = pr.astype(F32)
            t = pf * gp[p]
            gs.append((t - pf * jnp.sum(t, axis=-1, keepdims=True)).astype(BF))
        for p in range(PAIRS):
            both = dot(gs[p], merged[r, at[p][1]])
            merged[r, at[p][0]] = ((both[:SEQ] * low_half + both[SEQ:] * high_half) * 0.125).astype(BF)
            merged[r, at[p][1]] = dot(gs[p], q2[p], ((0,), (0,))).astype(BF)

    for part in range(3):

        def attend_part(s):
            attend_back(s + 2 * part)

        loop(2, attend_part)
        if part != 1:
            red.pump(DOWN, UP)
    cross.go(2, act2.at[0, :, other(3 * D // 2)], gm_s, place.sibling)
    ready("tokens")

    def g_tokens(j):
        slot = lax.rem(j + 1, 2)
        qkv_load(j, slot).wait()
        c = span(j, 256)
        gsec[:, c] = gsec[:, c] + dot(merged[...], w_big[slot, :, :3 * D], ((1,), (1,)))
        pl.when(j < 1)(lambda: qkv_load(j + 2, slot).start())

    lax.fori_loop(0, 1, lambda j, c: (g_tokens(j), c)[1], 0)
    cross.landed(2, gm_s, place.sibling)
    for k in range(3):
        own = merged[:, pl.ds(pl.multiple_of(core * (3 * D // 2) + 384 * k, 128), 384)]

        def grad_qkv():
            lay(red.held[QKV, k], dot(tok2[0], own, ((0,), (0,))) + dot(tok2[1], gm_s[:, 384 * k:384 * k + 384], ((0,), (0,))))

        once(grad_qkv)
        red.start((QKV, k))
    red.pump(DOWN, UP)
    cross.landed(1, attn_s, place.sibling)

    def grad_out():
        g = dot(ctx2[0], attn[:, mine(384)], ((0,), (0,))) + dot(ctx2[1], attn_s[...], ((0,), (0,)))
        for k in range(3):
            lay(red.held[OUT, k], g[:, 128 * k:128 * k + 128])

    once(grad_out)
    cross.landed(3, packed_s, place.sibling)

    def small_half(c):
        red.held[SMALL, 1][...] = packed[:, :, :, 16 * c:16 * c + 16, :] + packed_s[...]

    place.on_core(small_half)
    red.start((OUT, 0), (OUT, 1), (OUT, 2), (SMALL, 1))
    red.pump(DOWN, UP)
    lax.fori_loop(1, 3, lambda j, c: (g_tokens(j), c)[1], 0)
    red.pump()
    store = pltpu.make_async_copy(gsec, o_gtok, insem.at[len(loads)])
    store.start()
    red.end()
    cross.sent()
    place.on_core(lambda c: cross.copy(3, packed.at[:, :, :, pl.ds(16 - 16 * c, 16)], packed_s, place.sibling).wait_send())
    store.wait()


def backward(*args):
    hbm, vmem = pl.BlockSpec(memory_space=pl.ANY), pl.BlockSpec(memory_space=pltpu.VMEM)

    def arr(*shape, dtype=F32):
        return jax.ShapeDtypeStruct(shape, dtype)

    dma = pltpu.SemaphoreType.DMA
    count = len(PIECES)
    scratch = [
        pltpu.VMEM((2, TOK, D), BF), pltpu.VMEM((2, TOK, FF), BF), pltpu.VMEM((TOK, FF), BF),
        pltpu.VMEM((2, TOK, D), BF), pltpu.VMEM((2, TOK, D), BF), pltpu.VMEM((2, TOK, D), BF),
        pltpu.VMEM((TOK, D), BF), pltpu.VMEM((TOK, 128), F32), pltpu.VMEM((TOK, D), F32),
        pltpu.VMEM((TOK, D), BF), pltpu.VMEM((TOK, D // 2), BF), pltpu.VMEM((TOK, D), BF),
        pltpu.VMEM((TOK, FF // 2), BF), pltpu.VMEM((TOK, 3 * D // 2), BF),
        pltpu.VMEM((SEQ_DEV * PAIRS, 256, 128), BF),
        pltpu.VMEM((2, 256, FF), BF), pltpu.VMEM((2, 2, 4, 96, D), BF), pltpu.VMEM((D, D), BF),
        pltpu.VMEM((2, 4, 4, 32, 128), BF), pltpu.VMEM((2, 4, 4, 16, 128), BF), pltpu.VMEM((8, D), F32),
    ] + reduce_scratch() + [
        dma((count * SUMS,)), dma((count * SUMS,)), dma((count,)), dma((count,)), dma((16,)), dma((4,)), dma((4,)), dma((4,)),
    ]
    return pl.pallas_call(
        backward_kernel,
        out_shape=[arr(TOK, D), arr(24, 3 * D), arr(24, D), arr(24, FF), arr(96, D), arr(32, 128)],
        in_specs=[hbm] * 15 + [vmem] * 2,
        out_specs=[hbm] + [vmem] * 5,
        scratch_shapes=scratch,
        compiler_params=pltpu.CompilerParams(collective_id=1, has_side_effects=True, vmem_limit_bytes=VMEM),
        cost_estimate=pl.CostEstimate(flops=24 * 10**9, bytes_accessed=60 * 10**6, transcendentals=0),
        name="backward",
    )(*args)


def finish_kernel(act, logits, gtok, qkv, out, up, down, small, *outs):
    o_act, o_logits, o_gtok, o_qkv, o_out, o_g1, o_up, o_down, o_g2, o_proj, o_pool, o_hid, o_cls = outs
    o_act[...] = act[...]
    o_gtok[...] = gtok[...]

    @pl.when(pl.program_id(0) == 0)
    def _():
        o_logits[...] = logits[0:SEQ_DEV, 0:14]
        o_qkv[...] = qkv[...]
        o_out[...] = out[...]
        o_up[...] = up[...]
        o_down[...] = down[...]
        o_proj[...] = small[0:24]
        o_hid[...] = small[24:28]
        o_cls[...] = small[28:32, 0:14]
        o_g1[...] = small[28:29, 16:40]
        o_g2[...] = small[28:29, 40:64]
        o_pool[...] = small[28:29, 64:68]


def finish(*args):
    def spec(shape):
        if shape[0] == TOK:
            return pl.BlockSpec((SEQ, shape[1]), lambda i: (i, 0))
        return pl.BlockSpec(shape, lambda i: (0, 0))

    shapes = ((TOK, D), (SEQ_DEV, 14), (TOK, D), (24, 3 * D), (24, D), (1, 24), (24, FF), (96, D), (1, 24), (24, 128),
              (1, 4), (4, 128), (4, 14))
    return pl.pallas_call(
        finish_kernel,
        grid=(SEQ_DEV,),
        out_shape=[jax.ShapeDtypeStruct(s, F32 if n else BF) for n, s in enumerate(shapes)],
        in_specs=[spec(a.shape) for a in args],
        out_specs=[spec(s) for s in shapes],
        name="finish",
    )(*args)


def local(tokens, exit_layer, w_qkv, w_out, gain_attn, w_up, w_down, gain_ffn, w_proj, pool_query, w_hid, w_cls,
          cot_out, cot_logits):
    line = jnp.concatenate([gain_attn, gain_ffn, pool_query])
    last = jnp.pad(w_cls, ((0, 0), (0, 128 - 14)))
    last = last + jnp.pad(line[None], ((0, 3), (16, 128 - 16 - line.shape[0])))
    small = jnp.concatenate([w_proj, w_hid, last], axis=0)
    (act, logits, f_qkv, f_out, f_up, f_down, merged, probs, ctx, normed, n1, r1, active, dact, gsec, dlow, tokens2,
     small_g, rows) = forward(tokens, cot_out, exit_layer, cot_logits, (small, w_qkv, w_out, w_up, w_down))
    g_tok, g_qkv, g_out, g_up, g_down, g_small = backward(
        tokens2, merged, probs, ctx, normed, n1, r1, active, dact, gsec, dlow, f_qkv, f_out, f_up, f_down, small_g, rows)
    outs = list(finish(act, logits, g_tok, g_qkv, g_out, g_up, g_down, g_small))
    for n in (5, 8, 10):
        outs[n] = outs[n].reshape(-1)
    return tuple(outs)


def solution(mesh):
    both, wide = P(("wide", "grp"), None), P("wide", None)
    in_specs = (both, P(("wide", "grp")), wide, wide, P("wide"), wide, wide, P("wide"), wide, P("wide"), wide, wide,
                both, both)
    out_specs = (both, both, both, wide, wide, P("wide"), wide, wide, P("wide"), wide, P("wide"), wide, wide)
    return jax.shard_map(local, mesh=mesh, in_specs=in_specs, out_specs=out_specs, check_vma=False)
```

```python
import functools
import jax
import jax.numpy as jnp
from jax import lax
from jax.sharding import PartitionSpec as P
from jax.experimental import pallas as pl
from jax.experimental.pallas import tpu as pltpu

D = 768
FF = 3072
TOK = 768
SEQ_DEV = 6
PAIRS = 6
SEQ = 128
LAYER = 3
MESH = pl.DeviceIdType.MESH
BF = jnp.bfloat16
F32 = jnp.float32
SIZE = {"x": 2, "z": 4, "y": 4}
ORDERS = (
    (("y", "z", "x"), ("z", "x", "y"), ("y", "x", "z")),
    (("z", "y", "x"), ("z", "x", "y"), ("y", "x", "z")),
)
EVENTS = 7
SUMS = 8
VMEM = 62 * 2**20


class Place:
    def __init__(self):
        wide, grp = lax.axis_index("wide"), lax.axis_index("grp")
        xl, z, y = wide // 16, (wide // 4) % 4, wide % 4
        x = (grp // 2) * 2 + xl
        self.core = grp % 2
        self.places = {("x", 0): xl, ("x", 1): 1 - xl}
        for axis, here in (("z", z), ("y", y)):
            for step in range(4):
                self.places[axis, step] = (here + step) % 4
        self.ids = {}
        for step in (1, 2, 3):
            far = (x + step) % 4
            self.ids["x", step] = ((far % 2) * 16 + z * 4 + y, (far // 2) * 2 + self.core)
            self.ids["y", step] = (xl * 16 + z * 4 + self.places["y", step], grp)
            self.ids["z", step] = (xl * 16 + self.places["z", step] * 4 + y, grp)
        self.sibling = (wide, grp + 1 - 2 * self.core)

    def near(self, axis, step):
        return self.ids[axis, step % 4]

    def at(self, axis, step=0):
        return self.places[axis, step % SIZE[axis]]

    def box(self, have, **fixed):
        out = []
        for axis in ("x", "z", "y"):
            if axis in fixed:
                out.append(fixed[axis])
            elif axis in have:
                out.append(slice(None))
            else:
                out.append(self.at(axis))
        return tuple(out)

    def on_core(self, step):
        for core in (0, 1):
            pl.when(self.core == core)(functools.partial(step, core))


def greet(place):
    barrier = pltpu.get_barrier_semaphore()
    ids = [place.near(a, s) for a in ("x", "y", "z") for s in (1, -1, 2)] + [place.sibling]
    for i in ids:
        pl.semaphore_signal(barrier, inc=1, device_id=i, device_id_type=MESH)
    pl.semaphore_wait(barrier, len(ids))


class Wire:
    def __init__(self, send, recv):
        self.send, self.recv = send, recv
        self.started = []

    def copy(self, n, src, dst, to):
        return pltpu.make_async_remote_copy(
            src_ref=src, dst_ref=dst, send_sem=self.send.at[n], recv_sem=self.recv.at[n],
            device_id=to, device_id_type=MESH,
        )

    def go(self, n, src, dst, to):
        self.copy(n, src, dst, to).start()
        self.started.append((n, src, dst, to))

    def landed(self, n, dst, to):
        self.copy(n, dst, dst, to).wait_recv()

    def sent(self):
        for c in self.started:
            self.copy(*c).wait_send()


def piece(kind, core, k, width):
    if kind == "cols":
        return (slice(None), pl.ds((core * 3 + k) * (width // 6), width // 6))
    return (pl.ds(core * 16, 16), slice(None)) if k == 1 else None


class Lane:
    def __init__(self, send, recv, first_send, first_recv):
        self.send, self.recv, self.first_send, self.first_recv = send, recv, first_send, first_recv
        self.out, self.count = {}, 0

    def copy(self, slot, e, src, dst, to):
        return pltpu.make_async_remote_copy(
            src_ref=src, dst_ref=dst, send_sem=self.send.at[self.first_send + slot],
            recv_sem=self.recv.at[self.first_recv + e], device_id=to, device_id_type=MESH,
        )

    def go(self, e, src, dst, to):
        slot = self.count % 3
        self.count += 1
        if slot in self.out:
            self.copy(slot, *self.out[slot]).wait_send()
        self.copy(slot, e, src, dst, to).start()
        self.out[slot] = (e, src, dst, to)

    def landed(self, e, dst, to):
        self.copy(0, e, dst, dst, to).wait_recv()

    def sent(self):
        for slot, c in self.out.items():
            self.copy(slot, *c).wait_send()


def gather_unit(place, lane, sib, core, order, own, full):
    way = 1 if core == 0 else -1
    have, e = [], 0
    for axis in order:
        mine = place.box(have)
        src = full(mine) if have else own
        ahead, back, far = place.near(axis, way), place.near(axis, -way), place.near(axis, 2)
        last = axis == order[2]
        if axis == "x":
            lane.go(e, src, full(mine), ahead)
            yield
            got = place.box(have, x=place.at("x", 1))
            lane.landed(e, full(got), ahead)
            if last:
                sib(got)
            e += 1
        elif not have:
            for n, to in enumerate((ahead, back, far)):
                lane.go(e + n, src, full(mine), to)
            yield
            for n, step in enumerate((-way, way, 2)):
                lane.landed(e + n, full(place.box(have, **{axis: place.at(axis, step)})), ahead)
            e += 3
        else:
            lane.go(e, src, full(mine), ahead)
            lane.go(e + 1, src, full(mine), back)
            yield
            got = place.box(have, **{axis: place.at(axis, -way)})
            lane.landed(e, full(got), ahead)
            lane.go(e + 2, full(got), full(got), ahead)
            if last:
                sib(got)
            yield
            for late, step in ((1, way), (2, 2)):
                got = place.box(have, **{axis: place.at(axis, step)})
                lane.landed(e + late, full(got), ahead)
                if last:
                    sib(got)
            e += 3
        have.append(axis)
        if axis == order[1]:
            sib(place.box(have))


class Gather:
    def __init__(self, place, kinds, shards, fulls, send, recv, side, keep):
        self.place, self.kinds, self.shards, self.fulls = place, kinds, shards, fulls
        self.side, self.keep = side, keep
        n = len(kinds)
        self.lanes = [[], []]
        self.units = [[[] for _ in range(n)] for _ in range(2)]
        for core in range(2):
            for i in range(n):
                for k in range(3):
                    tail = piece(kinds[i], core, k, shards[i].shape[-1])
                    if tail is None:
                        continue
                    at = len(self.lanes[core])
                    lane = Lane(send, recv, at * 3, at * EVENTS)
                    self.lanes[core].append(lane)
                    full = functools.partial(self.part, i, tail)
                    sib = functools.partial(self.pass_on, i, full)
                    self.units[core][i].append(gather_unit(
                        place, lane, sib, core, ORDERS[core][k], shards[i].at[tail], full))

    def part(self, i, tail, box):
        return self.fulls[i].at[box + tail]

    def half(self, i, core):
        size = self.shards[i].shape[-1] // 2
        if self.kinds[i] == "cols":
            return (slice(None), pl.ds(core * size, size))
        return (pl.ds(core * 16, 16), slice(None))

    def to_side(self, sems, n, src, dst):
        return pltpu.make_async_remote_copy(
            src_ref=src, dst_ref=dst, send_sem=sems.at[n], recv_sem=sems.at[len(self.kinds) + n],
            device_id=self.place.sibling, device_id_type=MESH)

    def pass_on(self, i, full, box):
        self.to_side(self.side, i, full(box), full(box)).start()

    def own(self, i, core):
        half = self.half(i, 1 - core)
        return self.to_side(self.keep, i, self.shards[i].at[half], self.fulls[i].at[self.place.box(()) + half])

    def own_start(self):
        self.place.on_core(lambda core: [self.own(i, core).start() for i in range(len(self.kinds))] and None)

    def own_landed(self):
        def one(core):
            for i in range(len(self.kinds)):
                self.own(i, core).wait_send()
                self.own(i, 1 - core).wait_recv()

        self.place.on_core(one)

    def step(self, *arrays):
        def one(core):
            for i in arrays:
                for u in self.units[core][i]:
                    next(u, None)

        self.place.on_core(one)

    def everything(self, i, core):
        part = self.fulls[i].at[(slice(None),) * 3 + self.half(i, core)]
        return self.to_side(self.side, i, part, part)

    def whole(self, *arrays):
        def one(core):
            for i in arrays:
                self.everything(i, 1 - core).wait_recv()

        self.place.on_core(one)

    def end(self):
        def one(core):
            for lane in self.lanes[core]:
                lane.sent()
            for i in range(len(self.kinds)):
                self.everything(i, core).wait_send()

        self.place.on_core(one)


def dot(a, b, dims=((1,), (0,))):
    return lax.dot_general(a, b, (dims, ((), ())), preferred_element_type=F32)


def exact(a, b, dims=((1,), (0,))):
    return lax.dot_general(a, b, (dims, ((), ())), precision=lax.Precision.HIGHEST, preferred_element_type=F32)


def iota(shape, dim):
    return lax.broadcasted_iota(jnp.int32, shape, dim)


def over24(i):
    return (i * 2731) >> 16


def ones_where(hit):
    return jnp.where(hit, 1.0, 0.0).astype(BF)


def picks():
    i, j = iota((768, 1024), 0), iota((768, 1024), 1)
    proj = ones_where(j == i + 8 * over24(i))
    i, j = iota((128, 1024), 0), iota((128, 1024), 1)
    at = 32 * (i >> 2) + (i & 3)
    hid, cls = ones_where(j == at + 24), ones_where(j == at + 28)
    i, j = iota((32, 1024), 0), iota((32, 1024), 1)
    misc = ones_where(j == 32 * i + 28)
    return proj, hid, cls, misc


def spread(first, size, per):
    i, l = iota((128, size), 0), iota((128, size), 1)
    block = over24(l) if per == 24 else l >> 2
    w, m = iota((32, size), 0), iota((32, size), 1)
    held = over24(m) if per == 24 else m >> 2
    return ones_where(i - first == l - per * block), held == w


ROWS = (("gain_attn", 16, 768, 24), ("gain_ffn", 40, 768, 24), ("pool", 64, 128, 4))


def normalise(h):
    centre = h - jnp.mean(h, axis=-1, keepdims=True)
    r = lax.rsqrt(jnp.mean(centre * centre, axis=-1, keepdims=True) + 1e-06)
    return centre * r, r


def norm_back(g, gain, n, r):
    gn = g * gain
    return r * (gn - jnp.mean(gn, axis=-1, keepdims=True) - n * jnp.mean(gn * n, axis=-1, keepdims=True))


TANH_A = 0.7978845608028654
TANH_B = 0.7978845608028654 * 0.044715


def gelu(u):
    u2 = u * u
    h = 0.5 + 0.5 * jnp.tanh(u * (TANH_A + TANH_B * u2))
    y = u * h
    return y, h + y * (1.0 - h) * (2.0 * TANH_A + 6.0 * TANH_B * u2)


def at_block(i):
    return i // 8, (i // 2) % 4, i % 2


def join(blocks, whole):
    def one(i, carry):
        x, z, y = at_block(i)
        pair = jnp.concatenate([blocks[x, z, 2 * y], blocks[x, z, 2 * y + 1]], axis=0)
        whole[pl.ds(pl.multiple_of(i * 48, 48), 48), :] = pair
        return carry

    lax.fori_loop(0, 16, one, 0)


def loop(n, step):
    def one(i, carry):
        step(i)
        return carry

    lax.fori_loop(0, n, one, 0)


def once(step):
    step()


def span(i, size):
    return pl.ds(pl.multiple_of(i * size, size), size)


def halves():
    lane = iota((1, 128), 1)
    return jnp.where(lane < 64, 1.0, 0.0), jnp.where(lane < 64, 0.0, 1.0)


KINDS = ("small", "cols", "cols", "cols", "cols")
SMALL, QKV, OUT, UP, DOWN = range(5)


def forward_kernel(tokens, cot, exit_layer, cot_logits, s_small, s_qkv, s_out, s_up, s_down,
                   o_act, o_logits, o_wqkv, o_wout, o_wup, o_merged, o_probs, o_ctx, o_normed, o_n1, o_r1,
                   o_active, o_gup, o_gup_s, o_gsec, o_dlow, o_tokens2, o_small, rows,
                   b_small, b_qkv, b_out, b_up, b_down, w_qkv, w_out, w_up, tok, cotv, merged, probs, ctx, normed, n1, r1,
                   active, dact, gsec, r2, dlow, out, projected, gproj, wproj, hid, cls,
                   alive, alive_seq, cotl, send, recv, ssem, lsem, insem, outsem, xsend, xrecv):
    place = Place()
    loads = [pltpu.make_async_copy(tokens, tok, insem.at[0]), pltpu.make_async_copy(cot, cotv, insem.at[1])]
    for c in loads:
        c.start()
    greet(place)
    g = Gather(place, KINDS, (s_small, s_qkv, s_out, s_up, s_down), (b_small, b_qkv, b_out, b_up, b_down),
               send, recv, ssem, lsem)
    stores = []
    cross = Wire(xsend, xrecv)

    def keep(src, dst):
        c = pltpu.make_async_copy(src, dst, outsem.at[len(stores)])
        c.start()
        stores.append(c)

    def share(n, src, dst):
        keep(src, dst.at[0])
        cross.go(n, src, dst.at[1], place.sibling)

    g.step(QKV, SMALL)
    g.own_start()
    g.step(OUT, UP, DOWN)
    loads[0].wait()
    cotl[...] = jnp.zeros((8, 128), F32)
    cotl[0:SEQ_DEV, 0:14] = cot_logits[...]
    alive_seq[...] = jnp.zeros((8, 128), F32)
    for s in range(SEQ_DEV):
        stays = jnp.clip(exit_layer[s] - (LAYER - 1), 0, 1).astype(F32)
        alive[pl.ds(s * SEQ, SEQ), :] = jnp.full((SEQ, 128), stays)
        alive_seq[pl.ds(s, 1), :] = jnp.full((1, 128), stays)
    g.own_landed()
    g.step(QKV, SMALL)
    g.step(OUT, UP, DOWN)
    g.step(QKV, SMALL)
    g.step(QKV, SMALL)
    g.step(OUT, UP, DOWN)
    g.step(QKV, SMALL)
    g.whole(QKV, SMALL)
    join(b_qkv, w_qkv)

    def qkv(j):
        c = span(j, D)
        merged[:, c] = dot(tok[...], w_qkv[:, c]).astype(BF)

    loop(3, qkv)
    keep(w_qkv, o_wqkv)
    keep(merged, o_merged)
    g.step(OUT, UP)

    def small_weights():
        p_proj, p_hid, p_cls, p_misc = picks()
        pack = b_small[...].reshape(1024, 128)
        wproj[...] = dot(p_proj, pack).astype(BF)
        hid[...] = dot(p_hid, pack)
        cls[...] = jnp.where(iota((128, 128), 1) < 14, dot(p_cls, pack), 0.0)
        misc = dot(p_misc, pack).astype(BF)
        for n, (name, first, size, per) in enumerate(ROWS):
            tile, held = spread(first, size, per)
            row = jnp.sum(jnp.where(held, dot(misc, tile), 0.0), axis=0, keepdims=True)
            rows[n, :, pl.ds(0, size)] = jnp.broadcast_to(row, (8, size))

    once(small_weights)
    low_half, high_half = halves()

    qa, qb = (low_half * 0.125).astype(BF), (high_half * 0.125).astype(BF)

    def attend(s):
        r = span(s, SEQ)
        scores, prs = [], []
        for p in range(PAIRS):
            q, k = (merged[r, pl.ds(768 * a + 128 * p, 128)] for a in range(2))
            scores.append(dot(jnp.concatenate([q * qa, q * qb], axis=0), k, ((1,), (1,))))
        for p in range(PAIRS):
            e = jnp.exp(scores[p] - jnp.max(scores[p], axis=-1, keepdims=True))
            prs.append((e * (1.0 / jnp.sum(e, axis=-1, keepdims=True))).astype(BF))
            probs[s * PAIRS + p] = prs[p]
        for p in range(PAIRS):
            both = dot(prs[p], merged[r, pl.ds(1536 + 128 * p, 128)])
            ctx[r, pl.ds(128 * p, 128)] = (both[:SEQ] * low_half + both[SEQ:] * high_half).astype(BF)

    for part, late in enumerate((DOWN, None, UP)):

        def attend_two(s):
            attend(s + 2 * part)

        loop(2, attend_two)
        if late:
            g.step(late)
        if part == 1:
            g.step(OUT)
    keep(probs, o_probs)
    g.whole(OUT)
    join(b_out, w_out)
    gain1 = rows[0, pl.ds(0, 1), :]

    def mix(j):
        r = span(j, 384)
        n, inv = normalise(tok[r, :].astype(F32) + dot(ctx[r, :], w_out[...]))
        n1[r, :] = n.astype(BF)
        normed[r, :] = (n * gain1).astype(BF)
        r1[r, :] = jnp.broadcast_to(inv, (384, 128))

    loop(2, mix)
    g.whole(UP)
    share(2, normed, o_normed)
    share(1, ctx, o_ctx)
    share(0, tok, o_tokens2)
    keep(w_out, o_wout)
    keep(n1, o_n1)
    keep(r1, o_r1)
    join(b_up, w_up)

    def active_part(j):
        c = span(j, D)
        return pltpu.make_async_remote_copy(
            src_ref=active.at[:, c], dst_ref=o_active.at[1, :, c], send_sem=xsend.at[5 + j], recv_sem=xrecv.at[5 + j],
            device_id=place.sibling, device_id_type=MESH)

    def upward(j):
        c = span(j, D)
        y, dy = gelu(dot(normed[...], w_up[:, c]))
        active[:, c] = y.astype(BF)
        dact[:, c] = dy.astype(BF)
        active_part(j).start()

    def upward_late(j):
        upward(j + 2)

    loop(2, upward)
    g.step(DOWN)
    loop(2, upward_late)
    g.whole(DOWN)
    keep(active, o_active.at[0])
    keep(w_up, o_wup)
    loads[1].wait()
    gain2 = rows[1, pl.ds(0, 1), :]

    def downward(j):
        r = span(j, 384)
        second = normed[r, :].astype(F32) + dot(active[r, :], b_down[...].reshape(FF, D))
        n, inv = normalise(second)
        gsec[r, :] = n
        r2[r, :] = jnp.broadcast_to(inv, (384, 128))
        low = (n * gain2).astype(BF)
        out[r, :] = low
        projected[r, :] = dot(low, wproj[...])

    loop(2, downward)

    query = rows[2, pl.ds(0, 1), pl.ds(0, 128)]

    def student():
        weights, pooled = [], []
        for s in range(SEQ_DEV):
            pr = projected[pl.ds(s * SEQ, SEQ), :]
            t = pr * query
            per_head = []
            for half in (low_half, high_half):
                score = jnp.sum(t * half, axis=-1, keepdims=True) * 0.125
                e = jnp.exp(score - jnp.max(score, axis=0, keepdims=True))
                per_head.append(e / jnp.sum(e, axis=0, keepdims=True))
            weights.append(per_head)
            pooled.append(jnp.sum(pr * (per_head[0] * low_half + per_head[1] * high_half), axis=0, keepdims=True))
        none = jnp.zeros((1, 128), F32)
        pooled = jnp.concatenate(pooled + [none, none], axis=0)
        hidden = jnp.tanh(exact(pooled, hid[...]))
        o_logits[...] = exact(hidden, cls[...]) * alive_seq[...]
        g_log = cotl[...] * alive_seq[...]
        o_small[1] = exact(hidden, g_log, ((0,), (0,))).astype(BF)
        g_pre = exact(g_log, cls[...], ((1,), (1,))) * (1.0 - hidden * hidden)
        o_small[0] = exact(pooled, g_pre, ((0,), (0,))).astype(BF)
        g_pooled = exact(g_pre, hid[...], ((1,), (1,)))
        g_query = none
        for s in range(SEQ_DEV):
            r = pl.ds(s * SEQ, SEQ)
            pr = projected[r, :]
            gp = g_pooled[s:s + 1]
            t = pr * gp
            total = (weights[s][0] * low_half + weights[s][1] * high_half) * gp
            for half, w in zip((low_half, high_half), weights[s]):
                dw = jnp.sum(t * half, axis=-1, keepdims=True)
                ds = w * (dw - jnp.sum(w * dw, axis=0, keepdims=True)) * 0.125
                total = total + ds * (query * half)
                g_query = g_query + jnp.sum(ds * pr, axis=0, keepdims=True) * half
            gproj[r, :] = total.astype(BF)
        o_small[2] = jnp.broadcast_to(g_query, (128, 128)).astype(BF)

    once(student)

    def back(j):
        r = span(j, 384)
        keep_tok = alive[r, pl.ds(0, 1)]
        low = out[r, :]
        g_out = keep_tok * cotv[r, :].astype(F32) + dot(gproj[r, :], wproj[...], ((1,), (1,)))
        n = gsec[r, :]
        part = jnp.sum(g_out * n, axis=0, keepdims=True)
        rows[3, pl.ds(0, 1), :] = jnp.where(j == 0, part, part + rows[3, pl.ds(0, 1), :])
        g2 = norm_back(g_out, gain2, n, r2[r, pl.ds(0, 1)])
        gsec[r, :] = g2
        dlow[r, :] = g2.astype(BF)
        cotv[r, :] = (keep_tok * low.astype(F32)).astype(BF)
        low_part(j).start()
        for c in late(j):
            c.start()

    def low_part(j):
        r = span(j, 384)
        return pltpu.make_async_remote_copy(
            src_ref=dlow.at[r], dst_ref=o_dlow.at[1, r], send_sem=xsend.at[9 + j], recv_sem=xrecv.at[9 + j],
            device_id=place.sibling, device_id_type=MESH)

    def late(j):
        r = span(j, 384)
        return [pltpu.make_async_copy(src.at[r], dst.at[r], outsem.at[16 + 3 * j + n])
                for n, (src, dst) in enumerate(((dlow, o_dlow.at[0]), (gsec, o_gsec), (cotv, o_act)))]

    loop(2, back)

    def hidden_copy(j):
        c = span(j, D)
        return pltpu.make_async_copy(dact.at[:, c], o_gup.at[:, c], outsem.at[22 + j])

    def hidden_part(j):
        return pltpu.make_async_remote_copy(
            src_ref=dact.at[:, span(j, D)], dst_ref=o_gup_s.at[:, span(lax.rem(j, 2), D)],
            send_sem=xsend.at[11 + lax.rem(j, 2)], recv_sem=xrecv.at[11 + lax.rem(j, 2)],
            device_id=place.sibling, device_id_type=MESH)

    def hidden(j):
        c = span(j, D)
        part = b_down[j // 2, pl.ds(lax.rem(j, 2) * 2, 2)].reshape(D, D)
        dact[:, c] = (dot(dlow[...], part, ((1,), (1,))) * dact[:, c].astype(F32)).astype(BF)
        hidden_copy(j).start()
        pl.when(j // 2 != place.core)(lambda: hidden_part(j).start())

    loop(4, hidden)

    def proj_grad():
        o_small[3:9] = dot(out[...], gproj[...], ((0,), (0,))).astype(BF).reshape(6, 128, 128)

    once(proj_grad)
    g.end()
    for c in stores + late(0) + late(1) + [hidden_copy(j) for j in range(4)] + [hidden_part(j) for j in range(2)]:
        c.wait()
    for n, dst in ((0, o_tokens2), (1, o_ctx), (2, o_normed)):
        cross.landed(n, dst.at[1], place.sibling)
    cross.sent()
    for c in [active_part(j) for j in range(4)] + [low_part(j) for j in range(2)]:
        c.wait()


def forward(tokens, cot, exit_layer, cot_logits, shards):
    hbm, vmem = pl.BlockSpec(memory_space=pl.ANY), pl.BlockSpec(memory_space=pltpu.VMEM)
    n = len(KINDS)
    count = n * 3 - 2

    def arr(*shape, dtype=BF):
        return jax.ShapeDtypeStruct(shape, dtype)

    outs = [
        (arr(TOK, D), hbm), (arr(8, 128, dtype=F32), vmem),
        (arr(D, 3 * D), hbm), (arr(D, D), hbm), (arr(D, FF), hbm),
        (arr(TOK, 3 * D), hbm), (arr(SEQ_DEV * PAIRS, 256, 128), hbm), (arr(2, TOK, D), hbm), (arr(2, TOK, D), hbm),
        (arr(TOK, D), hbm), (arr(TOK, 128, dtype=F32), hbm), (arr(2, TOK, FF), hbm), (arr(TOK, FF), hbm), (arr(TOK, FF // 2), hbm),
        (arr(TOK, D, dtype=F32), hbm), (arr(2, TOK, D), hbm), (arr(2, TOK, D), hbm),
        (arr(9, 128, 128), vmem), (arr(4, 8, D, dtype=F32), vmem),
    ]
    dma = pltpu.SemaphoreType.DMA
    scratch = [
        pltpu.VMEM((2, 4, 4, 32, 128), BF), pltpu.VMEM((2, 4, 4, 24, 3 * D), BF), pltpu.VMEM((2, 4, 4, 24, D), BF),
        pltpu.VMEM((2, 4, 4, 24, FF), BF), pltpu.VMEM((2, 4, 4, 96, D), BF),
        pltpu.VMEM((D, 3 * D), BF), pltpu.VMEM((D, D), BF), pltpu.VMEM((D, FF), BF),
        pltpu.VMEM((TOK, D), BF), pltpu.VMEM((TOK, D), BF), pltpu.VMEM((TOK, 3 * D), BF),
        pltpu.VMEM((SEQ_DEV * PAIRS, 256, 128), BF), pltpu.VMEM((TOK, D), BF), pltpu.VMEM((TOK, D), BF),
        pltpu.VMEM((TOK, D), BF), pltpu.VMEM((TOK, 128), F32), pltpu.VMEM((TOK, FF), BF), pltpu.VMEM((TOK, FF), BF),
        pltpu.VMEM((TOK, D), F32), pltpu.VMEM((TOK, 128), F32), pltpu.VMEM((TOK, D), BF), pltpu.VMEM((TOK, D), BF),
        pltpu.VMEM((TOK, 128), F32), pltpu.VMEM((TOK, 128), BF), pltpu.VMEM((D, 128), BF),
        pltpu.VMEM((128, 128), F32), pltpu.VMEM((128, 128), F32),
        pltpu.VMEM((TOK, 128), F32), pltpu.VMEM((8, 128), F32), pltpu.VMEM((8, 128), F32),
        dma((count * 3,)), dma((count * EVENTS,)), dma((2 * n,)), dma((2 * n,)),
        dma((2,)), dma((26,)), dma((13,)), dma((13,)),
    ]
    return pl.pallas_call(
        forward_kernel,
        out_shape=[o for o, _ in outs],
        in_specs=[hbm, hbm, pl.BlockSpec(memory_space=pltpu.SMEM), vmem] + [hbm] * n,
        out_specs=[s for _, s in outs],
        scratch_shapes=scratch,
        compiler_params=pltpu.CompilerParams(collective_id=0, has_side_effects=True, vmem_limit_bytes=VMEM),
        cost_estimate=pl.CostEstimate(flops=12 * 10**9, bytes_accessed=60 * 10**6, transcendentals=4 * 10**6),
        name="forward",
    )(tokens, cot, exit_layer, cot_logits, *shards)


def landing(order):
    out, left = [], ["x", "z", "y"]
    for axis in reversed(order):
        left = [a for a in left if a != axis]
        out.append((1 if axis == "x" else 3, tuple(SIZE[a] for a in left)))
    return out


def add_box(place, held, left, fixed, terms):
    dims = tuple(SIZE[a] for a in left)

    def step(i):
        index = []
        for d in reversed(dims):
            index.append(i % d)
            i = i // d
        index = tuple(reversed(index))
        at = dict(zip(left, index))
        b = tuple(fixed[a] if a in fixed else at[a] if a in at else place.at(a) for a in ("x", "z", "y"))
        total = held[b]
        for t in terms:
            total = total + t[index]
        held[b] = total

    if dims:
        count = 1
        for d in dims:
            count *= d
        loop(count, step)
    else:
        step(0)


def reduce_unit(place, lane, side, number, core, order, held, lands, last, result, twin, put):
    way = 1 if core == 0 else -1
    left, e = ["x", "z", "y"], 0
    for axis, bufs in zip(reversed(order), lands):
        left = [a for a in left if a != axis]
        ahead, back = place.near(axis, way), place.near(axis, -way)
        mine = {axis: place.at(axis)}
        if not left:
            for n, (step, to) in enumerate(((way, ahead), (-way, back), (2, place.near(axis, 2)))):
                lane.go(e + n, held.at[place.box(left, **{axis: place.at(axis, step)})], bufs[n], to)
            yield
            for n in range(3):
                lane.landed(e + n, bufs[n], ahead)
            add_box(place, held, left, mine, bufs)
            e += 3
        elif axis == "x":
            lane.go(e, held.at[place.box(left, x=place.at("x", 1))], bufs[0], ahead)
            yield
            lane.landed(e, bufs[0], ahead)
            add_box(place, held, left, mine, [bufs[0]])
            e += 1
        else:
            lane.go(e, held.at[place.box(left, **{axis: place.at(axis, 2)})], bufs[0], ahead)
            lane.go(e + 1, held.at[place.box(left, **{axis: place.at(axis, -way)})], bufs[1], back)
            yield
            lane.landed(e, bufs[0], ahead)
            onward = {axis: place.at(axis, way)}
            add_box(place, held, left, onward, [bufs[0]])
            lane.go(e + 2, held.at[place.box(left, **onward)], bufs[2], ahead)
            yield
            lane.landed(e + 1, bufs[1], ahead)
            lane.landed(e + 2, bufs[2], ahead)
            add_box(place, held, left, mine, [bufs[1], bufs[2]])
            e += 3
    own = place.box(())
    lane.go(e, held.at[own], last, place.near("x", 2))
    yield
    lane.landed(e, last, place.near("x", 2))
    total = held[own] + last[...]
    result[...] = total
    side.go(number, result, twin, place.sibling)
    put[0][...] = total.astype(F32)
    yield
    side.landed(number, twin, place.sibling)
    put[1][...] = twin[...].astype(F32)


STEPS = 7
FIRST = (QKV, OUT, SMALL, DOWN, UP)
PIECES = [(i, k) for i in (DOWN, UP, OUT, QKV, SMALL) for k in range(3) if i != SMALL or k == 1]


def piece_shape(i):
    return {SMALL: (16, 128), QKV: (24, 384), OUT: (24, 128), UP: (24, 512), DOWN: (96, 128)}[i]


def reduce_scratch():
    out = []
    for i, k in PIECES:
        shape = piece_shape(i)
        out.append(pltpu.VMEM((2, 4, 4) + shape, BF))
        for copies, dims in landing(ORDERS[0][k]):
            out.extend([pltpu.VMEM(dims + shape, BF)] * copies)
        out.extend([pltpu.VMEM(shape, BF)] * 3)
    return out


class Reduce:
    def __init__(self, place, scratch, outs, send, recv, ssend, srecv):
        self.place = place
        self.lanes = [[Lane(send, recv, 3 * n, SUMS * n) for n in range(len(PIECES))] for _ in range(2)]
        self.sides = [Wire(ssend, srecv) for _ in range(2)]
        self.held, self.units, self.live, self.done = {}, [{}, {}], [], {}
        for n, (i, k) in enumerate(PIECES):
            held = scratch.pop(0)
            lands = [[scratch.pop(0) for _ in range(copies)] for copies, _ in landing(ORDERS[0][k])]
            last, result, twin = (scratch.pop(0) for _ in range(3))
            self.held[i, k] = held
            for core in range(2):
                kind = "small" if i == SMALL else "cols"
                width = outs[i].shape[-1]
                put = (outs[i].at[piece(kind, core, k, width)], outs[i].at[piece(kind, 1 - core, k, width)])
                self.units[core][i, k] = reduce_unit(
                    place, self.lanes[core][n], self.sides[core], n, core, ORDERS[core][k],
                    held, lands, last, result, twin, put)

    def advance(self, pieces):
        def one(core):
            for p in pieces:
                next(self.units[core][p], None)

        self.place.on_core(one)

    def start(self, *pieces):
        self.advance(pieces)
        for p in pieces:
            self.live.append(p)
            self.done[p] = 1

    def pump(self, *arrays):
        todo = sorted((p for p in self.live if not arrays or p[0] in arrays), key=lambda p: FIRST.index(p[0]))
        self.advance(todo)
        for p in todo:
            self.done[p] += 1
            if self.done[p] == STEPS:
                self.live.remove(p)

    def end(self):
        while self.live:
            self.pump()

        def one(core):
            for lane in self.lanes[core]:
                lane.sent()
            self.sides[core].sent()

        self.place.on_core(one)


def lay(held, value):
    for i in range(16):
        x, z, y = at_block(i)
        for j in range(2):
            held[x, z, 2 * y + j] = value[48 * i + 24 * j:48 * i + 24 * j + 24].astype(BF)


def backward_kernel(tokens2, merged_h, probs_h, ctx2_h, normed2_h, n1_h, r1_h, active2_h, gup_h, gup_s_h, gsec_h, dlow2_h,
                    wqkv_h, wout_h, wup_h, small, rows,
                    o_gtok, o_qkv, o_out, o_up, o_down, o_small,
                    tok2, act2, gup, normed2, ctx2, dlow2, n1, r1, gsec, attn, attn_s, gctx, gup_s, gm_s, probs,
                    w_big, w_out, packed, packed_s, g_row, *rest):
    scratch = list(rest[:-8])
    send, recv, ssend, srecv, insem, wsem, xsend, xrecv = rest[-8:]
    place = Place()
    core = place.core
    loads = {}

    def load(name, src, dst):
        c = pltpu.make_async_copy(src, dst, insem.at[len(loads)])
        c.start()
        loads[name] = c

    def ready(*names):
        for name in names:
            loads[name].wait()

    def w_load(i, src, dst):
        c = pltpu.make_async_copy(src, dst, wsem.at[i])
        return c

    def active_load(j):
        return pltpu.make_async_copy(active2_h.at[:, :, span(j, D)], act2.at[:, :, span(j, D)], insem.at[14 + j])

    load("dlow", dlow2_h, dlow2)
    for j in range(4):
        active_load(j).start()
    greet(place)
    red = Reduce(place, scratch, {QKV: o_qkv, OUT: o_out, UP: o_up, DOWN: o_down, SMALL: o_small},
                 send, recv, ssend, srecv)
    cross = Wire(xsend, xrecv)

    def mine(size):
        return pl.ds(pl.multiple_of(core * size, 128), size)

    def other(size):
        return pl.ds(pl.multiple_of((1 - core) * size, 128), size)

    load("gup", gup_h, gup)
    load("gup_s", gup_s_h, gup_s)
    load("normed", normed2_h, normed2)

    def up_load(j, slot):
        return w_load(slot, wup_h.at[span(j, 256)], w_big.at[slot])

    def qkv_load(j, slot):
        return w_load(slot, wqkv_h.at[span(j, 256)], w_big.at[slot, :, pl.ds(0, 3 * D)])

    ready("dlow")

    def down(j):
        active_load(j).wait()
        left = dlow2[:, :, mine(384)].reshape(2 * TOK, 384)
        g = dot(left, act2[:, :, span(j, D)].reshape(2 * TOK, D), ((0,), (0,))).T.astype(BF)
        for k in range(3):
            red.held[DOWN, k][j // 2, pl.ds(lax.rem(j, 2) * 2, 2)] = g[:, 128 * k:128 * k + 128].reshape(2, 4, 96, 128)

    loop(4, down)
    red.start((DOWN, 0), (DOWN, 1), (DOWN, 2))
    for j in range(2):
        up_load(j, j).start()
    load("gsec", gsec_h, gsec)
    load("n1", n1_h, n1)
    load("r1", r1_h, r1)
    load("wout", wout_h, w_out)
    load("merged", merged_h, act2.at[0, :, pl.ds(0, 3 * D)])
    merged = act2.at[0, :, pl.ds(0, 3 * D)]
    load("probs", probs_h, probs)
    load("ctx", ctx2_h, ctx2)
    load("tokens", tokens2, tok2)
    ready("gup", "gup_s", "normed")
    for k in range(3):
        own = gup[:, pl.ds(pl.multiple_of(core * (FF // 2) + 512 * k, 128), 512)]

        def grad_up():
            lay(red.held[UP, k], dot(normed2[0], own, ((0,), (0,))) + dot(normed2[1], gup_s[:, 512 * k:512 * k + 512], ((0,), (0,))))

        once(grad_up)
        red.start((UP, k))
    ready("gsec", "n1", "r1")

    def g_normed(j):
        slot = lax.rem(j, 2)
        up_load(j, slot).wait()
        c = span(j, 256)
        gsec[:, c] = gsec[:, c] + dot(gup[...], w_big[slot], ((1,), (1,)))
        pl.when(j < 1)(lambda: up_load(j + 2, slot).start())

    loop(3, g_normed)
    for j in range(2):
        qkv_load(j, 1 - j).start()
    gain1 = rows[0, pl.ds(0, 1), :]

    def norm1(j):
        r = span(j, 384)
        g, n = gsec[r, :], n1[r, :].astype(F32)
        part = jnp.sum(g * n, axis=0, keepdims=True)
        g_row[0:1] = jnp.where(j == 0, part, part + g_row[0:1])
        g = norm_back(g, gain1, n, r1[r, pl.ds(0, 1)])
        gsec[r, :] = g
        attn[r, :] = g.astype(BF)

    loop(2, norm1)
    cross.go(1, attn.at[:, other(384)], attn_s, place.sibling)
    ready("wout", "ctx")

    def context(j):
        r = span(j, 384)
        gctx[r, :] = dot(attn[r, :], w_out[...], ((1,), (1,))).astype(BF)

    loop(2, context)

    ready("merged", "probs")

    low_half, high_half = halves()
    la, lb = low_half.astype(BF), high_half.astype(BF)
    qa, qb = (low_half * 0.125).astype(BF), (high_half * 0.125).astype(BF)

    def attend_back(s):
        r = span(s, SEQ)
        at = [[pl.ds(768 * a + 128 * p, 128) for a in range(3)] for p in range(PAIRS)]
        d2, q2, gp, gs = [], [], [], []
        for p in range(PAIRS):
            q, d = merged[r, at[p][0]], gctx[r, pl.ds(128 * p, 128)]
            d2.append(jnp.concatenate([d * la, d * lb], axis=0))
            q2.append(jnp.concatenate([q * qa, q * qb], axis=0))
            gp.append(dot(d2[p], merged[r, at[p][2]], ((1,), (1,))))
        for p in range(PAIRS):
            pr = probs[s * PAIRS + p]
            merged[r, at[p][2]] = dot(pr, d2[p], ((0,), (0,))).astype(BF)
            pf = pr.astype(F32)
            t = pf * gp[p]
            gs.append((t - pf * jnp.sum(t, axis=-1, keepdims=True)).astype(BF))
        for p in range(PAIRS):
            both = dot(gs[p], merged[r, at[p][1]])
            merged[r, at[p][0]] = ((both[:SEQ] * low_half + both[SEQ:] * high_half) * 0.125).astype(BF)
            merged[r, at[p][1]] = dot(gs[p], q2[p], ((0,), (0,))).astype(BF)

    def gm_part(part):
        r = pl.ds(256 * part, 256)
        return pltpu.make_async_remote_copy(
            src_ref=act2.at[0, r, other(3 * D // 2)], dst_ref=gm_s.at[r], send_sem=xsend.at[4 + part],
            recv_sem=xrecv.at[4 + part], device_id=place.sibling, device_id_type=MESH)

    for part in range(3):

        def attend_part(s):
            attend_back(s + 2 * part)

        loop(2, attend_part)
        if part == 0:
            red.pump(DOWN)
        if part == 2:
            red.pump(DOWN, UP)
        gm_part(part).start()
    ready("tokens")

    def g_tokens(j):
        slot = lax.rem(j + 1, 2)
        qkv_load(j, slot).wait()
        c = span(j, 256)
        gsec[:, c] = gsec[:, c] + dot(merged[...], w_big[slot, :, :3 * D], ((1,), (1,)))
        pl.when(j < 1)(lambda: qkv_load(j + 2, slot).start())

    lax.fori_loop(0, 1, lambda j, c: (g_tokens(j), c)[1], 0)
    for part in range(3):
        gm_part(part).wait_recv()
    for k in range(3):
        own = merged[:, pl.ds(pl.multiple_of(core * (3 * D // 2) + 384 * k, 128), 384)]

        def grad_qkv():
            lay(red.held[QKV, k], dot(tok2[0], own, ((0,), (0,))) + dot(tok2[1], gm_s[:, 384 * k:384 * k + 384], ((0,), (0,))))

        once(grad_qkv)
        red.start((QKV, k))
    def pack_small():
        p_proj, p_hid, p_cls, p_misc = picks()
        pack = dot(p_proj, small[3:9].reshape(D, 128), ((0,), (0,)))
        pack = pack + dot(p_hid, small[0], ((0,), (0,)))
        lane = iota((128, 128), 1)
        pack = pack + dot(p_cls, jnp.where(lane < 14, small[1].astype(F32), 0.0).astype(BF), ((0,), (0,)))
        values = (g_row[0:1], rows[3, pl.ds(0, 1), :], small[2, pl.ds(0, 1), :].astype(F32))
        misc = jnp.zeros((32, 128), F32)
        for (name, first, size, per), value in zip(ROWS, values):
            tile, held = spread(first, size, per)
            misc = misc + dot(jnp.where(held, value, 0.0).astype(BF), tile, ((1,), (1,)))
        packed[...] = (pack + dot(p_misc, misc.astype(BF), ((0,), (0,)))).astype(BF).reshape(2, 4, 4, 32, 128)

    once(pack_small)
    place.on_core(lambda c: cross.copy(3, packed.at[:, :, :, pl.ds(16 - 16 * c, 16)], packed_s, place.sibling).start())

    cross.landed(1, attn_s, place.sibling)

    def grad_out():
        g = dot(ctx2[0], attn[:, mine(384)], ((0,), (0,))) + dot(ctx2[1], attn_s[...], ((0,), (0,)))
        for k in range(3):
            lay(red.held[OUT, k], g[:, 128 * k:128 * k + 128])

    once(grad_out)
    cross.landed(3, packed_s, place.sibling)

    def small_half(c):
        red.held[SMALL, 1][...] = packed[:, :, :, 16 * c:16 * c + 16, :] + packed_s[...]

    place.on_core(small_half)
    red.start((OUT, 0), (OUT, 1), (OUT, 2), (SMALL, 1))
    red.pump(DOWN, UP)
    lax.fori_loop(1, 3, lambda j, c: (g_tokens(j), c)[1], 0)
    red.pump()
    store = pltpu.make_async_copy(gsec, o_gtok, insem.at[len(loads)])
    store.start()
    red.end()
    cross.sent()
    for part in range(3):
        gm_part(part).wait_send()
    place.on_core(lambda c: cross.copy(3, packed.at[:, :, :, pl.ds(16 - 16 * c, 16)], packed_s, place.sibling).wait_send())
    store.wait()


def backward(*args):
    hbm, vmem = pl.BlockSpec(memory_space=pl.ANY), pl.BlockSpec(memory_space=pltpu.VMEM)

    def arr(*shape, dtype=F32):
        return jax.ShapeDtypeStruct(shape, dtype)

    dma = pltpu.SemaphoreType.DMA
    count = len(PIECES)
    scratch = [
        pltpu.VMEM((2, TOK, D), BF), pltpu.VMEM((2, TOK, FF), BF), pltpu.VMEM((TOK, FF), BF),
        pltpu.VMEM((2, TOK, D), BF), pltpu.VMEM((2, TOK, D), BF), pltpu.VMEM((2, TOK, D), BF),
        pltpu.VMEM((TOK, D), BF), pltpu.VMEM((TOK, 128), F32), pltpu.VMEM((TOK, D), F32),
        pltpu.VMEM((TOK, D), BF), pltpu.VMEM((TOK, D // 2), BF), pltpu.VMEM((TOK, D), BF),
        pltpu.VMEM((TOK, FF // 2), BF), pltpu.VMEM((TOK, 3 * D // 2), BF),
        pltpu.VMEM((SEQ_DEV * PAIRS, 256, 128), BF),
        pltpu.VMEM((2, 256, FF), BF), pltpu.VMEM((D, D), BF),
        pltpu.VMEM((2, 4, 4, 32, 128), BF), pltpu.VMEM((2, 4, 4, 16, 128), BF), pltpu.VMEM((8, D), F32),
    ] + reduce_scratch() + [
        dma((count * 3,)), dma((count * SUMS,)), dma((count,)), dma((count,)), dma((18,)), dma((2,)), dma((7,)), dma((7,)),
    ]
    return pl.pallas_call(
        backward_kernel,
        out_shape=[arr(TOK, D), arr(24, 3 * D), arr(24, D), arr(24, FF), arr(96, D), arr(32, 128)],
        in_specs=[hbm] * 15 + [vmem] * 2,
        out_specs=[hbm] + [vmem] * 5,
        scratch_shapes=scratch,
        compiler_params=pltpu.CompilerParams(collective_id=1, has_side_effects=True, vmem_limit_bytes=VMEM),
        cost_estimate=pl.CostEstimate(flops=24 * 10**9, bytes_accessed=60 * 10**6, transcendentals=0),
        name="backward",
    )(*args)


def finish_kernel(act, logits, gtok, qkv, out, up, down, small, *rest):
    o_act, o_logits, o_gtok, o_qkv, o_out, o_g1, o_up, o_down, o_g2, o_proj, o_pool, o_hid, o_cls = rest[:13]
    h_gtok, h_act, h_qkv, h_up, h_down, h_out, sems = rest[13:]
    moves = [(gtok, h_gtok, o_gtok, r) for r in range(3)] + [(act, h_act, o_act, r) for r in range(3)]
    moves += [(qkv, h_qkv, o_qkv, None), (up, h_up, o_up, None), (down, h_down, o_down, None), (out, h_out, o_out, None)]

    def at(ref, r):
        return ref if r is None else ref.at[pl.ds(256 * r, 256)]

    come = [pltpu.make_async_copy(at(a, r), at(h, r), sems.at[n]) for n, (a, h, o, r) in enumerate(moves)]
    go = [pltpu.make_async_copy(at(h, r), at(o, r), sems.at[len(moves) + n]) for n, (a, h, o, r) in enumerate(moves)]
    for c in come:
        c.start()
    o_logits[...] = logits[0:SEQ_DEV, 0:14]
    o_proj[...] = small[0:24]
    o_hid[...] = small[24:28]
    o_cls[...] = small[28:32, 0:14]
    o_g1[...] = small[28:29, 16:40]
    o_g2[...] = small[28:29, 40:64]
    o_pool[...] = small[28:29, 64:68]
    for c, d in zip(come, go):
        c.wait()
        d.start()
    for d in go:
        d.wait()


def finish(*args):
    hbm, vmem = pl.BlockSpec(memory_space=pl.ANY), pl.BlockSpec(memory_space=pltpu.VMEM)
    shapes = ((TOK, D), (SEQ_DEV, 14), (TOK, D), (24, 3 * D), (24, D), (1, 24), (24, FF), (96, D), (1, 24), (24, 128),
              (1, 4), (4, 128), (4, 14))
    moved = (0, 2, 3, 4, 6, 7)
    return pl.pallas_call(
        finish_kernel,
        out_shape=[jax.ShapeDtypeStruct(s, F32 if n else BF) for n, s in enumerate(shapes)],
        in_specs=[hbm, vmem, hbm, hbm, hbm, hbm, hbm, vmem],
        out_specs=[hbm if n in moved else vmem for n in range(len(shapes))],
        scratch_shapes=[pltpu.VMEM((TOK, D), F32), pltpu.VMEM((TOK, D), BF), pltpu.VMEM((24, 3 * D), F32),
                        pltpu.VMEM((24, FF), F32), pltpu.VMEM((96, D), F32), pltpu.VMEM((24, D), F32),
                        pltpu.SemaphoreType.DMA((20,))],
        compiler_params=pltpu.CompilerParams(vmem_limit_bytes=VMEM),
        name="finish",
    )(*args)


def local(tokens, exit_layer, w_qkv, w_out, gain_attn, w_up, w_down, gain_ffn, w_proj, pool_query, w_hid, w_cls,
          cot_out, cot_logits):
    parts = ((w_proj, 0, 0), (w_hid, 24, 0), (w_cls, 28, 0), (gain_attn[None], 28, 16), (gain_ffn[None], 28, 40),
             (pool_query[None], 28, 64))
    small = sum(jnp.pad(p, ((r, 32 - r - p.shape[0]), (c, 128 - c - p.shape[1]))) for p, r, c in parts)
    (act, logits, f_qkv, f_out, f_up, merged, probs, ctx, normed, n1, r1, active, gup, gup_s, gsec, dlow, tokens2,
     small_g, rows) = forward(tokens, cot_out, exit_layer, cot_logits, (small, w_qkv, w_out, w_up, w_down))
    g_tok, g_qkv, g_out, g_up, g_down, g_small = backward(
        tokens2, merged, probs, ctx, normed, n1, r1, active, gup, gup_s, gsec, dlow, f_qkv, f_out, f_up, small_g, rows)
    outs = list(finish(act, logits, g_tok, g_qkv, g_out, g_up, g_down, g_small))
    for n in (5, 8, 10):
        outs[n] = outs[n].reshape(-1)
    return tuple(outs)


def solution(mesh):
    both, wide = P(("wide", "grp"), None), P("wide", None)
    in_specs = (both, P(("wide", "grp")), wide, wide, P("wide"), wide, wide, P("wide"), wide, P("wide"), wide, wide,
                both, both)
    out_specs = (both, both, both, wide, wide, P("wide"), wide, wide, P("wide"), wide, P("wide"), wide, wide)
    return jax.shard_map(local, mesh=mesh, in_specs=in_specs, out_specs=out_specs, check_vma=False)
```

```python
import functools
import jax
import jax.numpy as jnp
from jax import lax
from jax.sharding import PartitionSpec as P
from jax.experimental import pallas as pl
from jax.experimental.pallas import tpu as pltpu

D = 768
FF = 3072
TOK = 768
SEQ_DEV = 6
PAIRS = 6
SEQ = 128
LAYER = 3
MESH = pl.DeviceIdType.MESH
BF = jnp.bfloat16
F32 = jnp.float32
SIZE = {"x": 2, "z": 4, "y": 4}
ORDERS = (
    (("y", "z", "x"), ("z", "x", "y"), ("y", "x", "z")),
    (("z", "y", "x"), ("z", "x", "y"), ("y", "x", "z")),
)
EVENTS = 7
SUMS = 8
VMEM = 62 * 2**20


class Place:
    def __init__(self):
        wide, grp = lax.axis_index("wide"), lax.axis_index("grp")
        xl, z, y = wide // 16, (wide // 4) % 4, wide % 4
        x = (grp // 2) * 2 + xl
        self.core = grp % 2
        self.places = {("x", 0): xl, ("x", 1): 1 - xl}
        for axis, here in (("z", z), ("y", y)):
            for step in range(4):
                self.places[axis, step] = (here + step) % 4
        self.ids = {}
        for step in (1, 2, 3):
            far = (x + step) % 4
            self.ids["x", step] = ((far % 2) * 16 + z * 4 + y, (far // 2) * 2 + self.core)
            self.ids["y", step] = (xl * 16 + z * 4 + self.places["y", step], grp)
            self.ids["z", step] = (xl * 16 + self.places["z", step] * 4 + y, grp)
        self.sibling = (wide, grp + 1 - 2 * self.core)

    def near(self, axis, step):
        return self.ids[axis, step % 4]

    def at(self, axis, step=0):
        return self.places[axis, step % SIZE[axis]]

    def box(self, have, **fixed):
        out = []
        for axis in ("x", "z", "y"):
            if axis in fixed:
                out.append(fixed[axis])
            elif axis in have:
                out.append(slice(None))
            else:
                out.append(self.at(axis))
        return tuple(out)

    def on_core(self, step):
        for core in (0, 1):
            pl.when(self.core == core)(functools.partial(step, core))


def greet(place):
    barrier = pltpu.get_barrier_semaphore()
    ids = [place.near(a, s) for a in ("x", "y", "z") for s in (1, -1, 2)] + [place.sibling]
    for i in ids:
        pl.semaphore_signal(barrier, inc=1, device_id=i, device_id_type=MESH)
    pl.semaphore_wait(barrier, len(ids))


class Wire:
    def __init__(self, send, recv):
        self.send, self.recv = send, recv
        self.started = []

    def copy(self, n, src, dst, to):
        return pltpu.make_async_remote_copy(
            src_ref=src, dst_ref=dst, send_sem=self.send.at[n], recv_sem=self.recv.at[n],
            device_id=to, device_id_type=MESH,
        )

    def go(self, n, src, dst, to):
        self.copy(n, src, dst, to).start()
        self.started.append((n, src, dst, to))

    def landed(self, n, dst, to):
        self.copy(n, dst, dst, to).wait_recv()

    def sent(self):
        for c in self.started:
            self.copy(*c).wait_send()


def piece(kind, core, k, width):
    if kind == "cols":
        return (slice(None), pl.ds((core * 3 + k) * (width // 6), width // 6))
    return (pl.ds(core * 16, 16), slice(None)) if k == 1 else None


class Lane:
    def __init__(self, send, recv, first_send, first_recv):
        self.send, self.recv, self.first_send, self.first_recv = send, recv, first_send, first_recv
        self.out, self.count = {}, 0

    def copy(self, slot, e, src, dst, to):
        return pltpu.make_async_remote_copy(
            src_ref=src, dst_ref=dst, send_sem=self.send.at[self.first_send + slot],
            recv_sem=self.recv.at[self.first_recv + e], device_id=to, device_id_type=MESH,
        )

    def go(self, e, src, dst, to):
        slot = self.count % 3
        self.count += 1
        if slot in self.out:
            self.copy(slot, *self.out[slot]).wait_send()
        self.copy(slot, e, src, dst, to).start()
        self.out[slot] = (e, src, dst, to)

    def landed(self, e, dst, to):
        self.copy(0, e, dst, dst, to).wait_recv()

    def sent(self):
        for slot, c in self.out.items():
            self.copy(slot, *c).wait_send()


def gather_unit(place, lane, sib, core, order, own, full):
    way = 1 if core == 0 else -1
    have, e = [], 0
    for axis in order:
        mine = place.box(have)
        src = full(mine) if have else own
        ahead, back, far = place.near(axis, way), place.near(axis, -way), place.near(axis, 2)
        last = axis == order[2]
        if axis == "x":
            lane.go(e, src, full(mine), ahead)
            yield
            got = place.box(have, x=place.at("x", 1))
            lane.landed(e, full(got), ahead)
            if last:
                sib(got)
            e += 1
        elif not have:
            for n, to in enumerate((ahead, back, far)):
                lane.go(e + n, src, full(mine), to)
            yield
            for n, step in enumerate((-way, way, 2)):
                lane.landed(e + n, full(place.box(have, **{axis: place.at(axis, step)})), ahead)
            e += 3
        else:
            lane.go(e, src, full(mine), ahead)
            lane.go(e + 1, src, full(mine), back)
            yield
            got = place.box(have, **{axis: place.at(axis, -way)})
            lane.landed(e, full(got), ahead)
            lane.go(e + 2, full(got), full(got), ahead)
            if last:
                sib(got)
            yield
            for late, step in ((1, way), (2, 2)):
                got = place.box(have, **{axis: place.at(axis, step)})
                lane.landed(e + late, full(got), ahead)
                if last:
                    sib(got)
            e += 3
        have.append(axis)
        if axis == order[1]:
            sib(place.box(have))


class Gather:
    def __init__(self, place, kinds, shards, fulls, send, recv, side, keep):
        self.place, self.kinds, self.shards, self.fulls = place, kinds, shards, fulls
        self.side, self.keep = side, keep
        n = len(kinds)
        self.lanes = [[], []]
        self.units = [[[] for _ in range(n)] for _ in range(2)]
        for core in range(2):
            for i in range(n):
                for k in range(3):
                    tail = piece(kinds[i], core, k, shards[i].shape[-1])
                    if tail is None:
                        continue
                    at = len(self.lanes[core])
                    lane = Lane(send, recv, at * 3, at * EVENTS)
                    self.lanes[core].append(lane)
                    full = functools.partial(self.part, i, tail)
                    sib = functools.partial(self.pass_on, i, full)
                    self.units[core][i].append(gather_unit(
                        place, lane, sib, core, ORDERS[core][k], shards[i].at[tail], full))

    def part(self, i, tail, box):
        return self.fulls[i].at[box + tail]

    def half(self, i, core):
        size = self.shards[i].shape[-1] // 2
        if self.kinds[i] == "cols":
            return (slice(None), pl.ds(core * size, size))
        return (pl.ds(core * 16, 16), slice(None))

    def to_side(self, sems, n, src, dst):
        return pltpu.make_async_remote_copy(
            src_ref=src, dst_ref=dst, send_sem=sems.at[n], recv_sem=sems.at[len(self.kinds) + n],
            device_id=self.place.sibling, device_id_type=MESH)

    def pass_on(self, i, full, box):
        self.to_side(self.side, i, full(box), full(box)).start()

    def own(self, i, core):
        half = self.half(i, 1 - core)
        return self.to_side(self.keep, i, self.shards[i].at[half], self.fulls[i].at[self.place.box(()) + half])

    def own_start(self):
        self.place.on_core(lambda core: [self.own(i, core).start() for i in range(len(self.kinds))] and None)

    def own_landed(self):
        def one(core):
            for i in range(len(self.kinds)):
                self.own(i, core).wait_send()
                self.own(i, 1 - core).wait_recv()

        self.place.on_core(one)

    def step(self, *arrays, back=False):
        def one(core):
            for i in arrays:
                units = self.units[core][i]
                for u in units[1:] + units[:1] if back else units:
                    next(u, None)

        self.place.on_core(one)

    def everything(self, i, core):
        part = self.fulls[i].at[(slice(None),) * 3 + self.half(i, core)]
        return self.to_side(self.side, i, part, part)

    def whole(self, *arrays):
        def one(core):
            for i in arrays:
                self.everything(i, 1 - core).wait_recv()

        self.place.on_core(one)

    def end(self):
        def one(core):
            for lane in self.lanes[core]:
                lane.sent()
            for i in range(len(self.kinds)):
                self.everything(i, core).wait_send()

        self.place.on_core(one)


def dot(a, b, dims=((1,), (0,))):
    return lax.dot_general(a, b, (dims, ((), ())), preferred_element_type=F32)


def exact(a, b, dims=((1,), (0,))):
    return lax.dot_general(a, b, (dims, ((), ())), precision=lax.Precision.HIGHEST, preferred_element_type=F32)


def iota(shape, dim):
    return lax.broadcasted_iota(jnp.int32, shape, dim)


def over24(i):
    return (i * 2731) >> 16


def ones_where(hit):
    return jnp.where(hit, 1.0, 0.0).astype(BF)


def picks():
    i, j = iota((768, 1024), 0), iota((768, 1024), 1)
    proj = ones_where(j == i + 8 * over24(i))
    i, j = iota((128, 1024), 0), iota((128, 1024), 1)
    at = 32 * (i >> 2) + (i & 3)
    hid, cls = ones_where(j == at + 24), ones_where(j == at + 28)
    i, j = iota((32, 1024), 0), iota((32, 1024), 1)
    misc = ones_where(j == 32 * i + 28)
    return proj, hid, cls, misc


def spread(first, size, per):
    i, l = iota((128, size), 0), iota((128, size), 1)
    block = over24(l) if per == 24 else l >> 2
    w, m = iota((32, size), 0), iota((32, size), 1)
    held = over24(m) if per == 24 else m >> 2
    return ones_where(i - first == l - per * block), held == w


ROWS = (("gain_attn", 16, 768, 24), ("gain_ffn", 40, 768, 24), ("pool", 64, 128, 4))


def normalise(h):
    centre = h - jnp.mean(h, axis=-1, keepdims=True)
    r = lax.rsqrt(jnp.mean(centre * centre, axis=-1, keepdims=True) + 1e-06)
    return centre * r, r


def norm_back(g, gain, n, r):
    gn = g * gain
    return r * (gn - jnp.mean(gn, axis=-1, keepdims=True) - n * jnp.mean(gn * n, axis=-1, keepdims=True))


TANH_A = 0.7978845608028654
TANH_B = 0.7978845608028654 * 0.044715


def gelu(u):
    u2 = u * u
    h = 0.5 + 0.5 * jnp.tanh(u * (TANH_A + TANH_B * u2))
    y = u * h
    return y, h + y * (1.0 - h) * (2.0 * TANH_A + 6.0 * TANH_B * u2)


def at_block(i):
    return i // 8, (i // 2) % 4, i % 2


def join(blocks, whole):
    def one(i, carry):
        x, z, y = at_block(i)
        pair = jnp.concatenate([blocks[x, z, 2 * y], blocks[x, z, 2 * y + 1]], axis=0)
        whole[pl.ds(pl.multiple_of(i * 48, 48), 48), :] = pair
        return carry

    lax.fori_loop(0, 16, one, 0)


def loop(n, step):
    def one(i, carry):
        step(i)
        return carry

    lax.fori_loop(0, n, one, 0)


def once(step):
    step()


def span(i, size):
    return pl.ds(pl.multiple_of(i * size, size), size)


def halves():
    lane = iota((1, 128), 1)
    return jnp.where(lane < 64, 1.0, 0.0), jnp.where(lane < 64, 0.0, 1.0)


KINDS = ("small", "cols", "cols", "cols", "cols")
SMALL, QKV, OUT, UP, DOWN = range(5)


def forward_kernel(tokens, cot, exit_layer, cot_logits, i_proj, i_hid, i_cls, i_gain1, i_gain2, i_pool, s_qkv, s_out, s_up, s_down,
                   o_act, o_logits, o_wqkv, o_wout, o_wup, o_merged, o_probs, o_ctx, o_normed, o_n1, o_r1,
                   o_active, o_gup, o_gup_s, o_gsec, o_dlow, o_tokens2, o_small, rows,
                   b_small, b_qkv, b_out, b_up, b_down, w_qkv, w_out, w_up, tok, cotv, merged, probs, ctx, normed, n1, r1,
                   active, dact, gsec, r2, dlow, out, projected, gproj, wproj, hid, cls,
                   alive, alive_seq, cotl, wide_small, s_small, send, recv, ssem, lsem, insem, outsem, xsend, xrecv):
    place = Place()
    loads = [pltpu.make_async_copy(tokens, tok, insem.at[0]), pltpu.make_async_copy(cot, cotv, insem.at[1])]
    for c in loads:
        c.start()
    wide_small[0:24] = i_proj[...].astype(F32)
    wide_small[24:28] = i_hid[...].astype(F32)
    line = [jnp.zeros((1, 16), F32)] + [i[...].astype(F32) for i in (i_gain1, i_gain2, i_pool)]
    wide_small[28:29] = jnp.concatenate(line + [jnp.zeros((1, 60), F32)], axis=1)
    wide_small[29:32] = jnp.zeros((3, 128), F32)
    wide_small[28:32, 0:14] = i_cls[...].astype(F32)
    s_small[...] = wide_small[...].astype(BF)
    greet(place)
    g = Gather(place, KINDS, (s_small, s_qkv, s_out, s_up, s_down), (b_small, b_qkv, b_out, b_up, b_down),
               send, recv, ssem, lsem)
    stores = []
    cross = Wire(xsend, xrecv)

    def keep(src, dst):
        c = pltpu.make_async_copy(src, dst, outsem.at[len(stores)])
        c.start()
        stores.append(c)

    def share(n, src, dst):
        keep(src, dst.at[0])
        cross.go(n, src, dst.at[1], place.sibling)

    g.step(QKV, SMALL)
    g.own_start()
    g.step(OUT, UP, DOWN)
    loads[0].wait()
    cotl[...] = jnp.zeros((8, 128), F32)
    cotl[0:SEQ_DEV, 0:14] = cot_logits[...]
    alive_seq[...] = jnp.zeros((8, 128), F32)
    for s in range(SEQ_DEV):
        stays = jnp.clip(exit_layer[s] - (LAYER - 1), 0, 1).astype(F32)
        alive[pl.ds(s * SEQ, SEQ), :] = jnp.full((SEQ, 128), stays)
        alive_seq[pl.ds(s, 1), :] = jnp.full((1, 128), stays)
    g.own_landed()
    g.step(QKV, SMALL)
    g.step(OUT, UP, DOWN)
    g.step(QKV, SMALL)
    g.step(QKV, SMALL)
    g.step(OUT, UP, DOWN)
    g.step(QKV, SMALL, back=True)
    g.whole(QKV, SMALL)
    join(b_qkv, w_qkv)

    def qkv(j):
        c = span(j, D)
        merged[:, c] = dot(tok[...], w_qkv[:, c]).astype(BF)

    loop(3, qkv)
    keep(w_qkv, o_wqkv)
    keep(merged, o_merged)
    g.step(OUT, UP)

    def small_weights():
        p_proj, p_hid, p_cls, p_misc = picks()
        pack = b_small[...].reshape(1024, 128)
        wproj[...] = dot(p_proj, pack).astype(BF)
        hid[...] = dot(p_hid, pack)
        cls[...] = jnp.where(iota((128, 128), 1) < 14, dot(p_cls, pack), 0.0)
        misc = dot(p_misc, pack).astype(BF)
        for n, (name, first, size, per) in enumerate(ROWS):
            tile, held = spread(first, size, per)
            row = jnp.sum(jnp.where(held, dot(misc, tile), 0.0), axis=0, keepdims=True)
            rows[n, :, pl.ds(0, size)] = jnp.broadcast_to(row, (8, size))

    once(small_weights)
    low_half, high_half = halves()

    qa, qb = (low_half * 0.125).astype(BF), (high_half * 0.125).astype(BF)

    def attend(s):
        r = span(s, SEQ)
        scores, prs = [], []
        for p in range(PAIRS):
            q, k = (merged[r, pl.ds(768 * a + 128 * p, 128)] for a in range(2))
            scores.append(dot(jnp.concatenate([q * qa, q * qb], axis=0), k, ((1,), (1,))))
        for p in range(PAIRS):
            e = jnp.exp(scores[p] - jnp.max(scores[p], axis=-1, keepdims=True))
            prs.append((e * (1.0 / jnp.sum(e, axis=-1, keepdims=True))).astype(BF))
            probs[s * PAIRS + p] = prs[p]
        for p in range(PAIRS):
            both = dot(prs[p], merged[r, pl.ds(1536 + 128 * p, 128)])
            ctx[r, pl.ds(128 * p, 128)] = (both[:SEQ] * low_half + both[SEQ:] * high_half).astype(BF)

    for part in range(3):

        def attend_two(s):
            attend(s + 2 * part)

        loop(2, attend_two)
        if part == 0:
            g.step(DOWN)
        elif part == 1:
            g.step(OUT, back=True)
        else:
            g.step(UP, back=True)
    keep(probs, o_probs)
    g.whole(OUT)
    join(b_out, w_out)
    gain1 = rows[0, pl.ds(0, 1), :]

    def mix(j):
        r = span(j, 384)
        n, inv = normalise(tok[r, :].astype(F32) + dot(ctx[r, :], w_out[...]))
        n1[r, :] = n.astype(BF)
        normed[r, :] = (n * gain1).astype(BF)
        r1[r, :] = jnp.broadcast_to(inv, (384, 128))

    loop(2, mix)
    g.whole(UP)
    share(2, normed, o_normed)
    share(1, ctx, o_ctx)
    share(0, tok, o_tokens2)
    keep(w_out, o_wout)
    keep(n1, o_n1)
    keep(r1, o_r1)
    join(b_up, w_up)

    def active_part(j):
        c = span(j, D)
        return pltpu.make_async_remote_copy(
            src_ref=active.at[:, c], dst_ref=o_active.at[1, :, c], send_sem=xsend.at[5 + j], recv_sem=xrecv.at[5 + j],
            device_id=place.sibling, device_id_type=MESH)

    def upward(j):
        c = span(j, D)
        y, dy = gelu(dot(normed[...], w_up[:, c]))
        active[:, c] = y.astype(BF)
        dact[:, c] = dy.astype(BF)
        active_part(j).start()

    def upward_late(j):
        upward(j + 2)

    loop(2, upward)
    g.step(DOWN, back=True)
    loop(2, upward_late)
    g.whole(DOWN)
    keep(active, o_active.at[0])
    keep(w_up, o_wup)
    loads[1].wait()
    gain2 = rows[1, pl.ds(0, 1), :]

    def downward(j):
        r = span(j, 384)
        second = normed[r, :].astype(F32) + dot(active[r, :], b_down[...].reshape(FF, D))
        n, inv = normalise(second)
        gsec[r, :] = n
        r2[r, :] = jnp.broadcast_to(inv, (384, 128))
        low = (n * gain2).astype(BF)
        out[r, :] = low
        projected[r, :] = dot(low, wproj[...])

    loop(2, downward)

    query = rows[2, pl.ds(0, 1), pl.ds(0, 128)]

    def student():
        weights, pooled = [], []
        for s in range(SEQ_DEV):
            pr = projected[pl.ds(s * SEQ, SEQ), :]
            t = pr * query
            per_head = []
            for half in (low_half, high_half):
                score = jnp.sum(t * half, axis=-1, keepdims=True) * 0.125
                e = jnp.exp(score - jnp.max(score, axis=0, keepdims=True))
                per_head.append(e / jnp.sum(e, axis=0, keepdims=True))
            weights.append(per_head)
            pooled.append(jnp.sum(pr * (per_head[0] * low_half + per_head[1] * high_half), axis=0, keepdims=True))
        none = jnp.zeros((1, 128), F32)
        pooled = jnp.concatenate(pooled + [none, none], axis=0)
        hidden = jnp.tanh(exact(pooled, hid[...]))
        o_logits[...] = exact(hidden, cls[...]) * alive_seq[...]
        g_log = cotl[...] * alive_seq[...]
        o_small[1] = exact(hidden, g_log, ((0,), (0,))).astype(BF)
        g_pre = exact(g_log, cls[...], ((1,), (1,))) * (1.0 - hidden * hidden)
        o_small[0] = exact(pooled, g_pre, ((0,), (0,))).astype(BF)
        g_pooled = exact(g_pre, hid[...], ((1,), (1,)))
        g_query = none
        for s in range(SEQ_DEV):
            r = pl.ds(s * SEQ, SEQ)
            pr = projected[r, :]
            gp = g_pooled[s:s + 1]
            t = pr * gp
            total = (weights[s][0] * low_half + weights[s][1] * high_half) * gp
            for half, w in zip((low_half, high_half), weights[s]):
                dw = jnp.sum(t * half, axis=-1, keepdims=True)
                ds = w * (dw - jnp.sum(w * dw, axis=0, keepdims=True)) * 0.125
                total = total + ds * (query * half)
                g_query = g_query + jnp.sum(ds * pr, axis=0, keepdims=True) * half
            gproj[r, :] = total.astype(BF)
        o_small[2] = jnp.broadcast_to(g_query, (128, 128)).astype(BF)

    once(student)

    def back(j):
        r = span(j, 384)
        keep_tok = alive[r, pl.ds(0, 1)]
        low = out[r, :]
        g_out = keep_tok * cotv[r, :].astype(F32) + dot(gproj[r, :], wproj[...], ((1,), (1,)))
        n = gsec[r, :]
        part = jnp.sum(g_out * n, axis=0, keepdims=True)
        rows[3, pl.ds(0, 1), :] = jnp.where(j == 0, part, part + rows[3, pl.ds(0, 1), :])
        g2 = norm_back(g_out, gain2, n, r2[r, pl.ds(0, 1)])
        gsec[r, :] = g2
        dlow[r, :] = g2.astype(BF)
        cotv[r, :] = (keep_tok * low.astype(F32)).astype(BF)
        low_part(j).start()
        for c in late(j):
            c.start()

    def low_part(j):
        r = span(j, 384)
        return pltpu.make_async_remote_copy(
            src_ref=dlow.at[r], dst_ref=o_dlow.at[1, r], send_sem=xsend.at[9 + j], recv_sem=xrecv.at[9 + j],
            device_id=place.sibling, device_id_type=MESH)

    def late(j):
        r = span(j, 384)
        return [pltpu.make_async_copy(src.at[r], dst.at[r], outsem.at[16 + 3 * j + n])
                for n, (src, dst) in enumerate(((dlow, o_dlow.at[0]), (gsec, o_gsec), (cotv, o_act)))]

    loop(2, back)

    def hidden_copy(j):
        c = span(j, D)
        return pltpu.make_async_copy(dact.at[:, c], o_gup.at[:, c], outsem.at[22 + j])

    def hidden_part(j):
        return pltpu.make_async_remote_copy(
            src_ref=dact.at[:, span(j, D)], dst_ref=o_gup_s.at[:, span(lax.rem(j, 2), D)],
            send_sem=xsend.at[11 + lax.rem(j, 2)], recv_sem=xrecv.at[11 + lax.rem(j, 2)],
            device_id=place.sibling, device_id_type=MESH)

    def hidden(i):
        j = lax.rem(i + 2 - 2 * place.core, 4)
        c = span(j, D)
        part = b_down[j // 2, pl.ds(lax.rem(j, 2) * 2, 2)].reshape(D, D)
        dact[:, c] = (dot(dlow[...], part, ((1,), (1,))) * dact[:, c].astype(F32)).astype(BF)
        hidden_copy(j).start()
        pl.when(j // 2 != place.core)(lambda: hidden_part(j).start())

    loop(4, hidden)

    def proj_grad():
        o_small[3:9] = dot(out[...], gproj[...], ((0,), (0,))).astype(BF).reshape(6, 128, 128)

    once(proj_grad)
    g.end()
    for c in stores + late(0) + late(1) + [hidden_copy(j) for j in range(4)] + [hidden_part(j) for j in range(2)]:
        c.wait()
    for n, dst in ((0, o_tokens2), (1, o_ctx), (2, o_normed)):
        cross.landed(n, dst.at[1], place.sibling)
    cross.sent()
    for c in [active_part(j) for j in range(4)] + [low_part(j) for j in range(2)]:
        c.wait()


def forward(tokens, cot, exit_layer, cot_logits, small, shards):
    hbm, vmem = pl.BlockSpec(memory_space=pl.ANY), pl.BlockSpec(memory_space=pltpu.VMEM)
    n = len(KINDS)
    count = n * 3 - 2

    def arr(*shape, dtype=BF):
        return jax.ShapeDtypeStruct(shape, dtype)

    outs = [
        (arr(TOK, D), hbm), (arr(8, 128, dtype=F32), vmem),
        (arr(D, 3 * D), hbm), (arr(D, D), hbm), (arr(D, FF), hbm),
        (arr(TOK, 3 * D), hbm), (arr(SEQ_DEV * PAIRS, 256, 128), hbm), (arr(2, TOK, D), hbm), (arr(2, TOK, D), hbm),
        (arr(TOK, D), hbm), (arr(TOK, 128, dtype=F32), hbm), (arr(2, TOK, FF), hbm), (arr(TOK, FF), hbm), (arr(TOK, FF // 2), hbm),
        (arr(TOK, D, dtype=F32), hbm), (arr(2, TOK, D), hbm), (arr(2, TOK, D), hbm),
        (arr(9, 128, 128), vmem), (arr(4, 8, D, dtype=F32), vmem),
    ]
    dma = pltpu.SemaphoreType.DMA
    scratch = [
        pltpu.VMEM((2, 4, 4, 32, 128), BF), pltpu.VMEM((2, 4, 4, 24, 3 * D), BF), pltpu.VMEM((2, 4, 4, 24, D), BF),
        pltpu.VMEM((2, 4, 4, 24, FF), BF), pltpu.VMEM((2, 4, 4, 96, D), BF),
        pltpu.VMEM((D, 3 * D), BF), pltpu.VMEM((D, D), BF), pltpu.VMEM((D, FF), BF),
        pltpu.VMEM((TOK, D), BF), pltpu.VMEM((TOK, D), BF), pltpu.VMEM((TOK, 3 * D), BF),
        pltpu.VMEM((SEQ_DEV * PAIRS, 256, 128), BF), pltpu.VMEM((TOK, D), BF), pltpu.VMEM((TOK, D), BF),
        pltpu.VMEM((TOK, D), BF), pltpu.VMEM((TOK, 128), F32), pltpu.VMEM((TOK, FF), BF), pltpu.VMEM((TOK, FF), BF),
        pltpu.VMEM((TOK, D), F32), pltpu.VMEM((TOK, 128), F32), pltpu.VMEM((TOK, D), BF), pltpu.VMEM((TOK, D), BF),
        pltpu.VMEM((TOK, 128), F32), pltpu.VMEM((TOK, 128), BF), pltpu.VMEM((D, 128), BF),
        pltpu.VMEM((128, 128), F32), pltpu.VMEM((128, 128), F32),
        pltpu.VMEM((TOK, 128), F32), pltpu.VMEM((8, 128), F32), pltpu.VMEM((8, 128), F32),
        pltpu.VMEM((32, 128), F32), pltpu.VMEM((32, 128), BF),
        dma((count * 3,)), dma((count * EVENTS,)), dma((2 * n,)), dma((2 * n,)),
        dma((2,)), dma((26,)), dma((13,)), dma((13,)),
    ]
    return pl.pallas_call(
        forward_kernel,
        out_shape=[o for o, _ in outs],
        in_specs=[hbm, hbm, pl.BlockSpec(memory_space=pltpu.SMEM)] + [vmem] * 7 + [hbm] * 4,
        out_specs=[s for _, s in outs],
        scratch_shapes=scratch,
        compiler_params=pltpu.CompilerParams(collective_id=0, has_side_effects=True, vmem_limit_bytes=VMEM),
        cost_estimate=pl.CostEstimate(flops=12 * 10**9, bytes_accessed=60 * 10**6, transcendentals=4 * 10**6),
        name="forward",
    )(tokens, cot, exit_layer, cot_logits, *small, *shards)


def landing(order):
    out, left = [], ["x", "z", "y"]
    for axis in reversed(order):
        left = [a for a in left if a != axis]
        out.append((1 if axis == "x" else 3, tuple(SIZE[a] for a in left)))
    return out


def add_box(place, held, left, fixed, terms):
    dims = tuple(SIZE[a] for a in left)

    def step(i):
        index = []
        for d in reversed(dims):
            index.append(i % d)
            i = i // d
        index = tuple(reversed(index))
        at = dict(zip(left, index))
        b = tuple(fixed[a] if a in fixed else at[a] if a in at else place.at(a) for a in ("x", "z", "y"))
        total = held[b]
        for t in terms:
            total = total + t[index]
        held[b] = total

    if dims:
        count = 1
        for d in dims:
            count *= d
        lax.fori_loop(0, count, lambda i, c: (step(i), c)[1], 0, unroll=4)
    else:
        step(0)


def reduce_unit(place, lane, side, number, core, order, direct, held, lands, last, result, twin, put):
    way = 1 if core == 0 else -1
    left, e = ["x", "z", "y"], 0
    for axis, bufs in zip(reversed(order), lands):
        left = [a for a in left if a != axis]
        ahead, back = place.near(axis, way), place.near(axis, -way)
        mine = {axis: place.at(axis)}
        if axis != "x" and (direct or not left):
            for n, (step, to) in enumerate(((way, ahead), (-way, back), (2, place.near(axis, 2)))):
                lane.go(e + n, held.at[place.box(left, **{axis: place.at(axis, step)})], bufs[n], to)
            yield
            for n in range(3):
                lane.landed(e + n, bufs[n], ahead)
            add_box(place, held, left, mine, bufs)
            e += 3
        elif axis == "x":
            lane.go(e, held.at[place.box(left, x=place.at("x", 1))], bufs[0], ahead)
            yield
            lane.landed(e, bufs[0], ahead)
            add_box(place, held, left, mine, [bufs[0]])
            e += 1
        else:
            lane.go(e, held.at[place.box(left, **{axis: place.at(axis, 2)})], bufs[0], ahead)
            lane.go(e + 1, held.at[place.box(left, **{axis: place.at(axis, -way)})], bufs[1], back)
            yield
            lane.landed(e, bufs[0], ahead)
            onward = {axis: place.at(axis, way)}
            add_box(place, held, left, onward, [bufs[0]])
            lane.go(e + 2, held.at[place.box(left, **onward)], bufs[2], ahead)
            yield
            lane.landed(e + 1, bufs[1], ahead)
            lane.landed(e + 2, bufs[2], ahead)
            add_box(place, held, left, mine, [bufs[1], bufs[2]])
            e += 3
    own = place.box(())
    lane.go(e, held.at[own], last, place.near("x", 2))
    yield
    lane.landed(e, last, place.near("x", 2))
    total = held[own] + last[...]
    result[...] = total
    side.go(number, result, twin, place.sibling)
    put[0][...] = total.astype(F32)
    yield
    side.landed(number, twin, place.sibling)
    put[1][...] = twin[...].astype(F32)


DIRECT = (QKV, OUT, SMALL)
FIRST = (QKV, OUT, SMALL, DOWN, UP)
PIECES = [(i, k) for i in (DOWN, UP, OUT, QKV, SMALL) for k in range(3) if i != SMALL or k == 1]


def piece_shape(i):
    return {SMALL: (16, 128), QKV: (24, 384), OUT: (24, 128), UP: (24, 512), DOWN: (96, 128)}[i]


def reduce_scratch():
    out = []
    for i, k in PIECES:
        shape = piece_shape(i)
        out.append(pltpu.VMEM((2, 4, 4) + shape, BF))
        for copies, dims in landing(ORDERS[0][k]):
            out.extend([pltpu.VMEM(dims + shape, BF)] * copies)
        out.extend([pltpu.VMEM(shape, BF)] * 3)
    return out


class Reduce:
    def __init__(self, place, scratch, outs, send, recv, ssend, srecv):
        self.place = place
        self.lanes = [[Lane(send, recv, 3 * n, SUMS * n) for n in range(len(PIECES))] for _ in range(2)]
        self.sides = [Wire(ssend, srecv) for _ in range(2)]
        self.held, self.units, self.live, self.done = {}, [{}, {}], [], {}
        for n, (i, k) in enumerate(PIECES):
            held = scratch.pop(0)
            lands = [[scratch.pop(0) for _ in range(copies)] for copies, _ in landing(ORDERS[0][k])]
            last, result, twin = (scratch.pop(0) for _ in range(3))
            self.held[i, k] = held
            for core in range(2):
                kind = "small" if i == SMALL else "cols"
                width = outs[i].shape[-1]
                put = (outs[i].at[piece(kind, core, k, width)], outs[i].at[piece(kind, 1 - core, k, width)])
                self.units[core][i, k] = reduce_unit(
                    place, self.lanes[core][n], self.sides[core], n, core, ORDERS[core][k], i in DIRECT,
                    held, lands, last, result, twin, put)

    def advance(self, pieces):
        def one(core):
            for p in pieces:
                next(self.units[core][p], None)

        self.place.on_core(one)

    def start(self, *pieces):
        self.advance(pieces)
        for p in pieces:
            self.live.append(p)
            self.done[p] = 1

    def pump(self, *arrays):
        todo = sorted((p for p in self.live if not arrays or p[0] in arrays), key=lambda p: FIRST.index(p[0]))
        self.advance(todo)
        for p in todo:
            self.done[p] += 1
            if self.done[p] == (6 if p[0] in DIRECT else 7):
                self.live.remove(p)

    def end(self):
        while self.live:
            self.pump()

        def one(core):
            for lane in self.lanes[core]:
                lane.sent()
            self.sides[core].sent()

        self.place.on_core(one)


def lay(held, value):
    for i in range(16):
        x, z, y = at_block(i)
        for j in range(2):
            held[x, z, 2 * y + j] = value[48 * i + 24 * j:48 * i + 24 * j + 24].astype(BF)


def backward_kernel(tokens2, merged_h, probs_h, ctx2_h, normed2_h, n1_h, r1_h, active2_h, gup_h, gup_s_h, gsec_h, dlow2_h,
                    wqkv_h, wout_h, wup_h, small_h, rows_h,
                    o_gtok, o_qkv, o_out, o_up, o_down, o_small,
                    tok2, act2, gup, normed2, ctx2, dlow2, n1, r1, gsec, attn, attn_s, gctx, gup_s, gm_s, probs,
                    w_big, w_out, packed, packed_s, g_row, small, rows, *rest):
    scratch = list(rest[:-8])
    send, recv, ssend, srecv, insem, wsem, xsend, xrecv = rest[-8:]
    place = Place()
    core = place.core
    loads = {}

    def load(name, src, dst):
        c = pltpu.make_async_copy(src, dst, insem.at[len(loads)])
        c.start()
        loads[name] = c

    def ready(*names):
        for name in names:
            loads[name].wait()

    def w_load(i, src, dst):
        c = pltpu.make_async_copy(src, dst, wsem.at[i])
        return c

    def active_load(j):
        return pltpu.make_async_copy(active2_h.at[:, :, span(j, D)], act2.at[:, :, span(j, D)], insem.at[18 + j])

    load("dlow", dlow2_h, dlow2)
    for j in range(4):
        active_load(j).start()
    greet(place)
    red = Reduce(place, scratch, {QKV: o_qkv, OUT: o_out, UP: o_up, DOWN: o_down, SMALL: o_small},
                 send, recv, ssend, srecv)
    cross = Wire(xsend, xrecv)

    def mine(size):
        return pl.ds(pl.multiple_of(core * size, 128), size)

    def other(size):
        return pl.ds(pl.multiple_of((1 - core) * size, 128), size)

    load("rows", rows_h, rows)
    load("small", small_h, small)
    load("gup", gup_h, gup)
    load("gup_s", gup_s_h, gup_s)
    load("normed", normed2_h, normed2)

    def up_load(j, slot):
        return w_load(slot, wup_h.at[span(j, 256)], w_big.at[slot])

    def qkv_load(j, slot):
        return w_load(slot, wqkv_h.at[span(j, 256)], w_big.at[slot, :, pl.ds(0, 3 * D)])

    ready("dlow")

    def down(j):
        active_load(j).wait()
        left = dlow2[:, :, mine(384)].reshape(2 * TOK, 384)
        g = dot(left, act2[:, :, span(j, D)].reshape(2 * TOK, D), ((0,), (0,))).T.astype(BF)
        for k in range(3):
            red.held[DOWN, k][j // 2, pl.ds(lax.rem(j, 2) * 2, 2)] = g[:, 128 * k:128 * k + 128].reshape(2, 4, 96, 128)

    loop(4, down)
    red.start((DOWN, 0), (DOWN, 1), (DOWN, 2))
    for j in range(2):
        up_load(j, j).start()
    load("gsec", gsec_h, gsec)
    load("n1", n1_h, n1)
    load("r1", r1_h, r1)
    load("wout", wout_h, w_out)
    load("merged", merged_h, act2.at[0, :, pl.ds(0, 3 * D)])
    merged = act2.at[0, :, pl.ds(0, 3 * D)]
    load("probs", probs_h, probs)
    load("ctx", ctx2_h, ctx2)
    load("tokens", tokens2, tok2)
    ready("gup", "gup_s", "normed")
    for k in range(3):
        own = gup[:, pl.ds(pl.multiple_of(core * (FF // 2) + 512 * k, 128), 512)]

        def grad_up():
            lay(red.held[UP, k], dot(normed2[0], own, ((0,), (0,))) + dot(normed2[1], gup_s[:, 512 * k:512 * k + 512], ((0,), (0,))))

        once(grad_up)
        red.start((UP, k))
    ready("gsec", "n1", "r1", "rows", "small")

    def g_normed(j):
        slot = lax.rem(j, 2)
        up_load(j, slot).wait()
        c = span(j, 256)
        gsec[:, c] = gsec[:, c] + dot(gup[...], w_big[slot], ((1,), (1,)))
        pl.when(j < 1)(lambda: up_load(j + 2, slot).start())

    loop(3, g_normed)
    for j in range(2):
        qkv_load(j, 1 - j).start()
    gain1 = rows[0, pl.ds(0, 1), :]

    def norm1(j):
        r = span(j, 384)
        g, n = gsec[r, :], n1[r, :].astype(F32)
        part = jnp.sum(g * n, axis=0, keepdims=True)
        g_row[0:1] = jnp.where(j == 0, part, part + g_row[0:1])
        g = norm_back(g, gain1, n, r1[r, pl.ds(0, 1)])
        gsec[r, :] = g
        attn[r, :] = g.astype(BF)

    loop(2, norm1)
    cross.go(1, attn.at[:, other(384)], attn_s, place.sibling)
    ready("wout", "ctx")

    def context(j):
        r = span(j, 384)
        gctx[r, :] = dot(attn[r, :], w_out[...], ((1,), (1,))).astype(BF)

    loop(2, context)

    ready("merged", "probs")

    low_half, high_half = halves()
    la, lb = low_half.astype(BF), high_half.astype(BF)
    qa, qb = (low_half * 0.125).astype(BF), (high_half * 0.125).astype(BF)

    def attend_back(s):
        r = span(s, SEQ)
        at = [[pl.ds(768 * a + 128 * p, 128) for a in range(3)] for p in range(PAIRS)]
        d2, q2, gp, gs = [], [], [], []
        for p in range(PAIRS):
            q, d = merged[r, at[p][0]], gctx[r, pl.ds(128 * p, 128)]
            d2.append(jnp.concatenate([d * la, d * lb], axis=0))
            q2.append(jnp.concatenate([q * qa, q * qb], axis=0))
            gp.append(dot(d2[p], merged[r, at[p][2]], ((1,), (1,))))
        for p in range(PAIRS):
            pr = probs[s * PAIRS + p]
            merged[r, at[p][2]] = dot(pr, d2[p], ((0,), (0,))).astype(BF)
            pf = pr.astype(F32)
            t = pf * gp[p]
            gs.append((t - pf * jnp.sum(t, axis=-1, keepdims=True)).astype(BF))
        for p in range(PAIRS):
            both = dot(gs[p], merged[r, at[p][1]])
            merged[r, at[p][0]] = ((both[:SEQ] * low_half + both[SEQ:] * high_half) * 0.125).astype(BF)
            merged[r, at[p][1]] = dot(gs[p], q2[p], ((0,), (0,))).astype(BF)

    def gm_part(part):
        r = pl.ds(256 * part, 256)
        return pltpu.make_async_remote_copy(
            src_ref=act2.at[0, r, other(3 * D // 2)], dst_ref=gm_s.at[r], send_sem=xsend.at[4 + part],
            recv_sem=xrecv.at[4 + part], device_id=place.sibling, device_id_type=MESH)

    for part in range(3):

        def attend_part(s):
            attend_back(s + 2 * part)

        loop(2, attend_part)
        if part == 0:
            red.pump(DOWN)
        if part == 2:
            red.pump(DOWN, UP)
        gm_part(part).start()
    ready("tokens")

    def g_tokens(j):
        slot = lax.rem(j + 1, 2)
        qkv_load(j, slot).wait()
        c = span(j, 256)
        gsec[:, c] = gsec[:, c] + dot(merged[...], w_big[slot, :, :3 * D], ((1,), (1,)))
        pl.when(j < 1)(lambda: qkv_load(j + 2, slot).start())

    lax.fori_loop(0, 1, lambda j, c: (g_tokens(j), c)[1], 0)
    for part in range(3):
        gm_part(part).wait_recv()
    for k in range(3):
        own = merged[:, pl.ds(pl.multiple_of(core * (3 * D // 2) + 384 * k, 128), 384)]

        def grad_qkv():
            lay(red.held[QKV, k], dot(tok2[0], own, ((0,), (0,))) + dot(tok2[1], gm_s[:, 384 * k:384 * k + 384], ((0,), (0,))))

        once(grad_qkv)
        red.start((QKV, k))
    def pack_small():
        p_proj, p_hid, p_cls, p_misc = picks()
        pack = dot(p_proj, small[3:9].reshape(D, 128), ((0,), (0,)))
        pack = pack + dot(p_hid, small[0], ((0,), (0,)))
        lane = iota((128, 128), 1)
        pack = pack + dot(p_cls, jnp.where(lane < 14, small[1].astype(F32), 0.0).astype(BF), ((0,), (0,)))
        values = (g_row[0:1], rows[3, pl.ds(0, 1), :], small[2, pl.ds(0, 1), :].astype(F32))
        misc = jnp.zeros((32, 128), F32)
        for (name, first, size, per), value in zip(ROWS, values):
            tile, held = spread(first, size, per)
            misc = misc + dot(jnp.where(held, value, 0.0).astype(BF), tile, ((1,), (1,)))
        packed[...] = (pack + dot(p_misc, misc.astype(BF), ((0,), (0,)))).astype(BF).reshape(2, 4, 4, 32, 128)

    once(pack_small)
    place.on_core(lambda c: cross.copy(3, packed.at[:, :, :, pl.ds(16 - 16 * c, 16)], packed_s, place.sibling).start())

    cross.landed(1, attn_s, place.sibling)

    def grad_out():
        g = dot(ctx2[0], attn[:, mine(384)], ((0,), (0,))) + dot(ctx2[1], attn_s[...], ((0,), (0,)))
        for k in range(3):
            lay(red.held[OUT, k], g[:, 128 * k:128 * k + 128])

    once(grad_out)
    cross.landed(3, packed_s, place.sibling)

    def small_half(c):
        red.held[SMALL, 1][...] = packed[:, :, :, 16 * c:16 * c + 16, :] + packed_s[...]

    place.on_core(small_half)
    red.start((OUT, 0), (OUT, 1), (OUT, 2), (SMALL, 1))
    red.pump(DOWN, UP)
    lax.fori_loop(1, 3, lambda j, c: (g_tokens(j), c)[1], 0)
    red.pump()
    store = pltpu.make_async_copy(gsec, o_gtok, insem.at[len(loads)])
    store.start()
    red.end()
    cross.sent()
    for part in range(3):
        gm_part(part).wait_send()
    place.on_core(lambda c: cross.copy(3, packed.at[:, :, :, pl.ds(16 - 16 * c, 16)], packed_s, place.sibling).wait_send())
    store.wait()


def backward(*args):
    hbm, vmem = pl.BlockSpec(memory_space=pl.ANY), pl.BlockSpec(memory_space=pltpu.VMEM)

    def arr(*shape, dtype=F32):
        return jax.ShapeDtypeStruct(shape, dtype)

    dma = pltpu.SemaphoreType.DMA
    count = len(PIECES)
    scratch = [
        pltpu.VMEM((2, TOK, D), BF), pltpu.VMEM((2, TOK, FF), BF), pltpu.VMEM((TOK, FF), BF),
        pltpu.VMEM((2, TOK, D), BF), pltpu.VMEM((2, TOK, D), BF), pltpu.VMEM((2, TOK, D), BF),
        pltpu.VMEM((TOK, D), BF), pltpu.VMEM((TOK, 128), F32), pltpu.VMEM((TOK, D), F32),
        pltpu.VMEM((TOK, D), BF), pltpu.VMEM((TOK, D // 2), BF), pltpu.VMEM((TOK, D), BF),
        pltpu.VMEM((TOK, FF // 2), BF), pltpu.VMEM((TOK, 3 * D // 2), BF),
        pltpu.VMEM((SEQ_DEV * PAIRS, 256, 128), BF),
        pltpu.VMEM((2, 256, FF), BF), pltpu.VMEM((D, D), BF),
        pltpu.VMEM((2, 4, 4, 32, 128), BF), pltpu.VMEM((2, 4, 4, 16, 128), BF), pltpu.VMEM((8, D), F32),
        pltpu.VMEM((9, 128, 128), BF), pltpu.VMEM((4, 8, D), F32),
    ] + reduce_scratch() + [
        dma((count * 3,)), dma((count * SUMS,)), dma((count,)), dma((count,)), dma((22,)), dma((2,)), dma((7,)), dma((7,)),
    ]
    return pl.pallas_call(
        backward_kernel,
        out_shape=[arr(TOK, D), arr(24, 3 * D), arr(24, D), arr(24, FF), arr(96, D), arr(32, 128)],
        in_specs=[hbm] * 17,
        out_specs=[hbm] + [vmem] * 5,
        scratch_shapes=scratch,
        compiler_params=pltpu.CompilerParams(collective_id=1, has_side_effects=True, vmem_limit_bytes=VMEM),
        cost_estimate=pl.CostEstimate(flops=24 * 10**9, bytes_accessed=60 * 10**6, transcendentals=0),
        name="backward",
    )(*args)


def finish_kernel(act, logits, gtok, qkv, out, up, down, small, *rest):
    o_act, o_logits, o_gtok, o_qkv, o_out, o_g1, o_up, o_down, o_g2, o_proj, o_pool, o_hid, o_cls = rest[:13]
    h_gtok, h_act, h_qkv, h_up, h_down, h_out, sems = rest[13:]
    moves = [(gtok, h_gtok, o_gtok, r) for r in range(3)] + [(act, h_act, o_act, r) for r in range(3)]
    moves += [(qkv, h_qkv, o_qkv, None), (up, h_up, o_up, None), (down, h_down, o_down, None), (out, h_out, o_out, None)]

    def at(ref, r):
        return ref if r is None else ref.at[pl.ds(256 * r, 256)]

    come = [pltpu.make_async_copy(at(a, r), at(h, r), sems.at[n]) for n, (a, h, o, r) in enumerate(moves)]
    go = [pltpu.make_async_copy(at(h, r), at(o, r), sems.at[len(moves) + n]) for n, (a, h, o, r) in enumerate(moves)]
    for c in come:
        c.start()
    o_logits[...] = logits[0:SEQ_DEV, 0:14]
    o_proj[...] = small[0:24]
    o_hid[...] = small[24:28]
    o_cls[...] = small[28:32, 0:14]
    o_g1[...] = small[28:29, 16:40]
    o_g2[...] = small[28:29, 40:64]
    o_pool[...] = small[28:29, 64:68]
    for c, d in zip(come, go):
        c.wait()
        d.start()
    for d in go:
        d.wait()


def finish(*args):
    hbm, vmem = pl.BlockSpec(memory_space=pl.ANY), pl.BlockSpec(memory_space=pltpu.VMEM)
    shapes = ((TOK, D), (SEQ_DEV, 14), (TOK, D), (24, 3 * D), (24, D), (1, 24), (24, FF), (96, D), (1, 24), (24, 128),
              (1, 4), (4, 128), (4, 14))
    moved = (0, 2, 3, 4, 6, 7)
    return pl.pallas_call(
        finish_kernel,
        out_shape=[jax.ShapeDtypeStruct(s, F32 if n else BF) for n, s in enumerate(shapes)],
        in_specs=[hbm, vmem, hbm, hbm, hbm, hbm, hbm, vmem],
        out_specs=[hbm if n in moved else vmem for n in range(len(shapes))],
        scratch_shapes=[pltpu.VMEM((TOK, D), F32), pltpu.VMEM((TOK, D), BF), pltpu.VMEM((24, 3 * D), F32),
                        pltpu.VMEM((24, FF), F32), pltpu.VMEM((96, D), F32), pltpu.VMEM((24, D), F32),
                        pltpu.SemaphoreType.DMA((20,))],
        compiler_params=pltpu.CompilerParams(vmem_limit_bytes=VMEM),
        name="finish",
    )(*args)


def local(tokens, exit_layer, w_qkv, w_out, gain_attn, w_up, w_down, gain_ffn, w_proj, pool_query, w_hid, w_cls,
          cot_out, cot_logits):
    small = (w_proj, w_hid, w_cls, gain_attn[None], gain_ffn[None], pool_query[None])
    (act, logits, f_qkv, f_out, f_up, merged, probs, ctx, normed, n1, r1, active, gup, gup_s, gsec, dlow, tokens2,
     small_g, rows) = forward(
         tokens, cot_out, exit_layer, cot_logits, small, (w_qkv, w_out, w_up, w_down))
    g_tok, g_qkv, g_out, g_up, g_down, g_small = backward(
        tokens2, merged, probs, ctx, normed, n1, r1, active, gup, gup_s, gsec, dlow, f_qkv, f_out, f_up, small_g, rows)
    outs = list(finish(act, logits, g_tok, g_qkv, g_out, g_up, g_down, g_small))
    for n in (5, 8, 10):
        outs[n] = outs[n].reshape(-1)
    return tuple(outs)


def solution(mesh):
    both, wide = P(("wide", "grp"), None), P("wide", None)
    in_specs = (both, P(("wide", "grp")), wide, wide, P("wide"), wide, wide, P("wide"), wide, P("wide"), wide, wide,
                both, both)
    out_specs = (both, both, both, wide, wide, P("wide"), wide, wide, P("wide"), wide, P("wide"), wide, wide)
    return jax.shard_map(local, mesh=mesh, in_specs=in_specs, out_specs=out_specs, check_vma=False)
```

```python
import functools
import jax
import jax.numpy as jnp
from jax import lax
from jax.sharding import PartitionSpec as P
from jax.experimental import pallas as pl
from jax.experimental.pallas import tpu as pltpu

D = 768
FF = 3072
TOK = 768
SEQ_DEV = 6
PAIRS = 6
SEQ = 128
LAYER = 3
MESH = pl.DeviceIdType.MESH
BF = jnp.bfloat16
F32 = jnp.float32
SIZE = {"x": 2, "z": 4, "y": 4}
ORDERS = (
    (("y", "z", "x"), ("z", "x", "y"), ("y", "x", "z")),
    (("z", "y", "x"), ("z", "x", "y"), ("y", "x", "z")),
)
EVENTS = 7
SUMS = 8
VMEM = 62 * 2**20


class Place:
    def __init__(self):
        wide, grp = lax.axis_index("wide"), lax.axis_index("grp")
        xl, z, y = wide // 16, (wide // 4) % 4, wide % 4
        x = (grp // 2) * 2 + xl
        self.core = grp % 2
        self.places = {("x", 0): xl, ("x", 1): 1 - xl}
        for axis, here in (("z", z), ("y", y)):
            for step in range(4):
                self.places[axis, step] = (here + step) % 4
        self.ids = {}
        for step in (1, 2, 3):
            far = (x + step) % 4
            self.ids["x", step] = ((far % 2) * 16 + z * 4 + y, (far // 2) * 2 + self.core)
            self.ids["y", step] = (xl * 16 + z * 4 + self.places["y", step], grp)
            self.ids["z", step] = (xl * 16 + self.places["z", step] * 4 + y, grp)
        self.sibling = (wide, grp + 1 - 2 * self.core)

    def near(self, axis, step):
        return self.ids[axis, step % 4]

    def at(self, axis, step=0):
        return self.places[axis, step % SIZE[axis]]

    def box(self, have, **fixed):
        out = []
        for axis in ("x", "z", "y"):
            if axis in fixed:
                out.append(fixed[axis])
            elif axis in have:
                out.append(slice(None))
            else:
                out.append(self.at(axis))
        return tuple(out)

    def on_core(self, step):
        for core in (0, 1):
            pl.when(self.core == core)(functools.partial(step, core))


def greet(place):
    barrier = pltpu.get_barrier_semaphore()
    ids = [place.near(a, s) for a in ("x", "y", "z") for s in (1, -1, 2)] + [place.sibling]
    for i in ids:
        pl.semaphore_signal(barrier, inc=1, device_id=i, device_id_type=MESH)
    pl.semaphore_wait(barrier, len(ids))


class Wire:
    def __init__(self, send, recv):
        self.send, self.recv = send, recv
        self.started = []

    def copy(self, n, src, dst, to):
        return pltpu.make_async_remote_copy(
            src_ref=src, dst_ref=dst, send_sem=self.send.at[n], recv_sem=self.recv.at[n],
            device_id=to, device_id_type=MESH,
        )

    def go(self, n, src, dst, to):
        self.copy(n, src, dst, to).start()
        self.started.append((n, src, dst, to))

    def landed(self, n, dst, to):
        self.copy(n, dst, dst, to).wait_recv()

    def sent(self):
        for c in self.started:
            self.copy(*c).wait_send()


def piece(kind, core, k, width):
    if kind == "cols":
        return (slice(None), pl.ds((core * 3 + k) * (width // 6), width // 6))
    return (pl.ds(core * 16, 16), slice(None)) if k == 1 else None


class Lane:
    def __init__(self, send, recv, first_send, first_recv):
        self.send, self.recv, self.first_send, self.first_recv = send, recv, first_send, first_recv
        self.out, self.count = {}, 0

    def copy(self, slot, e, src, dst, to):
        return pltpu.make_async_remote_copy(
            src_ref=src, dst_ref=dst, send_sem=self.send.at[self.first_send + slot],
            recv_sem=self.recv.at[self.first_recv + e], device_id=to, device_id_type=MESH,
        )

    def go(self, e, src, dst, to):
        slot = self.count % 3
        self.count += 1
        if slot in self.out:
            self.copy(slot, *self.out[slot]).wait_send()
        self.copy(slot, e, src, dst, to).start()
        self.out[slot] = (e, src, dst, to)

    def landed(self, e, dst, to):
        self.copy(0, e, dst, dst, to).wait_recv()

    def sent(self):
        for slot, c in self.out.items():
            self.copy(slot, *c).wait_send()


def gather_unit(place, lane, sib, core, order, own, full):
    way = 1 if core == 0 else -1
    have, e = [], 0
    for axis in order:
        mine = place.box(have)
        src = full(mine) if have else own
        ahead, back, far = place.near(axis, way), place.near(axis, -way), place.near(axis, 2)
        last = axis == order[2]
        if axis == "x":
            lane.go(e, src, full(mine), ahead)
            yield
            got = place.box(have, x=place.at("x", 1))
            lane.landed(e, full(got), ahead)
            if last:
                sib(got)
            e += 1
        elif not last:
            for n, to in enumerate((ahead, back, far)):
                lane.go(e + n, src, full(mine), to)
            yield
            for n, step in enumerate((-way, way, 2)):
                lane.landed(e + n, full(place.box(have, **{axis: place.at(axis, step)})), ahead)
            e += 3
        else:
            lane.go(e, src, full(mine), ahead)
            lane.go(e + 1, src, full(mine), back)
            yield
            got = place.box(have, **{axis: place.at(axis, -way)})
            lane.landed(e, full(got), ahead)
            lane.go(e + 2, full(got), full(got), ahead)
            if last:
                sib(got)
            yield
            for late, step in ((1, way), (2, 2)):
                got = place.box(have, **{axis: place.at(axis, step)})
                lane.landed(e + late, full(got), ahead)
                if last:
                    sib(got)
            e += 3
        have.append(axis)
        if axis == order[1]:
            sib(place.box(have))


class Gather:
    def __init__(self, place, kinds, shards, fulls, send, recv, side, keep):
        self.place, self.kinds, self.shards, self.fulls = place, kinds, shards, fulls
        self.side, self.keep = side, keep
        n = len(kinds)
        self.lanes = [[], []]
        self.units = [[[] for _ in range(n)] for _ in range(2)]
        for core in range(2):
            for i in range(n):
                for k in range(3):
                    tail = piece(kinds[i], core, k, shards[i].shape[-1])
                    if tail is None:
                        continue
                    at = len(self.lanes[core])
                    lane = Lane(send, recv, at * 3, at * EVENTS)
                    self.lanes[core].append(lane)
                    full = functools.partial(self.part, i, tail)
                    sib = functools.partial(self.pass_on, i, full)
                    self.units[core][i].append(gather_unit(
                        place, lane, sib, core, ORDERS[core][k], shards[i].at[tail], full))

    def part(self, i, tail, box):
        return self.fulls[i].at[box + tail]

    def half(self, i, core):
        size = self.shards[i].shape[-1] // 2
        if self.kinds[i] == "cols":
            return (slice(None), pl.ds(core * size, size))
        return (pl.ds(core * 16, 16), slice(None))

    def to_side(self, sems, n, src, dst):
        return pltpu.make_async_remote_copy(
            src_ref=src, dst_ref=dst, send_sem=sems.at[n], recv_sem=sems.at[len(self.kinds) + n],
            device_id=self.place.sibling, device_id_type=MESH)

    def pass_on(self, i, full, box):
        self.to_side(self.side, i, full(box), full(box)).start()

    def own(self, i, core):
        half = self.half(i, 1 - core)
        return self.to_side(self.keep, i, self.shards[i].at[half], self.fulls[i].at[self.place.box(()) + half])

    def own_start(self):
        self.place.on_core(lambda core: [self.own(i, core).start() for i in range(len(self.kinds))] and None)

    def own_landed(self):
        def one(core):
            for i in range(len(self.kinds)):
                self.own(i, core).wait_send()
                self.own(i, 1 - core).wait_recv()

        self.place.on_core(one)

    def step(self, *arrays):
        def one(core):
            for i in arrays:
                units = self.units[core][i]
                for u in units[1:] + units[:1]:
                    next(u, None)

        self.place.on_core(one)

    def everything(self, i, core):
        part = self.fulls[i].at[(slice(None),) * 3 + self.half(i, core)]
        return self.to_side(self.side, i, part, part)

    def whole(self, *arrays):
        def one(core):
            for i in arrays:
                self.everything(i, 1 - core).wait_recv()

        self.place.on_core(one)

    def end(self):
        def one(core):
            for lane in self.lanes[core]:
                lane.sent()
            for i in range(len(self.kinds)):
                self.everything(i, core).wait_send()

        self.place.on_core(one)


def dot(a, b, dims=((1,), (0,))):
    return lax.dot_general(a, b, (dims, ((), ())), preferred_element_type=F32)


def exact(a, b, dims=((1,), (0,))):
    return lax.dot_general(a, b, (dims, ((), ())), precision=lax.Precision.HIGHEST, preferred_element_type=F32)


def iota(shape, dim):
    return lax.broadcasted_iota(jnp.int32, shape, dim)


def over24(i):
    return (i * 2731) >> 16


def ones_where(hit):
    return jnp.where(hit, 1.0, 0.0).astype(BF)


def picks():
    i, j = iota((768, 1024), 0), iota((768, 1024), 1)
    proj = ones_where(j == i + 8 * over24(i))
    i, j = iota((128, 1024), 0), iota((128, 1024), 1)
    at = 32 * (i >> 2) + (i & 3)
    hid, cls = ones_where(j == at + 24), ones_where(j == at + 28)
    i, j = iota((32, 1024), 0), iota((32, 1024), 1)
    misc = ones_where(j == 32 * i + 28)
    return proj, hid, cls, misc


def spread(first, size, per):
    i, l = iota((128, size), 0), iota((128, size), 1)
    block = over24(l) if per == 24 else l >> 2
    w, m = iota((32, size), 0), iota((32, size), 1)
    held = over24(m) if per == 24 else m >> 2
    return ones_where(i - first == l - per * block), held == w


ROWS = (("gain_attn", 16, 768, 24), ("gain_ffn", 40, 768, 24), ("pool", 64, 128, 4))


def normalise(h):
    centre = h - jnp.mean(h, axis=-1, keepdims=True)
    r = lax.rsqrt(jnp.mean(centre * centre, axis=-1, keepdims=True) + 1e-06)
    return centre * r, r


def norm_back(g, gain, n, r):
    gn = g * gain
    return r * (gn - jnp.mean(gn, axis=-1, keepdims=True) - n * jnp.mean(gn * n, axis=-1, keepdims=True))


TANH_A = 0.7978845608028654
TANH_B = 0.7978845608028654 * 0.044715


def gelu(u):
    u2 = u * u
    h = 0.5 + 0.5 * jnp.tanh(u * (TANH_A + TANH_B * u2))
    y = u * h
    return y, h + y * (1.0 - h) * (2.0 * TANH_A + 6.0 * TANH_B * u2)


def at_block(i):
    return i // 8, (i // 2) % 4, i % 2


def join(blocks, whole):
    def one(i, carry):
        x, z, y = at_block(i)
        pair = jnp.concatenate([blocks[x, z, 2 * y], blocks[x, z, 2 * y + 1]], axis=0)
        whole[pl.ds(pl.multiple_of(i * 48, 48), 48), :] = pair
        return carry

    lax.fori_loop(0, 16, one, 0)


def loop(n, step):
    def one(i, carry):
        step(i)
        return carry

    lax.fori_loop(0, n, one, 0)


def once(step):
    step()


def span(i, size):
    return pl.ds(pl.multiple_of(i * size, size), size)


def halves():
    lane = iota((1, 128), 1)
    return jnp.where(lane < 64, 1.0, 0.0), jnp.where(lane < 64, 0.0, 1.0)


KINDS = ("small", "cols", "cols", "cols", "cols")
SMALL, QKV, OUT, UP, DOWN = range(5)


def forward_kernel(tokens, cot, exit_layer, cot_logits, i_proj, i_hid, i_cls, i_gain1, i_gain2, i_pool, s_qkv, s_out, s_up, s_down,
                   o_act, o_logits, o_wqkv, o_wout, o_wup, o_merged, o_probs, o_ctx, o_normed, o_n1, o_r1,
                   o_active, o_gup, o_gup_s, o_gsec, o_dlow, o_tokens2, o_small, rows,
                   b_small, b_qkv, b_out, b_up, b_down, w_qkv, w_out, w_up, tok, cotv, merged, probs, ctx, normed, n1, r1,
                   active, dact, gsec, r2, dlow, out, projected, gproj, wproj, hid, cls,
                   alive, alive_seq, cotl, wide_small, s_small, send, recv, ssem, lsem, insem, outsem, xsend, xrecv):
    place = Place()
    loads = [pltpu.make_async_copy(tokens, tok, insem.at[0]), pltpu.make_async_copy(cot, cotv, insem.at[1])]
    for c in loads:
        c.start()
    wide_small[0:24] = i_proj[...].astype(F32)
    wide_small[24:28] = i_hid[...].astype(F32)
    line = [jnp.zeros((1, 16), F32)] + [i[...].astype(F32) for i in (i_gain1, i_gain2, i_pool)]
    wide_small[28:29] = jnp.concatenate(line + [jnp.zeros((1, 60), F32)], axis=1)
    wide_small[29:32] = jnp.zeros((3, 128), F32)
    wide_small[28:32, 0:14] = i_cls[...].astype(F32)
    s_small[...] = wide_small[...].astype(BF)
    greet(place)
    g = Gather(place, KINDS, (s_small, s_qkv, s_out, s_up, s_down), (b_small, b_qkv, b_out, b_up, b_down),
               send, recv, ssem, lsem)
    stores = []
    cross = Wire(xsend, xrecv)

    def keep(src, dst):
        c = pltpu.make_async_copy(src, dst, outsem.at[len(stores)])
        c.start()
        stores.append(c)

    def share(n, src, dst):
        keep(src, dst.at[0])
        cross.go(n, src, dst.at[1], place.sibling)

    g.step(QKV, SMALL)
    g.own_start()
    g.step(OUT, UP, DOWN)
    loads[0].wait()
    cotl[...] = jnp.zeros((8, 128), F32)
    cotl[0:SEQ_DEV, 0:14] = cot_logits[...]
    alive_seq[...] = jnp.zeros((8, 128), F32)
    for s in range(SEQ_DEV):
        stays = jnp.clip(exit_layer[s] - (LAYER - 1), 0, 1).astype(F32)
        alive[pl.ds(s * SEQ, SEQ), :] = jnp.full((SEQ, 128), stays)
        alive_seq[pl.ds(s, 1), :] = jnp.full((1, 128), stays)
    g.own_landed()
    g.step(QKV, SMALL)
    g.step(OUT, UP, DOWN)
    g.step(QKV, SMALL)
    g.step(QKV, SMALL)
    g.step(OUT, UP, DOWN)
    g.step(QKV, SMALL)
    g.whole(QKV, SMALL)
    join(b_qkv, w_qkv)

    def qkv(j):
        c = span(j, D)
        merged[:, c] = dot(tok[...], w_qkv[:, c]).astype(BF)

    loop(3, qkv)
    keep(w_qkv, o_wqkv)
    keep(merged, o_merged)
    g.step(OUT, UP)

    def small_weights():
        p_proj, p_hid, p_cls, p_misc = picks()
        pack = b_small[...].reshape(1024, 128)
        wproj[...] = dot(p_proj, pack).astype(BF)
        hid[...] = dot(p_hid, pack)
        cls[...] = jnp.where(iota((128, 128), 1) < 14, dot(p_cls, pack), 0.0)
        misc = dot(p_misc, pack).astype(BF)
        for n, (name, first, size, per) in enumerate(ROWS):
            tile, held = spread(first, size, per)
            row = jnp.sum(jnp.where(held, dot(misc, tile), 0.0), axis=0, keepdims=True)
            rows[n, :, pl.ds(0, size)] = jnp.broadcast_to(row, (8, size))

    once(small_weights)
    low_half, high_half = halves()

    qa, qb = (low_half * 0.125).astype(BF), (high_half * 0.125).astype(BF)

    def attend(s):
        r = span(s, SEQ)
        scores, prs = [], []
        for p in range(PAIRS):
            q, k = (merged[r, pl.ds(768 * a + 128 * p, 128)] for a in range(2))
            scores.append(dot(jnp.concatenate([q * qa, q * qb], axis=0), k, ((1,), (1,))))
        for p in range(PAIRS):
            e = jnp.exp(scores[p] - jnp.max(scores[p], axis=-1, keepdims=True))
            prs.append((e * (1.0 / jnp.sum(e, axis=-1, keepdims=True))).astype(BF))
            probs[s * PAIRS + p] = prs[p]
        for p in range(PAIRS):
            both = dot(prs[p], merged[r, pl.ds(1536 + 128 * p, 128)])
            ctx[r, pl.ds(128 * p, 128)] = (both[:SEQ] * low_half + both[SEQ:] * high_half).astype(BF)

    for part in range(3):

        def attend_two(s):
            attend(s + 2 * part)

        loop(2, attend_two)
        if part == 0:
            g.step(DOWN)
        elif part == 1:
            g.step(OUT)
        else:
            g.step(UP)
    keep(probs, o_probs)
    g.whole(OUT)
    join(b_out, w_out)
    gain1 = rows[0, pl.ds(0, 1), :]

    def mix(j):
        r = span(j, 384)
        n, inv = normalise(tok[r, :].astype(F32) + dot(ctx[r, :], w_out[...]))
        n1[r, :] = n.astype(BF)
        normed[r, :] = (n * gain1).astype(BF)
        r1[r, :] = jnp.broadcast_to(inv, (384, 128))

    loop(2, mix)
    g.whole(UP)
    share(2, normed, o_normed)
    share(1, ctx, o_ctx)
    share(0, tok, o_tokens2)
    keep(w_out, o_wout)
    keep(n1, o_n1)
    keep(r1, o_r1)
    join(b_up, w_up)

    def active_part(j):
        c = span(j, D)
        return pltpu.make_async_remote_copy(
            src_ref=active.at[:, c], dst_ref=o_active.at[1, :, c], send_sem=xsend.at[5 + j], recv_sem=xrecv.at[5 + j],
            device_id=place.sibling, device_id_type=MESH)

    def upward(j):
        c = span(j, D)
        y, dy = gelu(dot(normed[...], w_up[:, c]))
        active[:, c] = y.astype(BF)
        dact[:, c] = dy.astype(BF)
        active_part(j).start()

    def upward_late(j):
        upward(j + 2)

    loop(2, upward)
    g.step(DOWN)
    loop(2, upward_late)
    g.whole(DOWN)
    keep(active, o_active.at[0])
    keep(w_up, o_wup)
    loads[1].wait()
    gain2 = rows[1, pl.ds(0, 1), :]

    def downward(j):
        r = span(j, 384)
        second = normed[r, :].astype(F32) + dot(active[r, :], b_down[...].reshape(FF, D))
        n, inv = normalise(second)
        gsec[r, :] = n
        r2[r, :] = jnp.broadcast_to(inv, (384, 128))
        low = (n * gain2).astype(BF)
        out[r, :] = low
        projected[r, :] = dot(low, wproj[...])

    loop(2, downward)

    query = rows[2, pl.ds(0, 1), pl.ds(0, 128)]

    def student():
        weights, pooled = [], []
        for s in range(SEQ_DEV):
            pr = projected[pl.ds(s * SEQ, SEQ), :]
            t = pr * query
            per_head = []
            for half in (low_half, high_half):
                score = jnp.sum(t * half, axis=-1, keepdims=True) * 0.125
                e = jnp.exp(score - jnp.max(score, axis=0, keepdims=True))
                per_head.append(e / jnp.sum(e, axis=0, keepdims=True))
            weights.append(per_head)
            pooled.append(jnp.sum(pr * (per_head[0] * low_half + per_head[1] * high_half), axis=0, keepdims=True))
        none = jnp.zeros((1, 128), F32)
        pooled = jnp.concatenate(pooled + [none, none], axis=0)
        hidden = jnp.tanh(exact(pooled, hid[...]))
        o_logits[...] = exact(hidden, cls[...]) * alive_seq[...]
        g_log = cotl[...] * alive_seq[...]
        o_small[1] = exact(hidden, g_log, ((0,), (0,))).astype(BF)
        g_pre = exact(g_log, cls[...], ((1,), (1,))) * (1.0 - hidden * hidden)
        o_small[0] = exact(pooled, g_pre, ((0,), (0,))).astype(BF)
        g_pooled = exact(g_pre, hid[...], ((1,), (1,)))
        g_query = none
        for s in range(SEQ_DEV):
            r = pl.ds(s * SEQ, SEQ)
            pr = projected[r, :]
            gp = g_pooled[s:s + 1]
            t = pr * gp
            total = (weights[s][0] * low_half + weights[s][1] * high_half) * gp
            for half, w in zip((low_half, high_half), weights[s]):
                dw = jnp.sum(t * half, axis=-1, keepdims=True)
                ds = w * (dw - jnp.sum(w * dw, axis=0, keepdims=True)) * 0.125
                total = total + ds * (query * half)
                g_query = g_query + jnp.sum(ds * pr, axis=0, keepdims=True) * half
            gproj[r, :] = total.astype(BF)
        o_small[2] = jnp.broadcast_to(g_query, (128, 128)).astype(BF)

    once(student)

    def back(j):
        r = span(j, 384)
        keep_tok = alive[r, pl.ds(0, 1)]
        low = out[r, :]
        g_out = keep_tok * cotv[r, :].astype(F32) + dot(gproj[r, :], wproj[...], ((1,), (1,)))
        n = gsec[r, :]
        part = jnp.sum(g_out * n, axis=0, keepdims=True)
        rows[3, pl.ds(0, 1), :] = jnp.where(j == 0, part, part + rows[3, pl.ds(0, 1), :])
        g2 = norm_back(g_out, gain2, n, r2[r, pl.ds(0, 1)])
        gsec[r, :] = g2
        dlow[r, :] = g2.astype(BF)
        cotv[r, :] = (keep_tok * low.astype(F32)).astype(BF)
        low_part(j).start()
        for c in late(j):
            c.start()

    def low_part(j):
        r = span(j, 384)
        return pltpu.make_async_remote_copy(
            src_ref=dlow.at[r], dst_ref=o_dlow.at[1, r], send_sem=xsend.at[9 + j], recv_sem=xrecv.at[9 + j],
            device_id=place.sibling, device_id_type=MESH)

    def late(j):
        r = span(j, 384)
        return [pltpu.make_async_copy(src.at[r], dst.at[r], outsem.at[16 + 3 * j + n])
                for n, (src, dst) in enumerate(((dlow, o_dlow.at[0]), (gsec, o_gsec), (cotv, o_act)))]

    loop(2, back)

    def hidden_copy(j):
        c = span(j, D)
        return pltpu.make_async_copy(dact.at[:, c], o_gup.at[:, c], outsem.at[22 + j])

    def hidden_part(j):
        return pltpu.make_async_remote_copy(
            src_ref=dact.at[:, span(j, D)], dst_ref=o_gup_s.at[:, span(lax.rem(j, 2), D)],
            send_sem=xsend.at[11 + lax.rem(j, 2)], recv_sem=xrecv.at[11 + lax.rem(j, 2)],
            device_id=place.sibling, device_id_type=MESH)

    def hidden(i):
        j = lax.rem(i + 2 - 2 * place.core, 4)
        c = span(j, D)
        part = b_down[j // 2, pl.ds(lax.rem(j, 2) * 2, 2)].reshape(D, D)
        dact[:, c] = (dot(dlow[...], part, ((1,), (1,))) * dact[:, c].astype(F32)).astype(BF)
        hidden_copy(j).start()
        pl.when(j // 2 != place.core)(lambda: hidden_part(j).start())

    loop(4, hidden)

    def proj_grad():
        o_small[3:9] = dot(out[...], gproj[...], ((0,), (0,))).astype(BF).reshape(6, 128, 128)

    once(proj_grad)
    g.end()
    for c in stores + late(0) + late(1) + [hidden_copy(j) for j in range(4)] + [hidden_part(j) for j in range(2)]:
        c.wait()
    for n, dst in ((0, o_tokens2), (1, o_ctx), (2, o_normed)):
        cross.landed(n, dst.at[1], place.sibling)
    cross.sent()
    for c in [active_part(j) for j in range(4)] + [low_part(j) for j in range(2)]:
        c.wait()


def forward(tokens, cot, exit_layer, cot_logits, small, shards):
    hbm, vmem = pl.BlockSpec(memory_space=pl.ANY), pl.BlockSpec(memory_space=pltpu.VMEM)
    n = len(KINDS)
    count = n * 3 - 2

    def arr(*shape, dtype=BF):
        return jax.ShapeDtypeStruct(shape, dtype)

    outs = [
        (arr(TOK, D), hbm), (arr(8, 128, dtype=F32), vmem),
        (arr(D, 3 * D), hbm), (arr(D, D), hbm), (arr(D, FF), hbm),
        (arr(TOK, 3 * D), hbm), (arr(SEQ_DEV * PAIRS, 256, 128), hbm), (arr(2, TOK, D), hbm), (arr(2, TOK, D), hbm),
        (arr(TOK, D), hbm), (arr(TOK, 128, dtype=F32), hbm), (arr(2, TOK, FF), hbm), (arr(TOK, FF), hbm), (arr(TOK, FF // 2), hbm),
        (arr(TOK, D, dtype=F32), hbm), (arr(2, TOK, D), hbm), (arr(2, TOK, D), hbm),
        (arr(9, 128, 128), vmem), (arr(4, 8, D, dtype=F32), vmem),
    ]
    dma = pltpu.SemaphoreType.DMA
    scratch = [
        pltpu.VMEM((2, 4, 4, 32, 128), BF), pltpu.VMEM((2, 4, 4, 24, 3 * D), BF), pltpu.VMEM((2, 4, 4, 24, D), BF),
        pltpu.VMEM((2, 4, 4, 24, FF), BF), pltpu.VMEM((2, 4, 4, 96, D), BF),
        pltpu.VMEM((D, 3 * D), BF), pltpu.VMEM((D, D), BF), pltpu.VMEM((D, FF), BF),
        pltpu.VMEM((TOK, D), BF), pltpu.VMEM((TOK, D), BF), pltpu.VMEM((TOK, 3 * D), BF),
        pltpu.VMEM((SEQ_DEV * PAIRS, 256, 128), BF), pltpu.VMEM((TOK, D), BF), pltpu.VMEM((TOK, D), BF),
        pltpu.VMEM((TOK, D), BF), pltpu.VMEM((TOK, 128), F32), pltpu.VMEM((TOK, FF), BF), pltpu.VMEM((TOK, FF), BF),
        pltpu.VMEM((TOK, D), F32), pltpu.VMEM((TOK, 128), F32), pltpu.VMEM((TOK, D), BF), pltpu.VMEM((TOK, D), BF),
        pltpu.VMEM((TOK, 128), F32), pltpu.VMEM((TOK, 128), BF), pltpu.VMEM((D, 128), BF),
        pltpu.VMEM((128, 128), F32), pltpu.VMEM((128, 128), F32),
        pltpu.VMEM((TOK, 128), F32), pltpu.VMEM((8, 128), F32), pltpu.VMEM((8, 128), F32),
        pltpu.VMEM((32, 128), F32), pltpu.VMEM((32, 128), BF),
        dma((count * 3,)), dma((count * EVENTS,)), dma((2 * n,)), dma((2 * n,)),
        dma((2,)), dma((26,)), dma((13,)), dma((13,)),
    ]
    return pl.pallas_call(
        forward_kernel,
        out_shape=[o for o, _ in outs],
        in_specs=[hbm, hbm, pl.BlockSpec(memory_space=pltpu.SMEM)] + [vmem] * 7 + [hbm] * 4,
        out_specs=[s for _, s in outs],
        scratch_shapes=scratch,
        compiler_params=pltpu.CompilerParams(collective_id=0, has_side_effects=True, vmem_limit_bytes=VMEM),
        cost_estimate=pl.CostEstimate(flops=12 * 10**9, bytes_accessed=60 * 10**6, transcendentals=4 * 10**6),
        name="forward",
    )(tokens, cot, exit_layer, cot_logits, *small, *shards)


def landing(order):
    out, left = [], ["x", "z", "y"]
    for axis in reversed(order):
        left = [a for a in left if a != axis]
        out.append((1 if axis == "x" else 3, tuple(SIZE[a] for a in left)))
    return out


def add_box(place, held, left, fixed, terms):
    dims = tuple(SIZE[a] for a in left)

    def step(i):
        index = []
        for d in reversed(dims):
            index.append(i % d)
            i = i // d
        index = tuple(reversed(index))
        at = dict(zip(left, index))
        b = tuple(fixed[a] if a in fixed else at[a] if a in at else place.at(a) for a in ("x", "z", "y"))
        total = held[b]
        for t in terms:
            total = total + t[index]
        held[b] = total

    if dims:
        count = 1
        for d in dims:
            count *= d
        lax.fori_loop(0, count, lambda i, c: (step(i), c)[1], 0, unroll=4)
    else:
        step(0)


def reduce_unit(place, lane, side, number, core, order, direct, held, lands, last, result, twin, put):
    way = 1 if core == 0 else -1
    left, e = ["x", "z", "y"], 0
    for axis, bufs in zip(reversed(order), lands):
        left = [a for a in left if a != axis]
        ahead, back = place.near(axis, way), place.near(axis, -way)
        mine = {axis: place.at(axis)}
        if axis != "x" and (direct or not left):
            for n, (step, to) in enumerate(((way, ahead), (-way, back), (2, place.near(axis, 2)))):
                lane.go(e + n, held.at[place.box(left, **{axis: place.at(axis, step)})], bufs[n], to)
            yield
            for n in range(3):
                lane.landed(e + n, bufs[n], ahead)
            add_box(place, held, left, mine, bufs)
            e += 3
        elif axis == "x":
            lane.go(e, held.at[place.box(left, x=place.at("x", 1))], bufs[0], ahead)
            yield
            lane.landed(e, bufs[0], ahead)
            add_box(place, held, left, mine, [bufs[0]])
            e += 1
        else:
            lane.go(e, held.at[place.box(left, **{axis: place.at(axis, 2)})], bufs[0], ahead)
            lane.go(e + 1, held.at[place.box(left, **{axis: place.at(axis, -way)})], bufs[1], back)
            yield
            lane.landed(e, bufs[0], ahead)
            onward = {axis: place.at(axis, way)}
            add_box(place, held, left, onward, [bufs[0]])
            lane.go(e + 2, held.at[place.box(left, **onward)], bufs[2], ahead)
            yield
            lane.landed(e + 1, bufs[1], ahead)
            lane.landed(e + 2, bufs[2], ahead)
            add_box(place, held, left, mine, [bufs[1], bufs[2]])
            e += 3
    own = place.box(())
    lane.go(e, held.at[own], last, place.near("x", 2))
    yield
    lane.landed(e, last, place.near("x", 2))
    total = held[own] + last[...]
    result[...] = total
    side.go(number, result, twin, place.sibling)
    put[0][...] = total.astype(F32)
    yield
    side.landed(number, twin, place.sibling)
    put[1][...] = twin[...].astype(F32)


DIRECT = (QKV, OUT, SMALL)
FIRST = (QKV, OUT, SMALL, DOWN, UP)
PIECES = [(i, k) for i in (DOWN, UP, OUT, QKV, SMALL) for k in range(3) if i != SMALL or k == 1]


def piece_shape(i):
    return {SMALL: (16, 128), QKV: (24, 384), OUT: (24, 128), UP: (24, 512), DOWN: (96, 128)}[i]


def reduce_scratch():
    out = []
    for i, k in PIECES:
        shape = piece_shape(i)
        out.append(pltpu.VMEM((2, 4, 4) + shape, BF))
        for copies, dims in landing(ORDERS[0][k]):
            out.extend([pltpu.VMEM(dims + shape, BF)] * copies)
        out.extend([pltpu.VMEM(shape, BF)] * 3)
    return out


class Reduce:
    def __init__(self, place, scratch, outs, send, recv, ssend, srecv):
        self.place = place
        self.lanes = [[Lane(send, recv, 3 * n, SUMS * n) for n in range(len(PIECES))] for _ in range(2)]
        self.sides = [Wire(ssend, srecv) for _ in range(2)]
        self.held, self.units, self.live, self.done = {}, [{}, {}], [], {}
        for n, (i, k) in enumerate(PIECES):
            held = scratch.pop(0)
            lands = [[scratch.pop(0) for _ in range(copies)] for copies, _ in landing(ORDERS[0][k])]
            last, result, twin = (scratch.pop(0) for _ in range(3))
            self.held[i, k] = held
            for core in range(2):
                kind = "small" if i == SMALL else "cols"
                width = outs[i].shape[-1]
                put = (outs[i].at[piece(kind, core, k, width)], outs[i].at[piece(kind, 1 - core, k, width)])
                self.units[core][i, k] = reduce_unit(
                    place, self.lanes[core][n], self.sides[core], n, core, ORDERS[core][k], i in DIRECT,
                    held, lands, last, result, twin, put)

    def advance(self, pieces):
        def one(core):
            for p in pieces:
                next(self.units[core][p], None)

        self.place.on_core(one)

    def start(self, *pieces):
        self.advance(pieces)
        for p in pieces:
            self.live.append(p)
            self.done[p] = 1

    def pump(self, *arrays):
        todo = sorted((p for p in self.live if not arrays or p[0] in arrays), key=lambda p: FIRST.index(p[0]))
        self.advance(todo)
        for p in todo:
            self.done[p] += 1
            if self.done[p] == (6 if p[0] in DIRECT else 7):
                self.live.remove(p)

    def end(self):
        while self.live:
            self.pump()

        def one(core):
            for lane in self.lanes[core]:
                lane.sent()
            self.sides[core].sent()

        self.place.on_core(one)


def lay(held, value):
    for i in range(16):
        x, z, y = at_block(i)
        for j in range(2):
            held[x, z, 2 * y + j] = value[48 * i + 24 * j:48 * i + 24 * j + 24].astype(BF)


def backward_kernel(tokens2, merged_h, probs_h, ctx2_h, normed2_h, n1_h, r1_h, active2_h, gup_h, gup_s_h, gsec_h, dlow2_h,
                    wqkv_h, wout_h, wup_h, small_h, rows_h,
                    o_gtok, o_qkv, o_out, o_up, o_down, o_small,
                    tok2, act2, gup, normed2, ctx2, dlow2, n1, r1, gsec, attn, attn_s, gctx, gup_s, gm_s, probs,
                    w_big, w_out, packed, packed_s, g_row, small, rows, *rest):
    scratch = list(rest[:-8])
    send, recv, ssend, srecv, insem, wsem, xsend, xrecv = rest[-8:]
    place = Place()
    core = place.core
    loads = {}

    def load(name, src, dst):
        c = pltpu.make_async_copy(src, dst, insem.at[len(loads)])
        c.start()
        loads[name] = c

    def ready(*names):
        for name in names:
            loads[name].wait()

    def w_load(i, src, dst):
        c = pltpu.make_async_copy(src, dst, wsem.at[i])
        return c

    def active_load(j):
        return pltpu.make_async_copy(active2_h.at[:, :, span(j, D)], act2.at[:, :, span(j, D)], insem.at[18 + j])

    load("dlow", dlow2_h, dlow2)
    for j in range(4):
        active_load(j).start()
    greet(place)
    red = Reduce(place, scratch, {QKV: o_qkv, OUT: o_out, UP: o_up, DOWN: o_down, SMALL: o_small},
                 send, recv, ssend, srecv)
    cross = Wire(xsend, xrecv)

    def mine(size):
        return pl.ds(pl.multiple_of(core * size, 128), size)

    def other(size):
        return pl.ds(pl.multiple_of((1 - core) * size, 128), size)

    load("rows", rows_h, rows)
    load("small", small_h, small)
    load("gup", gup_h, gup)
    load("gup_s", gup_s_h, gup_s)
    load("normed", normed2_h, normed2)

    def up_load(j, slot):
        return w_load(slot, wup_h.at[span(j, 256)], w_big.at[slot])

    def qkv_load(j, slot):
        return w_load(slot, wqkv_h.at[span(j, 256)], w_big.at[slot, :, pl.ds(0, 3 * D)])

    ready("dlow")

    def down(j):
        active_load(j).wait()
        left = dlow2[:, :, mine(384)].reshape(2 * TOK, 384)
        g = dot(left, act2[:, :, span(j, D)].reshape(2 * TOK, D), ((0,), (0,))).T.astype(BF)
        for k in range(3):
            red.held[DOWN, k][j // 2, pl.ds(lax.rem(j, 2) * 2, 2)] = g[:, 128 * k:128 * k + 128].reshape(2, 4, 96, 128)

    loop(4, down)
    red.start((DOWN, 0), (DOWN, 1), (DOWN, 2))
    for j in range(2):
        up_load(j, j).start()
    load("gsec", gsec_h, gsec)
    load("n1", n1_h, n1)
    load("r1", r1_h, r1)
    load("wout", wout_h, w_out)
    load("merged", merged_h, act2.at[0, :, pl.ds(0, 3 * D)])
    merged = act2.at[0, :, pl.ds(0, 3 * D)]
    load("probs", probs_h, probs)
    load("ctx", ctx2_h, ctx2)
    load("tokens", tokens2, tok2)
    ready("gup", "gup_s", "normed")
    for k in range(3):
        own = gup[:, pl.ds(pl.multiple_of(core * (FF // 2) + 512 * k, 128), 512)]

        def grad_up():
            lay(red.held[UP, k], dot(normed2[0], own, ((0,), (0,))) + dot(normed2[1], gup_s[:, 512 * k:512 * k + 512], ((0,), (0,))))

        once(grad_up)
        red.start((UP, k))
    ready("gsec", "n1", "r1", "rows", "small")

    def g_normed(j):
        slot = lax.rem(j, 2)
        up_load(j, slot).wait()
        c = span(j, 256)
        gsec[:, c] = gsec[:, c] + dot(gup[...], w_big[slot], ((1,), (1,)))
        pl.when(j < 1)(lambda: up_load(j + 2, slot).start())

    loop(3, g_normed)
    for j in range(2):
        qkv_load(j, 1 - j).start()
    gain1 = rows[0, pl.ds(0, 1), :]

    def norm1(j):
        r = span(j, 384)
        g, n = gsec[r, :], n1[r, :].astype(F32)
        part = jnp.sum(g * n, axis=0, keepdims=True)
        g_row[0:1] = jnp.where(j == 0, part, part + g_row[0:1])
        g = norm_back(g, gain1, n, r1[r, pl.ds(0, 1)])
        gsec[r, :] = g
        attn[r, :] = g.astype(BF)

    loop(2, norm1)
    cross.go(1, attn.at[:, other(384)], attn_s, place.sibling)
    ready("wout", "ctx")

    def context(j):
        r = span(j, 384)
        gctx[r, :] = dot(attn[r, :], w_out[...], ((1,), (1,))).astype(BF)

    loop(2, context)

    ready("merged", "probs")

    low_half, high_half = halves()
    la, lb = low_half.astype(BF), high_half.astype(BF)
    qa, qb = (low_half * 0.125).astype(BF), (high_half * 0.125).astype(BF)

    def attend_back(s):
        r = span(s, SEQ)
        at = [[pl.ds(768 * a + 128 * p, 128) for a in range(3)] for p in range(PAIRS)]
        d2, q2, gp, gs = [], [], [], []
        for p in range(PAIRS):
            q, d = merged[r, at[p][0]], gctx[r, pl.ds(128 * p, 128)]
            d2.append(jnp.concatenate([d * la, d * lb], axis=0))
            q2.append(jnp.concatenate([q * qa, q * qb], axis=0))
            gp.append(dot(d2[p], merged[r, at[p][2]], ((1,), (1,))))
        for p in range(PAIRS):
            pr = probs[s * PAIRS + p]
            merged[r, at[p][2]] = dot(pr, d2[p], ((0,), (0,))).astype(BF)
            pf = pr.astype(F32)
            t = pf * gp[p]
            gs.append((t - pf * jnp.sum(t, axis=-1, keepdims=True)).astype(BF))
        for p in range(PAIRS):
            both = dot(gs[p], merged[r, at[p][1]])
            merged[r, at[p][0]] = ((both[:SEQ] * low_half + both[SEQ:] * high_half) * 0.125).astype(BF)
            merged[r, at[p][1]] = dot(gs[p], q2[p], ((0,), (0,))).astype(BF)

    def gm_part(part):
        r = pl.ds(256 * part, 256)
        return pltpu.make_async_remote_copy(
            src_ref=act2.at[0, r, other(3 * D // 2)], dst_ref=gm_s.at[r], send_sem=xsend.at[4 + part],
            recv_sem=xrecv.at[4 + part], device_id=place.sibling, device_id_type=MESH)

    for part in range(3):

        def attend_part(s):
            attend_back(s + 2 * part)

        loop(2, attend_part)
        if part == 0:
            red.pump(DOWN)
        if part == 2:
            red.pump(DOWN, UP)
        gm_part(part).start()
    ready("tokens")

    def g_tokens(j):
        slot = lax.rem(j + 1, 2)
        qkv_load(j, slot).wait()
        c = span(j, 256)
        gsec[:, c] = gsec[:, c] + dot(merged[...], w_big[slot, :, :3 * D], ((1,), (1,)))
        pl.when(j < 1)(lambda: qkv_load(j + 2, slot).start())

    def pack_small():
        p_proj, p_hid, p_cls, p_misc = picks()
        pack = dot(p_proj, small[3:9].reshape(D, 128), ((0,), (0,)))
        pack = pack + dot(p_hid, small[0], ((0,), (0,)))
        lane = iota((128, 128), 1)
        pack = pack + dot(p_cls, jnp.where(lane < 14, small[1].astype(F32), 0.0).astype(BF), ((0,), (0,)))
        values = (g_row[0:1], rows[3, pl.ds(0, 1), :], small[2, pl.ds(0, 1), :].astype(F32))
        misc = jnp.zeros((32, 128), F32)
        for (name, first, size, per), value in zip(ROWS, values):
            tile, held = spread(first, size, per)
            misc = misc + dot(jnp.where(held, value, 0.0).astype(BF), tile, ((1,), (1,)))
        packed[...] = (pack + dot(p_misc, misc.astype(BF), ((0,), (0,)))).astype(BF).reshape(2, 4, 4, 32, 128)

    once(pack_small)
    place.on_core(lambda c: cross.copy(3, packed.at[:, :, :, pl.ds(16 - 16 * c, 16)], packed_s, place.sibling).start())

    cross.landed(1, attn_s, place.sibling)

    def grad_out():
        g = dot(ctx2[0], attn[:, mine(384)], ((0,), (0,))) + dot(ctx2[1], attn_s[...], ((0,), (0,)))
        for k in range(3):
            lay(red.held[OUT, k], g[:, 128 * k:128 * k + 128])

    once(grad_out)
    cross.landed(3, packed_s, place.sibling)

    def small_half(c):
        red.held[SMALL, 1][...] = packed[:, :, :, 16 * c:16 * c + 16, :] + packed_s[...]

    place.on_core(small_half)
    for part in range(3):
        gm_part(part).wait_recv()
    for k in range(3):
        own = merged[:, pl.ds(pl.multiple_of(core * (3 * D // 2) + 384 * k, 128), 384)]

        def grad_qkv():
            lay(red.held[QKV, k], dot(tok2[0], own, ((0,), (0,))) + dot(tok2[1], gm_s[:, 384 * k:384 * k + 384], ((0,), (0,))))

        once(grad_qkv)
        red.start((QKV, k))
    red.start((OUT, 0), (OUT, 1), (OUT, 2), (SMALL, 1))
    red.pump(DOWN, UP)
    loop(3, g_tokens)
    red.pump()
    store = pltpu.make_async_copy(gsec, o_gtok, insem.at[len(loads)])
    store.start()
    red.end()
    cross.sent()
    for part in range(3):
        gm_part(part).wait_send()
    place.on_core(lambda c: cross.copy(3, packed.at[:, :, :, pl.ds(16 - 16 * c, 16)], packed_s, place.sibling).wait_send())
    store.wait()


def backward(*args):
    hbm, vmem = pl.BlockSpec(memory_space=pl.ANY), pl.BlockSpec(memory_space=pltpu.VMEM)

    def arr(*shape, dtype=F32):
        return jax.ShapeDtypeStruct(shape, dtype)

    dma = pltpu.SemaphoreType.DMA
    count = len(PIECES)
    scratch = [
        pltpu.VMEM((2, TOK, D), BF), pltpu.VMEM((2, TOK, FF), BF), pltpu.VMEM((TOK, FF), BF),
        pltpu.VMEM((2, TOK, D), BF), pltpu.VMEM((2, TOK, D), BF), pltpu.VMEM((2, TOK, D), BF),
        pltpu.VMEM((TOK, D), BF), pltpu.VMEM((TOK, 128), F32), pltpu.VMEM((TOK, D), F32),
        pltpu.VMEM((TOK, D), BF), pltpu.VMEM((TOK, D // 2), BF), pltpu.VMEM((TOK, D), BF),
        pltpu.VMEM((TOK, FF // 2), BF), pltpu.VMEM((TOK, 3 * D // 2), BF),
        pltpu.VMEM((SEQ_DEV * PAIRS, 256, 128), BF),
        pltpu.VMEM((2, 256, FF), BF), pltpu.VMEM((D, D), BF),
        pltpu.VMEM((2, 4, 4, 32, 128), BF), pltpu.VMEM((2, 4, 4, 16, 128), BF), pltpu.VMEM((8, D), F32),
        pltpu.VMEM((9, 128, 128), BF), pltpu.VMEM((4, 8, D), F32),
    ] + reduce_scratch() + [
        dma((count * 3,)), dma((count * SUMS,)), dma((count,)), dma((count,)), dma((22,)), dma((2,)), dma((7,)), dma((7,)),
    ]
    return pl.pallas_call(
        backward_kernel,
        out_shape=[arr(TOK, D), arr(24, 3 * D), arr(24, D), arr(24, FF), arr(96, D), arr(32, 128)],
        in_specs=[hbm] * 17,
        out_specs=[hbm] + [vmem] * 5,
        scratch_shapes=scratch,
        compiler_params=pltpu.CompilerParams(collective_id=1, has_side_effects=True, vmem_limit_bytes=VMEM),
        cost_estimate=pl.CostEstimate(flops=24 * 10**9, bytes_accessed=60 * 10**6, transcendentals=0),
        name="backward",
    )(*args)


def finish_kernel(act, logits, gtok, qkv, out, up, down, small, *rest):
    o_act, o_logits, o_gtok, o_qkv, o_out, o_g1, o_up, o_down, o_g2, o_proj, o_pool, o_hid, o_cls = rest[:13]
    h_gtok, h_act, h_qkv, h_up, h_down, h_out, sems = rest[13:]
    moves = [(gtok, h_gtok, o_gtok, r) for r in range(3)] + [(act, h_act, o_act, r) for r in range(3)]
    moves += [(qkv, h_qkv, o_qkv, None), (up, h_up, o_up, None), (down, h_down, o_down, None), (out, h_out, o_out, None)]

    def at(ref, r):
        return ref if r is None else ref.at[pl.ds(256 * r, 256)]

    come = [pltpu.make_async_copy(at(a, r), at(h, r), sems.at[n]) for n, (a, h, o, r) in enumerate(moves)]
    go = [pltpu.make_async_copy(at(h, r), at(o, r), sems.at[len(moves) + n]) for n, (a, h, o, r) in enumerate(moves)]
    for c in come:
        c.start()
    o_logits[...] = logits[0:SEQ_DEV, 0:14]
    o_proj[...] = small[0:24]
    o_hid[...] = small[24:28]
    o_cls[...] = small[28:32, 0:14]
    o_g1[...] = small[28:29, 16:40]
    o_g2[...] = small[28:29, 40:64]
    o_pool[...] = small[28:29, 64:68]
    for c, d in zip(come, go):
        c.wait()
        d.start()
    for d in go:
        d.wait()


def finish(*args):
    hbm, vmem = pl.BlockSpec(memory_space=pl.ANY), pl.BlockSpec(memory_space=pltpu.VMEM)
    shapes = ((TOK, D), (SEQ_DEV, 14), (TOK, D), (24, 3 * D), (24, D), (1, 24), (24, FF), (96, D), (1, 24), (24, 128),
              (1, 4), (4, 128), (4, 14))
    moved = (0, 2, 3, 4, 6, 7)
    return pl.pallas_call(
        finish_kernel,
        out_shape=[jax.ShapeDtypeStruct(s, F32 if n else BF) for n, s in enumerate(shapes)],
        in_specs=[hbm, vmem, hbm, hbm, hbm, hbm, hbm, vmem],
        out_specs=[hbm if n in moved else vmem for n in range(len(shapes))],
        scratch_shapes=[pltpu.VMEM((TOK, D), F32), pltpu.VMEM((TOK, D), BF), pltpu.VMEM((24, 3 * D), F32),
                        pltpu.VMEM((24, FF), F32), pltpu.VMEM((96, D), F32), pltpu.VMEM((24, D), F32),
                        pltpu.SemaphoreType.DMA((20,))],
        compiler_params=pltpu.CompilerParams(vmem_limit_bytes=VMEM),
        name="finish",
    )(*args)


def local(tokens, exit_layer, w_qkv, w_out, gain_attn, w_up, w_down, gain_ffn, w_proj, pool_query, w_hid, w_cls,
          cot_out, cot_logits):
    small = (w_proj, w_hid, w_cls, gain_attn[None], gain_ffn[None], pool_query[None])
    (act, logits, f_qkv, f_out, f_up, merged, probs, ctx, normed, n1, r1, active, gup, gup_s, gsec, dlow, tokens2,
     small_g, rows) = forward(
         tokens, cot_out, exit_layer, cot_logits, small, (w_qkv, w_out, w_up, w_down))
    g_tok, g_qkv, g_out, g_up, g_down, g_small = backward(
        tokens2, merged, probs, ctx, normed, n1, r1, active, gup, gup_s, gsec, dlow, f_qkv, f_out, f_up, small_g, rows)
    outs = list(finish(act, logits, g_tok, g_qkv, g_out, g_up, g_down, g_small))
    for n in (5, 8, 10):
        outs[n] = outs[n].reshape(-1)
    return tuple(outs)


def solution(mesh):
    both, wide = P(("wide", "grp"), None), P("wide", None)
    in_specs = (both, P(("wide", "grp")), wide, wide, P("wide"), wide, wide, P("wide"), wide, P("wide"), wide, wide,
                both, both)
    out_specs = (both, both, both, wide, wide, P("wide"), wide, wide, P("wide"), wide, P("wide"), wide, wide)
    return jax.shard_map(local, mesh=mesh, in_specs=in_specs, out_specs=out_specs, check_vma=False)
```
